32 devices in a mesh: segment: 2 (over y), lon: 4 (over x, core), lat: 4 (over z).
Axes of the slice: x: 2, y: 2, z: 4, core: 2. Of those that a mesh axis runs over, the one named last changes fastest.
Arguments:
- latents: bfloat16 [2, 24, 48, 1024], P(None, 'lat', 'lon'), may hold values from -48 to 48
- land_mask: int32 [24, 48], P('lat', 'lon'), may hold values 0 or 1
- land_embed: bfloat16 [1024], replicated, may hold values from -6 to 6
- qkv_weight: bfloat16 [2, 1024, 3072], P('segment'), may hold values from -0.25625 to 0.25625
- out_weight: bfloat16 [2, 1024, 1024], P('segment'), may hold values from -0.5625 to 0.5625
- norm_gain: float32 [2, 1024], replicated, may hold values from 0.5 to 1.5
- offsets: int32 [2, 2], replicated, may hold values from 0 to 11, as said below
Outputs:
- sections: bfloat16 [2, 2, 24, 48, 1024], P('segment', None, 'lat', 'lon')
The draws below stay inside these ranges and needn't reach their ends.
Inputs may be any that keep to these rules, and one draw needn't show every extreme that they name: offsets[s, 0] lies in 0 to 5 and offsets[s, 1] in 0 to 11; one of the two sections has offsets[s, 0] = 5 and offsets[s, 1] = 11.
All inputs are finite; a program needn't handle non-finite values. No bound on the sum of `land_mask` on one device may be relied on, other than what follows from the above.
Results may differ from the reference program's by a relative error of at most 0.015.
Values may be sent and summed in bfloat16 or wider, within the bound.
A program may use at most 64 MiB of HBM per device.

```python
import math
import jax
import jax.numpy as jnp
from jax import lax

D = 1024
HEADS = 16
HEAD = 64
WLAT = 6
WLON = 12
LB = 2
NLAT = 24
NLON = 48


def draw_latents(key, part):
    base_key = jax.random.fold_in(jax.random.fold_in(key, 11), 0)
    values = jnp.clip(jax.random.normal(base_key, (LB, NLAT, NLON, D), jnp.float32), -6.0, 6.0)
    return values.astype(jnp.bfloat16)


def draw_qkv_weight(key, part):
    first_key, second_key, third_key = jax.random.split(jax.random.fold_in(key, 23), 3)
    scale = D ** (-0.5)
    shared = jnp.clip(jax.random.normal(first_key, (2, D, D), jnp.float32), -6.0, 6.0)
    apart = jnp.clip(jax.random.normal(second_key, (2, D, D), jnp.float32), -6.0, 6.0)
    valued = jnp.clip(jax.random.normal(third_key, (2, D, D), jnp.float32), -6.0, 6.0)
    query_part = shared * scale
    key_part = (0.5 * shared + 0.866 * apart) * scale
    value_part = valued * scale
    return jnp.concatenate([query_part, key_part, value_part], axis=2).astype(jnp.bfloat16)


def draw_out_weight(key, part):
    base_key, column_key = jax.random.split(jax.random.fold_in(key, 37))
    values = jnp.clip(jax.random.normal(base_key, (2, D, D), jnp.float32), -6.0, 6.0)
    column_scale = jnp.exp(jax.random.uniform(column_key, (2, 1, D), minval=math.log(0.3), maxval=math.log(3.0)))
    return (values * D ** (-0.5) * column_scale).astype(jnp.bfloat16)


def draw_offsets(key, part):
    lat_key, lon_key, pick_key = jax.random.split(jax.random.fold_in(key, 41), 3)
    lat_shift = jax.random.randint(lat_key, (2,), 0, WLAT)
    lon_shift = jax.random.randint(lon_key, (2,), 0, WLON)
    chosen = jax.random.randint(pick_key, (), 0, 2)
    segment_ids = jnp.arange(2, dtype=jnp.int32)
    lat_shift = jnp.where(segment_ids == chosen, WLAT - 1, lat_shift)
    lon_shift = jnp.where(segment_ids == chosen, WLON - 1, lon_shift)
    return jnp.stack([lat_shift, lon_shift], axis=1).astype(jnp.int32)


def with_ends(entries, key, low, largest):
    index_at = [jax.random.randint(jax.random.fold_in(key, axis), (), 0, length) for axis, length in enumerate(entries.shape)]
    longest = entries.shape.index(max(entries.shape))
    next_to = index_at[:longest] + [(index_at[longest] + 1) % entries.shape[longest]] + index_at[longest + 1:]
    return entries.at[tuple(index_at)].set(low).at[tuple(next_to)].set(largest)


def normal_values(stream_key, extent, deviation, reach, held_as=jnp.bfloat16):
    entries = deviation * jax.random.normal(stream_key, extent, jnp.float32)
    return jnp.clip(entries, min=-reach, max=reach).astype(held_as)


def setup_inputs(seed: int = 0) -> dict:
    key_list = jax.random.split(jax.random.key(seed), 8)
    return {
        "latents": draw_latents(jax.random.fold_in(key_list[7], 71), 0),
        "land_mask": with_ends((jax.random.randint(key_list[1], (NLAT, NLON), 0, 10) < 3).astype(jnp.int32), jax.random.fold_in(key_list[1], 1), 0, 1),
        "land_embed": normal_values(key_list[2], (D,), 1.0, 6.0),
        "qkv_weight": draw_qkv_weight(jax.random.fold_in(key_list[7], 71), 0),
        "out_weight": draw_out_weight(jax.random.fold_in(key_list[7], 71), 0),
        "norm_gain": jnp.clip(1.0 + 0.1 * jax.random.normal(key_list[5], (2, D), jnp.float32), 0.5, 1.5),
        "offsets": draw_offsets(jax.random.fold_in(key_list[7], 71), 0),
    }


def run_section(field, wqkv, wout, gain, lat_offset, lon_offset):
    total_rows, total_cols, width = field.shape
    cell_count = WLAT * WLON
    rolled = jnp.roll(field, (-lat_offset, -lon_offset), (0, 1))
    row_windows = total_rows // WLAT
    col_windows = total_cols // WLON
    cells = rolled.reshape(row_windows, WLAT, col_windows, WLON, width).transpose(0, 2, 1, 3, 4)
    cells = cells.reshape(row_windows, col_windows, cell_count, width)
    wrapped = jnp.arange(total_rows, dtype=jnp.int32) + lat_offset >= total_rows
    flags = jnp.broadcast_to(wrapped.reshape(row_windows, 1, WLAT, 1), (row_windows, col_windows, WLAT, WLON))
    flags = flags.reshape(row_windows, col_windows, cell_count)

    def one_row(pair):
        row_cells, row_flags = pair
        flat = row_cells.reshape(-1, width)
        packed = jnp.dot(flat, wqkv, preferred_element_type=jnp.float32).astype(jnp.bfloat16)
        packed = packed.reshape(col_windows, cell_count, 3, HEADS, HEAD)
        queries = packed[:, :, 0].astype(jnp.float32)
        keys = packed[:, :, 1].astype(jnp.float32)
        values = packed[:, :, 2].astype(jnp.float32)
        scores = jnp.einsum('nqhd,nkhd->nhqk', queries, keys) / math.sqrt(HEAD)
        allowed = row_flags[:, :, None] == row_flags[:, None, :]
        scores = jnp.where(allowed[:, None], scores, -1e+30)
        probs = jax.nn.softmax(scores, axis=-1).astype(jnp.bfloat16)
        attended = jnp.einsum('nhqk,nkhd->nqhd', probs.astype(jnp.float32), values)
        attended = attended.astype(jnp.bfloat16).reshape(-1, width)
        projected = jnp.dot(attended, wout, preferred_element_type=jnp.float32)
        centered = projected - lax.optimization_barrier(jnp.mean(projected, axis=-1, keepdims=True))
        variance = lax.optimization_barrier(jnp.mean(centered * centered, axis=-1, keepdims=True))
        branch = centered * lax.rsqrt(variance + 1e-05) * gain
        summed = (flat.astype(jnp.float32) + branch).astype(jnp.bfloat16)
        return summed.reshape(col_windows, cell_count, width)
    result = lax.map(one_row, (cells, flags))
    grid = result.reshape(row_windows, col_windows, WLAT, WLON, width).transpose(0, 2, 1, 3, 4)
    grid = grid.reshape(total_rows, total_cols, width)
    return jnp.roll(grid, (lat_offset, lon_offset), (0, 1))

def reference(latents, land_mask, land_embed, qkv_weight, out_weight, norm_gain, offsets):
    land_term = land_mask.astype(jnp.float32)[:, :, None] * land_embed.astype(jnp.float32)
    first_list = []
    second_list = []
    for block_index in range(LB):
        seeded = (latents[block_index].astype(jnp.float32) + land_term).astype(jnp.bfloat16)
        first_out = run_section(seeded, qkv_weight[0], out_weight[0], norm_gain[0], offsets[0, 0], offsets[0, 1])
        second_out = run_section(first_out, qkv_weight[1], out_weight[1], norm_gain[1], offsets[1, 0], offsets[1, 1])
        first_list.append(first_out)
        second_list.append(second_out)
    return jnp.stack([jnp.stack(first_list), jnp.stack(second_list)])
```

```python
import functools
import math

import jax
import jax.numpy as jnp
from jax import lax
from jax.experimental import pallas as pl
from jax.experimental.pallas import tpu as pltpu
from jax.sharding import PartitionSpec as P

HEADS = 16
WLAT = 6
WLON = 12
HALF_LAT = WLAT // 2
HALF_LON = WLON // 2
CELLS = WLAT * WLON
QUAD = 16
PAIR = 128
NT = (((1,), (1,)), ((), ()))
F32 = jnp.float32
BF16 = jnp.bfloat16


def dot(a, b):
    return jnp.dot(a, b, preferred_element_type=F32)


def iota(shape, axis):
    return lax.broadcasted_iota(jnp.int32, shape, axis)


def based(offset, window):
    return jnp.where(offset >= window // 2, offset - window, offset)


def split_by(value, size, count):
    high = sum((value >= size * k).astype(jnp.int32) for k in range(1, count))
    return high, value - size * high


def quarter_cell(t):
    late = t >= 4 * QUAD
    quarter = jnp.where(late, (t - 4 * QUAD) >> 1, t >> 4)
    j = jnp.where(late, QUAD + (t & 1), t & (QUAD - 1))
    row, column = split_by(j, HALF_LON, 3)
    return HALF_LAT * (quarter >> 1) + row, HALF_LON * (quarter & 1) + column


def source(row, column, lat_sign, lon_sign):
    row_out = (row < 0) | (row >= WLAT)
    column_out = (column < 0) | (column >= WLON)
    row = jnp.where(row_out, row - WLAT * lat_sign, row)
    column = jnp.where(column_out, column - WLON * lon_sign, column)
    low, row = split_by(row, HALF_LAT, 2)
    right, column = split_by(column, HALF_LON, 2)
    base = jnp.where(
        row_out,
        jnp.where(column_out, 8 * QUAD, 4 * QUAD + QUAD * right),
        jnp.where(column_out, 6 * QUAD + QUAD * low, 2 * QUAD * low + QUAD * right),
    )
    return base, HALF_LON * row + column


def choosers(row, column, lat_sign, lon_sign, pieces, main_ref, tail_ref):
    base, j = source(row, column, lat_sign, lon_sign)
    count = row.shape[0]
    lane = iota((count, 9 * QUAD), 1)
    main_ref[...] = (lane == jnp.where(j < QUAD, base + j, -1)).astype(F32).astype(BF16)
    tail = jnp.where(j >= QUAD, base + j - QUAD, -1000)
    for piece in range(pieces):
        tail_ref[pl.ds(piece * count, count), :] = (lane == tail + 2 * piece).astype(F32).astype(BF16)


def gathered(block, main_ref, tail_ref, width, pieces):
    count = main_ref.shape[0]
    tail = dot(tail_ref[...], block[:, width:])
    tail = jnp.concatenate([tail[p * count : (p + 1) * count] for p in range(pieces)], axis=1)
    return dot(main_ref[...], block[:, :width]) + tail


def store_quarters(cells, ref, level, width, pieces):
    piece = width // pieces
    ref[level, pl.ds(0, 4 * QUAD), pl.ds(0, width)] = cells[: 4 * QUAD].astype(BF16)
    stack = jnp.concatenate([cells[4 * QUAD :, p * piece : (p + 1) * piece] for p in range(pieces)], axis=0)
    to, at = iota((4 * QUAD, 8 * pieces), 0), iota((4 * QUAD, 8 * pieces), 1)
    wanted = 8 * ((to & (QUAD - 1)) >> 1) + 2 * (to >> 4) + (to & 1)
    pick = (at == wanted).astype(F32).astype(BF16)
    ref[level, pl.ds(0, 4 * QUAD), pl.ds(width, piece)] = dot(pick, stack.astype(BF16)).astype(BF16)


def seeded_cells(level, latents_ref, mask_ref, embed_ref):
    embed = embed_ref[...].astype(F32)
    diagonal = iota((WLON, WLON), 0) == iota((WLON, WLON), 1)
    rows = []
    for row in range(WLAT):
        land = jnp.where(diagonal, mask_ref[row : row + 1, :].astype(F32), 0.0)
        land = jnp.sum(land, axis=1, keepdims=True)
        rows.append(latents_ref[level, row].astype(F32) + land * embed)
    cells = jnp.concatenate(rows, axis=0).astype(BF16)
    row, column = quarter_cell(iota((CELLS, CELLS), 0))
    order = (iota((CELLS, CELLS), 1) == WLON * row + column).astype(F32).astype(BF16)
    return dot(order, cells)


def attended(q, k, v, bias, head_size):
    cells = q.shape[0]
    first = iota((cells, PAIR), 1) < head_size
    ones = jnp.ones((cells, PAIR), BF16)
    pairs = [slice(p * PAIR, (p + 1) * PAIR) for p in range(q.shape[1] // PAIR)]
    scores = []
    for pair in pairs:
        zero = jnp.zeros((cells, PAIR), F32)
        both = jnp.concatenate([jnp.where(first, q[:, pair], zero), jnp.where(first, zero, q[:, pair])], axis=0)
        scores.append(lax.dot_general(both.astype(BF16), k[:, pair].astype(BF16), NT, preferred_element_type=F32))
    weights = []
    for score in scores:
        score = score + bias
        weights.append(jnp.exp(score - jnp.max(score, axis=-1, keepdims=True)).astype(BF16))
    sums = [
        dot(weight, jnp.concatenate([v[:, pair].astype(BF16), ones], axis=1))
        for weight, pair in zip(weights, pairs)
    ]
    parts = []
    for both in sums:
        value = jnp.where(first, both[:cells, :PAIR], both[cells:, :PAIR])
        total = jnp.where(first, both[:cells, PAIR:], both[cells:, PAIR:])
        parts.append((value / total).astype(BF16))
    return jnp.concatenate(parts, axis=1)


def section(x, bias, wqkv, wout, gain):
    width = x.shape[1]
    head_size = width // HEADS
    q = dot(x, wqkv[:, :width]) * (1.0 / math.sqrt(head_size))
    k = dot(x, wqkv[:, width : 2 * width])
    v = dot(x, wqkv[:, 2 * width :])
    projected = dot(attended(q, k, v, bias, head_size), wout[...])
    centered = projected - jnp.mean(projected, axis=-1, keepdims=True)
    variance = jnp.mean(centered * centered, axis=-1, keepdims=True)
    branch = centered * lax.rsqrt(variance + 1e-05) * gain
    return x.astype(F32) + branch


def kernel(
    lat_signs, lon_signs,
    offsets_ref, latents_ref, mask_ref, embed_ref, wqkv_hbm, wout_hbm, gain_ref, out_ref,
    entering, leaving, wqkv, wout, main_in, tail_in, main_out, tail_out, bias,
    weight_sem, send_sem, recv_sem, cross_send, cross_recv,
):
    segment, lon, lat = (lax.axis_index(axis) for axis in ("segment", "lon", "lat"))
    lons, lats = lax.axis_size("lon"), lax.axis_size("lat")
    levels = latents_ref.shape[0]
    width = latents_ref.shape[-1]
    pieces = width // PAIR
    at = lambda a, b: (segment, lax.rem(lon + b + lons, lons), lax.rem(lat + a + lats, lats))
    pick = lambda pair: pair[0] + segment * (pair[1] - pair[0])

    loads = [
        pltpu.make_async_copy(wqkv_hbm.at[0], wqkv, weight_sem.at[0]),
        pltpu.make_async_copy(wout_hbm.at[0], wout, weight_sem.at[1]),
    ]
    for load in loads:
        load.start()
    across = (1 - segment, lon, lat)
    partners = [at(a, b) for a in (-1, 0, 1) for b in (-1, 0, 1) if (a, b) != (0, 0)] + [across]
    barrier = pltpu.get_barrier_semaphore()
    for partner in partners:
        pl.semaphore_signal(barrier, inc=1, device_id=partner, device_id_type=pl.DeviceIdType.MESH)

    def exchange(index, ref, level):
        a, b = pick(lat_signs[index]), pick(lon_signs[index])
        low, right = (1 - a) // 2, (1 - b) // 2
        plan = (
            (2 * QUAD * low, 2 * QUAD, 4 * QUAD, at(-a, 0)),
            (QUAD * right, QUAD, 6 * QUAD, at(0, -b)),
            (2 * QUAD + QUAD * right, QUAD, 7 * QUAD, at(0, -b)),
            (2 * QUAD * low + QUAD * right, QUAD, 8 * QUAD, at(-a, -b)),
        )
        return [
            pltpu.make_async_remote_copy(
                src_ref=ref.at[level, pl.ds(pl.multiple_of(start, QUAD), count)],
                dst_ref=ref.at[level, pl.ds(target, count)],
                send_sem=send_sem.at[index, level, slot],
                recv_sem=recv_sem.at[index, level, slot],
                device_id=device,
                device_id_type=pl.DeviceIdType.MESH,
            )
            for slot, (start, count, target, device) in enumerate(plan)
        ]

    def crossing(level):
        return pltpu.make_async_remote_copy(
            src_ref=leaving.at[level, pl.ds(0, 4 * QUAD)],
            dst_ref=entering.at[level, pl.ds(0, 4 * QUAD)],
            send_sem=cross_send.at[level],
            recv_sem=cross_recv.at[level],
            device_id=across,
            device_id_type=pl.DeviceIdType.MESH,
        )

    def each_level(step):
        def run(level, carry):
            step(level)
            return carry

        lax.fori_loop(0, levels, run, 0)

    @pl.when(segment == 0)
    def _():
        def seed(level):
            store_quarters(seeded_cells(level, latents_ref, mask_ref, embed_ref), entering, level, width, pieces)

        each_level(seed)

    pl.semaphore_wait(barrier, len(partners))

    def enter(level):
        for copy in exchange(0, entering, level):
            copy.start()

    @pl.when(segment == 0)
    def _():
        each_level(enter)

    lat_base = [based(offsets_ref[s, 0], WLAT) for s in (0, 1)]
    lon_base = [based(offsets_ref[s, 1], WLON) for s in (0, 1)]
    first = segment == 0
    lat_own, lon_own = jnp.where(first, lat_base[0], lat_base[1]), jnp.where(first, lon_base[0], lon_base[1])
    lat_in = jnp.where(first, lat_base[0], lat_base[1] - lat_base[0])
    lon_in = jnp.where(first, lon_base[0], lon_base[1] - lon_base[0])
    offset = jnp.where(first, offsets_ref[0, 0], offsets_ref[1, 0])

    row, column = quarter_cell(iota((CELLS, 1), 0))
    choosers(row + lat_in, column + lon_in, pick(lat_signs[0]), pick(lon_signs[0]), pieces, main_in, tail_in)
    line = iota((WLAT * QUAD, 1), 0)
    row, column = line >> 4, jnp.minimum(line & (QUAD - 1), WLON - 1)
    choosers(row - lat_own, column - lon_own, pick(lat_signs[1]), pick(lon_signs[1]), pieces, main_out, tail_out)

    def wrapped(shape, axis):
        row, _ = quarter_cell(iota(shape, axis))
        held = lat * WLAT + lat_own + row
        held = jnp.where(held < 0, held + lats * WLAT, held)
        held = jnp.where(held >= lats * WLAT, held - lats * WLAT, held)
        return (held < offset).astype(jnp.int32)

    excluded = jnp.where(wrapped((CELLS, 1), 0) == wrapped((1, CELLS), 1), 0.0, -1e30)
    bias[pl.ds(0, CELLS), :] = excluded
    bias[pl.ds(CELLS, CELLS), :] = excluded
    for load in loads:
        load.wait()

    @pl.when(segment == 1)
    def _():
        def forward(level):
            crossing(level).wait_recv()
            enter(level)

        each_level(forward)

    gain = jnp.where(first, gain_ref[0:1, :], gain_ref[1:2, :])

    def work(level):
        for copy in exchange(0, entering, level):
            copy.wait_recv()
        x = gathered(entering[level], main_in, tail_in, width, pieces).astype(BF16)
        store_quarters(section(x, bias[...], wqkv, wout, gain), leaving, level, width, pieces)

        @pl.when(segment == 0)
        def _():
            crossing(level).start()

        for copy in exchange(1, leaving, level):
            copy.start()

    each_level(work)

    def finish(level):
        for copy in exchange(1, leaving, level):
            copy.wait_recv()
        cells = gathered(leaving[level], main_out, tail_out, width, pieces).astype(BF16)
        for row in range(WLAT):
            out_ref[0, level, row] = cells[row * QUAD : row * QUAD + WLON]

    each_level(finish)

    def settle(level):
        for index, ref in enumerate((entering, leaving)):
            for copy in exchange(index, ref, level):
                copy.wait_send()

        @pl.when(segment == 0)
        def _():
            crossing(level).wait_send()

    each_level(settle)


def sections(variant, offsets, latents, land_mask, land_embed, qkv_weight, out_weight, norm_gain):
    levels, _, _, width = latents.shape
    second_known = variant >= 4
    signs = []
    for bit in (2, 1):
        other = -1 if variant & bit else 1
        if second_known:
            entering, leaving = (other, -other), (-other, 1)
        else:
            entering, leaving = (-1, other), (1, -other)
        signs.append((entering, leaving))
    pieces = width // PAIR
    in_vmem = pl.BlockSpec(memory_space=pltpu.VMEM)
    in_hbm = pl.BlockSpec(memory_space=pl.ANY)
    block = (levels, 9 * QUAD, width + PAIR)
    return pl.pallas_call(
        functools.partial(kernel, signs[0], signs[1]),
        out_shape=jax.ShapeDtypeStruct((1,) + latents.shape, BF16),
        in_specs=[pl.BlockSpec(memory_space=pltpu.SMEM), in_vmem, in_vmem, in_vmem, in_hbm, in_hbm, in_vmem],
        out_specs=in_vmem,
        scratch_shapes=[
            pltpu.VMEM(block, BF16),
            pltpu.VMEM(block, BF16),
            pltpu.VMEM(qkv_weight.shape[1:], BF16),
            pltpu.VMEM(out_weight.shape[1:], BF16),
            pltpu.VMEM((CELLS, 9 * QUAD), BF16),
            pltpu.VMEM((CELLS * pieces, 9 * QUAD), BF16),
            pltpu.VMEM((WLAT * QUAD, 9 * QUAD), BF16),
            pltpu.VMEM((WLAT * QUAD * pieces, 9 * QUAD), BF16),
            pltpu.VMEM((2 * CELLS, CELLS), F32),
            pltpu.SemaphoreType.DMA((2,)),
            pltpu.SemaphoreType.DMA((2, levels, 4)),
            pltpu.SemaphoreType.DMA((2, levels, 4)),
            pltpu.SemaphoreType.DMA((levels,)),
            pltpu.SemaphoreType.DMA((levels,)),
        ],
        compiler_params=pltpu.CompilerParams(
            collective_id=variant, has_side_effects=True, vmem_limit_bytes=48 * 1024 * 1024
        ),
    )(offsets, latents, land_mask, land_embed, qkv_weight, out_weight, norm_gain)


def body(latents, land_mask, land_embed, qkv_weight, out_weight, norm_gain, offsets):
    assert latents.shape[1:3] == (WLAT, WLON)
    window = jnp.array([[WLAT, WLON]], jnp.int32)
    negative = (2 * offsets >= window).astype(jnp.int32) * jnp.array([[2, 1], [8, 4]], jnp.int32)
    unusual = (offsets[0:1] != window - 1).astype(jnp.int32) * 16
    code = jnp.sum(negative + jnp.pad(unusual, ((0, 1), (0, 0))))
    variant = jnp.where(code >= 16, 4 + (code & 3), (code >> 2) & 3)
    ways = [functools.partial(sections, v) for v in range(8)]
    return lax.switch(
        variant, ways, offsets, latents, land_mask, land_embed.reshape(1, -1), qkv_weight, out_weight, norm_gain
    )


def solution(mesh):
    return jax.shard_map(
        body,
        mesh=mesh,
        in_specs=(
            P(None, "lat", "lon", None),
            P("lat", "lon"),
            P(),
            P("segment", None, None),
            P("segment", None, None),
            P(),
            P(),
        ),
        out_specs=P("segment", None, "lat", "lon", None),
        check_vma=False,
    )
```

```python
import functools
import math

import jax
import jax.numpy as jnp
from jax import lax
from jax.experimental import pallas as pl
from jax.experimental.pallas import tpu as pltpu
from jax.sharding import PartitionSpec as P

HEADS = 16
WLAT = 6
WLON = 12
HALF_LAT = WLAT // 2
HALF_LON = WLON // 2
CELLS = WLAT * WLON
QUAD = 16
PAIR = 128
NT = (((1,), (1,)), ((), ()))
F32 = jnp.float32
BF16 = jnp.bfloat16


def dot(a, b):
    return jnp.dot(a, b, preferred_element_type=F32)


def iota(shape, axis):
    return lax.broadcasted_iota(jnp.int32, shape, axis)


def based(offset, window):
    return jnp.where(offset >= window // 2, offset - window, offset)


def split_by(value, size, count):
    high = sum((value >= size * k).astype(jnp.int32) for k in range(1, count))
    return high, value - size * high


def quarter_cell(t):
    late = t >= 4 * QUAD
    quarter = jnp.where(late, (t - 4 * QUAD) >> 1, t >> 4)
    j = jnp.where(late, QUAD + (t & 1), t & (QUAD - 1))
    row, column = split_by(j, HALF_LON, 3)
    return HALF_LAT * (quarter >> 1) + row, HALF_LON * (quarter & 1) + column


def source(row, column, lat_sign, lon_sign):
    row_out = (row < 0) | (row >= WLAT)
    column_out = (column < 0) | (column >= WLON)
    row = jnp.where(row_out, row - WLAT * lat_sign, row)
    column = jnp.where(column_out, column - WLON * lon_sign, column)
    low, row = split_by(row, HALF_LAT, 2)
    right, column = split_by(column, HALF_LON, 2)
    base = jnp.where(
        row_out,
        jnp.where(column_out, 8 * QUAD, 4 * QUAD + QUAD * right),
        jnp.where(column_out, 6 * QUAD + QUAD * low, 2 * QUAD * low + QUAD * right),
    )
    return base, HALF_LON * row + column


def choosers(row, column, lat_sign, lon_sign, pieces, main_ref, tail_ref, wanted=None):
    base, j = source(row, column, lat_sign, lon_sign)
    if wanted is not None:
        base = jnp.where(wanted, base, -2000)
    count = row.shape[0]
    lane = iota((count, 9 * QUAD), 1)
    main_ref[...] = (lane == jnp.where(j < QUAD, base + j, -1000)).astype(F32).astype(BF16)
    tail = jnp.where(j >= QUAD, base + j - QUAD, -1000)
    for piece in range(pieces):
        tail_ref[pl.ds(piece * count, count), :] = (lane == tail + 2 * piece).astype(F32).astype(BF16)


def gathered(block, main_ref, tail_ref, width, pieces):
    count = main_ref.shape[0]
    tail = dot(tail_ref[...], block[:, width:])
    tail = jnp.concatenate([tail[p * count : (p + 1) * count] for p in range(pieces)], axis=1)
    return dot(main_ref[...], block[:, :width]) + tail


def store_quarters(cells, ref, level, width, pieces):
    cells = cells.astype(F32)
    piece = width // pieces
    ref[level, pl.ds(0, 4 * QUAD), pl.ds(0, width)] = cells[: 4 * QUAD].astype(BF16)
    stack = jnp.concatenate([cells[4 * QUAD :, p * piece : (p + 1) * piece] for p in range(pieces)], axis=0)
    to, at = iota((4 * QUAD, 8 * pieces), 0), iota((4 * QUAD, 8 * pieces), 1)
    wanted = 8 * ((to & (QUAD - 1)) >> 1) + 2 * (to >> 4) + (to & 1)
    pick = (at == wanted).astype(F32).astype(BF16)
    ref[level, pl.ds(0, 4 * QUAD), pl.ds(width, piece)] = dot(pick, stack.astype(BF16)).astype(BF16)


def seed(entering, latents_ref, mask_ref, embed_ref, pieces):
    levels, width = latents_ref.shape[2:]
    embed = embed_ref[...].astype(F32).reshape(1, width)
    across = WLON * levels
    spread = iota((across, WLON), 0)
    spread = (spread >= levels * iota((across, WLON), 1)) & (spread < levels * iota((across, WLON), 1) + levels)
    rows = []
    for row in range(WLAT):
        land = jnp.where(spread, mask_ref[row : row + 1, :].astype(F32), 0.0)
        land = jnp.sum(land, axis=1, keepdims=True)
        rows.append(latents_ref[row].astype(F32).reshape(across, width) + land * embed)
    cells = jnp.concatenate(rows, axis=0).astype(BF16)
    row, column = quarter_cell(iota((CELLS, CELLS * levels), 0))
    wanted = levels * (WLON * row + column)
    at = iota((CELLS, CELLS * levels), 1)
    for level in range(levels):
        order = (at == wanted + level).astype(F32).astype(BF16)
        store_quarters(dot(order, cells), entering, level, width, pieces)


def attended(q, k, v, bias, head_size):
    cells = q.shape[0]
    first = iota((cells, PAIR), 1) < head_size
    ones = jnp.ones((cells, PAIR), BF16)
    pairs = [slice(p * PAIR, (p + 1) * PAIR) for p in range(q.shape[1] // PAIR)]
    scores = []
    for pair in pairs:
        zero = jnp.zeros((cells, PAIR), F32)
        both = jnp.concatenate([jnp.where(first, q[:, pair], zero), jnp.where(first, zero, q[:, pair])], axis=0)
        scores.append(lax.dot_general(both.astype(BF16), k[:, pair].astype(BF16), NT, preferred_element_type=F32))
    weights = []
    for score in scores:
        score = score + bias
        weights.append(jnp.exp(score - jnp.max(score, axis=-1, keepdims=True)).astype(BF16))
    sums = [
        dot(weight, jnp.concatenate([v[:, pair].astype(BF16), ones], axis=1))
        for weight, pair in zip(weights, pairs)
    ]
    parts = []
    for both in sums:
        value = jnp.where(first, both[:cells, :PAIR], both[cells:, :PAIR])
        total = jnp.where(first, both[:cells, PAIR:], both[cells:, PAIR:])
        parts.append((value / total).astype(BF16))
    return jnp.concatenate(parts, axis=1)


def section(x, bias, wqkv, wout, gain):
    width = x.shape[1]
    head_size = width // HEADS
    q = dot(x, wqkv[:, :width]) * (1.0 / math.sqrt(head_size))
    k = dot(x, wqkv[:, width : 2 * width])
    v = dot(x, wqkv[:, 2 * width :])
    projected = dot(attended(q, k, v, bias, head_size), wout[...])
    centered = projected - jnp.mean(projected, axis=-1, keepdims=True)
    variance = jnp.mean(centered * centered, axis=-1, keepdims=True)
    branch = centered * lax.rsqrt(variance + 1e-05) * gain
    return x.astype(F32) + branch


def kernel(
    lat_signs, lon_signs,
    offsets_ref, latents_ref, mask_ref, embed_ref, wqkv_hbm, wout_hbm, gain_ref, out_ref,
    entering, leaving, wqkv, wout, main_in, tail_in, main_out, tail_out, bias, total,
    weight_sem, send_sem, recv_sem, cross_send, cross_recv,
):
    segment, lon, lat = (lax.axis_index(axis) for axis in ("segment", "lon", "lat"))
    lons, lats = lax.axis_size("lon"), lax.axis_size("lat")
    levels, width = latents_ref.shape[2:]
    pieces = width // PAIR
    at = lambda a, b: (segment, lax.rem(lon + b + lons, lons), lax.rem(lat + a + lats, lats))
    pick = lambda pair: pair[0] + segment * (pair[1] - pair[0])

    loads = [
        pltpu.make_async_copy(wqkv_hbm.at[0], wqkv, weight_sem.at[0]),
        pltpu.make_async_copy(wout_hbm.at[0], wout, weight_sem.at[1]),
    ]
    for load in loads:
        load.start()
    across = (1 - segment, lon, lat)
    partners = [at(a, b) for a in (-1, 0, 1) for b in (-1, 0, 1) if (a, b) != (0, 0)] + [across]
    barrier = pltpu.get_barrier_semaphore()
    for partner in partners:
        pl.semaphore_signal(barrier, inc=1, device_id=partner, device_id_type=pl.DeviceIdType.MESH)

    def exchange(index, ref, level):
        a, b = pick(lat_signs[index]), pick(lon_signs[index])
        low, right = (1 - a) // 2, (1 - b) // 2
        plan = (
            (2 * QUAD * low, 2 * QUAD, 4 * QUAD, at(-a, 0)),
            (QUAD * right, QUAD, 6 * QUAD, at(0, -b)),
            (2 * QUAD + QUAD * right, QUAD, 7 * QUAD, at(0, -b)),
            (2 * QUAD * low + QUAD * right, QUAD, 8 * QUAD, at(-a, -b)),
        )
        return [
            pltpu.make_async_remote_copy(
                src_ref=ref.at[level, pl.ds(pl.multiple_of(start, QUAD), count)],
                dst_ref=ref.at[level, pl.ds(target, count)],
                send_sem=send_sem.at[index, level, slot],
                recv_sem=recv_sem.at[index, level, slot],
                device_id=device,
                device_id_type=pl.DeviceIdType.MESH,
            )
            for slot, (start, count, target, device) in enumerate(plan)
        ]

    low_next = (1 - lat_signs[0][1]) // 2

    def crossing(level, part):
        rows = pl.ds(2 * QUAD * (low_next if part == 0 else 1 - low_next), 2 * QUAD)
        return pltpu.make_async_remote_copy(
            src_ref=leaving.at[level, rows],
            dst_ref=entering.at[level, rows],
            send_sem=cross_send.at[level, part],
            recv_sem=cross_recv.at[level, part],
            device_id=across,
            device_id_type=pl.DeviceIdType.MESH,
        )

    def each_level(step):
        def run(level, carry):
            step(level)
            return carry

        lax.fori_loop(0, levels, run, 0)

    @pl.when(segment == 0)
    def _():
        seed(entering, latents_ref, mask_ref, embed_ref, pieces)

    pl.semaphore_wait(barrier, len(partners))

    def enter(level):
        for copy in exchange(0, entering, level):
            copy.start()

    @pl.when(segment == 0)
    def _():
        each_level(enter)

    lat_base = [based(offsets_ref[s, 0], WLAT) for s in (0, 1)]
    lon_base = [based(offsets_ref[s, 1], WLON) for s in (0, 1)]
    first = segment == 0
    lat_own, lon_own = jnp.where(first, lat_base[0], lat_base[1]), jnp.where(first, lon_base[0], lon_base[1])
    lat_in = jnp.where(first, lat_base[0], lat_base[1] - lat_base[0])
    lon_in = jnp.where(first, lon_base[0], lon_base[1] - lon_base[0])
    offset = jnp.where(first, offsets_ref[0, 0], offsets_ref[1, 0])

    row, column = quarter_cell(iota((CELLS, 1), 0))
    choosers(row + lat_in, column + lon_in, pick(lat_signs[0]), pick(lon_signs[0]), pieces, main_in, tail_in)
    line = iota((CELLS * levels, 1), 0)
    row, column = split_by(line, WLON * levels, WLAT)
    column, held_level = split_by(column, levels, WLON)
    for level in range(levels):
        choosers(
            row - lat_own, column - lon_own, pick(lat_signs[1]), pick(lon_signs[1]),
            pieces, main_out.at[level], tail_out.at[level], held_level == level,
        )

    def wrapped(shape, axis):
        row, _ = quarter_cell(iota(shape, axis))
        held = lat * WLAT + lat_own + row
        held = jnp.where(held < 0, held + lats * WLAT, held)
        held = jnp.where(held >= lats * WLAT, held - lats * WLAT, held)
        return (held < offset).astype(jnp.int32)

    excluded = jnp.where(wrapped((CELLS, 1), 0) == wrapped((1, CELLS), 1), 0.0, -1e30)
    bias[pl.ds(0, CELLS), :] = excluded
    bias[pl.ds(CELLS, CELLS), :] = excluded
    for load in loads:
        load.wait()

    @pl.when(segment == 1)
    def _():
        def forward(level):
            copies = exchange(0, entering, level)
            crossing(level, 0).wait_recv()
            for slot in (0, 3, 1 + low_next):
                copies[slot].start()
            crossing(level, 1).wait_recv()
            copies[2 - low_next].start()

        each_level(forward)

    gain = jnp.where(first, gain_ref[0:1, :], gain_ref[1:2, :])

    def work(level):
        for copy in exchange(0, entering, level):
            copy.wait_recv()
        x = gathered(entering[level], main_in, tail_in, width, pieces).astype(BF16)
        store_quarters(section(x, bias[...], wqkv, wout, gain), leaving, level, width, pieces)

        @pl.when(segment == 0)
        def _():
            for part in (0, 1):
                crossing(level, part).start()

        for copy in exchange(1, leaving, level):
            copy.start()

    each_level(work)

    total[...] = jnp.zeros_like(total)

    def finish(level):
        for copy in exchange(1, leaving, level):
            copy.wait_recv()
        total[...] += gathered(leaving[level], main_out.at[level], tail_out.at[level], width, pieces)

    each_level(finish)
    out_ref[...] = total[...].astype(BF16).reshape(out_ref.shape)

    def settle(level):
        for index, ref in enumerate((entering, leaving)):
            for copy in exchange(index, ref, level):
                copy.wait_send()

        @pl.when(segment == 0)
        def _():
            for part in (0, 1):
                crossing(level, part).wait_send()

    each_level(settle)


def sections(variant, offsets, latents, land_mask, land_embed, qkv_weight, out_weight, norm_gain):
    _, _, levels, width = latents.shape
    second_known = variant >= 4
    signs = []
    for bit in (2, 1):
        other = -1 if variant & bit else 1
        if second_known:
            entering, leaving = (other, -other), (-other, 1)
        else:
            entering, leaving = (-1, other), (1, -other)
        signs.append((entering, leaving))
    pieces = width // PAIR
    in_vmem = pl.BlockSpec(memory_space=pltpu.VMEM)
    in_hbm = pl.BlockSpec(memory_space=pl.ANY)
    block = (levels, 9 * QUAD, width + PAIR)
    return pl.pallas_call(
        functools.partial(kernel, signs[0], signs[1]),
        out_shape=jax.ShapeDtypeStruct(latents.shape, BF16),
        in_specs=[pl.BlockSpec(memory_space=pltpu.SMEM), in_vmem, in_vmem, in_vmem, in_hbm, in_hbm, in_vmem],
        out_specs=in_vmem,
        scratch_shapes=[
            pltpu.VMEM(block, BF16),
            pltpu.VMEM(block, BF16),
            pltpu.VMEM(qkv_weight.shape[1:], BF16),
            pltpu.VMEM(out_weight.shape[1:], BF16),
            pltpu.VMEM((CELLS, 9 * QUAD), BF16),
            pltpu.VMEM((CELLS * pieces, 9 * QUAD), BF16),
            pltpu.VMEM((levels, CELLS * levels, 9 * QUAD), BF16),
            pltpu.VMEM((levels, CELLS * levels * pieces, 9 * QUAD), BF16),
            pltpu.VMEM((2 * CELLS, CELLS), F32),
            pltpu.VMEM((CELLS * levels, width), F32),
            pltpu.SemaphoreType.DMA((2,)),
            pltpu.SemaphoreType.DMA((2, levels, 4)),
            pltpu.SemaphoreType.DMA((2, levels, 4)),
            pltpu.SemaphoreType.DMA((levels, 2)),
            pltpu.SemaphoreType.DMA((levels, 2)),
        ],
        compiler_params=pltpu.CompilerParams(
            collective_id=variant, has_side_effects=True, vmem_limit_bytes=48 * 1024 * 1024
        ),
    )(offsets, latents, land_mask, land_embed, qkv_weight, out_weight, norm_gain)


def body(latents, land_mask, land_embed, qkv_weight, out_weight, norm_gain, offsets):
    assert latents.shape[1:3] == (WLAT, WLON)
    lat_part, lon_part = offsets[:, 0:1], offsets[:, 1:2]
    signs = 2 * (lat_part >= HALF_LAT).astype(jnp.int32) + (lon_part >= HALF_LON).astype(jnp.int32)
    known = (lat_part == WLAT - 1) & (lon_part == WLON - 1)
    term = jnp.where(iota((2, 1), 0) == 0, jnp.where(known, 0, 1 + signs), signs)
    variant = jnp.sum(term)
    ways = [functools.partial(sections, v) for v in range(8)]
    out = lax.switch(
        variant, ways,
        offsets, latents.transpose(1, 2, 0, 3), land_mask, land_embed, qkv_weight, out_weight, norm_gain,
    )
    return out.transpose(2, 0, 1, 3)[None]


def solution(mesh):
    return jax.shard_map(
        body,
        mesh=mesh,
        in_specs=(
            P(None, "lat", "lon", None),
            P("lat", "lon"),
            P(),
            P("segment", None, None),
            P("segment", None, None),
            P(),
            P(),
        ),
        out_specs=P("segment", None, "lat", "lon", None),
        check_vma=False,
    )
```

```python
import functools
import math

import jax
import jax.numpy as jnp
from jax import lax
from jax.experimental import pallas as pl
from jax.experimental.pallas import tpu as pltpu
from jax.sharding import PartitionSpec as P

HEADS = 16
WLAT = 6
WLON = 12
HALF_LAT = WLAT // 2
HALF_LON = WLON // 2
CELLS = WLAT * WLON
QUAD = 16
PAIR = 128
NT = (((1,), (1,)), ((), ()))
F32 = jnp.float32
BF16 = jnp.bfloat16


def dot(a, b):
    return jnp.dot(a, b, preferred_element_type=F32)


def iota(shape, axis):
    return lax.broadcasted_iota(jnp.int32, shape, axis)


def based(offset, window):
    return jnp.where(offset >= window // 2, offset - window, offset)


def split_by(value, size, count):
    high = sum((value >= size * k).astype(jnp.int32) for k in range(1, count))
    return high, value - size * high


def quarter_cell(t):
    late = t >= 4 * QUAD
    quarter = jnp.where(late, (t - 4 * QUAD) >> 1, t >> 4)
    j = jnp.where(late, QUAD + (t & 1), t & (QUAD - 1))
    row, column = split_by(j, HALF_LON, 3)
    return HALF_LAT * (quarter >> 1) + row, HALF_LON * (quarter & 1) + column


def source(row, column, lat_sign, lon_sign, small):
    row_out = (row < 0) | (row >= WLAT)
    column_out = (column < 0) | (column >= WLON)
    row = jnp.where(row_out, row - WLAT * lat_sign, row)
    column = jnp.where(column_out, column - WLON * lon_sign, column)
    low, near_row = split_by(row, HALF_LAT, 2)
    right, near_column = split_by(column, HALF_LON, 2)
    base = jnp.where(
        row_out,
        jnp.where(column_out, 8 * QUAD, 4 * QUAD + QUAD * right),
        jnp.where(column_out, 6 * QUAD + QUAD * low, 2 * QUAD * low + QUAD * right),
    )
    j = HALF_LON * near_row + near_column
    if small is None:
        return base, j
    inside = ~(row_out | column_out)
    small_base = jnp.where(row_out, jnp.where(column_out, 8 * QUAD, 4 * QUAD), 6 * QUAD)
    small_j = jnp.where(row_out, jnp.where(column_out, QUAD, column), row)
    whole = inside | jnp.logical_not(small)
    return jnp.where(whole, base, small_base), jnp.where(whole, j, small_j)


def choosers(row, column, lat_sign, lon_sign, small, pieces, main_ref, tail_ref, wanted=None):
    base, j = source(row, column, lat_sign, lon_sign, small)
    if wanted is not None:
        base = jnp.where(wanted, base, -2000)
    count = row.shape[0]
    lane = iota((count, 9 * QUAD), 1)
    main_ref[...] = (lane == jnp.where(j < QUAD, base + j, -1000)).astype(F32).astype(BF16)
    tail = jnp.where(j >= QUAD, base + j - QUAD, -1000)
    for piece in range(pieces):
        tail_ref[pl.ds(piece * count, count), :] = (lane == tail + 2 * piece).astype(F32).astype(BF16)


def gathered(block, main_ref, tail_ref, width, pieces):
    count = main_ref.shape[0]
    tail = dot(tail_ref[...], block[:, width:])
    tail = jnp.concatenate([tail[p * count : (p + 1) * count] for p in range(pieces)], axis=1)
    return dot(main_ref[...], block[:, :width]) + tail


def store_quarters(cells, ref, level, width, pieces):
    cells = cells.astype(F32)
    piece = width // pieces
    ref[level, pl.ds(0, 4 * QUAD), pl.ds(0, width)] = cells[: 4 * QUAD].astype(BF16)
    stack = jnp.concatenate([cells[4 * QUAD :, p * piece : (p + 1) * piece] for p in range(pieces)], axis=0)
    to, at = iota((4 * QUAD, 8 * pieces), 0), iota((4 * QUAD, 8 * pieces), 1)
    wanted = 8 * ((to & (QUAD - 1)) >> 1) + 2 * (to >> 4) + (to & 1)
    pick = (at == wanted).astype(F32).astype(BF16)
    ref[level, pl.ds(0, 4 * QUAD), pl.ds(width, piece)] = dot(pick, stack.astype(BF16)).astype(BF16)


def store_edges(cells, lat_sign, lon_sign, line_ref, corner_ref, level, pieces):
    row_at, column_at = (0 if lat_sign > 0 else WLAT - 1), (0 if lon_sign > 0 else WLON - 1)
    to = iota((2 * QUAD, CELLS), 0)
    row, column = quarter_cell(iota((2 * QUAD, CELLS), 1))
    pick = ((row == row_at) & (column == to)) | ((column == column_at) & (row == to - QUAD))
    line_ref[level] = dot(pick.astype(F32).astype(BF16), cells.astype(BF16)).astype(BF16)
    half = HALF_LON * (row_at % HALF_LAT) + column_at % HALF_LON
    quarter = 2 * (row_at // HALF_LAT) + column_at // HALF_LON
    place = QUAD * quarter + half if half < QUAD else 4 * QUAD + 2 * quarter + half - QUAD
    piece = cells.shape[1] // pieces
    line = iota((QUAD, piece), 0)
    corner = jnp.zeros((QUAD, piece), F32)
    for p in range(pieces):
        corner = jnp.where(line == 2 * p, cells[place : place + 1, p * piece : (p + 1) * piece], corner)
    corner_ref[level] = corner.astype(BF16)


def seed(entering, latents_ref, mask_ref, embed_ref, pieces, edges):
    levels, width = latents_ref.shape[2:]
    embed = embed_ref[...].astype(F32).reshape(1, width)
    across = WLON * levels
    spread = iota((across, WLON), 0)
    spread = (spread >= levels * iota((across, WLON), 1)) & (spread < levels * iota((across, WLON), 1) + levels)
    rows = []
    for row in range(WLAT):
        land = jnp.where(spread, mask_ref[row : row + 1, :].astype(F32), 0.0)
        land = jnp.sum(land, axis=1, keepdims=True)
        rows.append(latents_ref[row].astype(F32).reshape(across, width) + land * embed)
    cells = jnp.concatenate(rows, axis=0).astype(BF16)
    row, column = quarter_cell(iota((CELLS, CELLS * levels), 0))
    wanted = levels * (WLON * row + column)
    at = iota((CELLS, CELLS * levels), 1)
    for level in range(levels):
        order = (at == wanted + level).astype(F32).astype(BF16)
        ordered = dot(order, cells)
        store_quarters(ordered, entering, level, width, pieces)
        edges(ordered, level)


def attended(q, k, v, bias, head_size):
    cells = q.shape[0]
    first = iota((cells, PAIR), 1) < head_size
    ones = jnp.ones((cells, PAIR), BF16)
    pairs = [slice(p * PAIR, (p + 1) * PAIR) for p in range(q.shape[1] // PAIR)]
    scores = []
    for pair in pairs:
        zero = jnp.zeros((cells, PAIR), F32)
        both = jnp.concatenate([jnp.where(first, q[:, pair], zero), jnp.where(first, zero, q[:, pair])], axis=0)
        scores.append(lax.dot_general(both.astype(BF16), k[:, pair].astype(BF16), NT, preferred_element_type=F32))
    weights = []
    for score in scores:
        score = score + bias
        weights.append(jnp.exp(score - jnp.max(score, axis=-1, keepdims=True)).astype(BF16))
    sums = [
        dot(weight, jnp.concatenate([v[:, pair].astype(BF16), ones], axis=1))
        for weight, pair in zip(weights, pairs)
    ]
    parts = []
    for both in sums:
        value = jnp.where(first, both[:cells, :PAIR], both[cells:, :PAIR])
        total = jnp.where(first, both[:cells, PAIR:], both[cells:, PAIR:])
        parts.append((value / total).astype(BF16))
    return jnp.concatenate(parts, axis=1)


def section(x, bias, wqkv, wout, gain):
    width = x.shape[1]
    head_size = width // HEADS
    q = dot(x, wqkv[:, :width]) * (1.0 / math.sqrt(head_size))
    k = dot(x, wqkv[:, width : 2 * width])
    v = dot(x, wqkv[:, 2 * width :])
    projected = dot(attended(q, k, v, bias, head_size), wout[...])
    centered = projected - jnp.mean(projected, axis=-1, keepdims=True)
    variance = jnp.mean(centered * centered, axis=-1, keepdims=True)
    branch = centered * lax.rsqrt(variance + 1e-05) * gain
    return x.astype(F32) + branch


def kernel(
    lat_signs, lon_signs, small_step,
    offsets_hbm, latents_hbm, mask_hbm, embed_hbm, wqkv_hbm, wout_hbm, gain_hbm, out_ref,
    offsets_ref, latents_ref, mask_ref, embed_ref, gain_ref,
    entering, leaving, lines, corners, wqkv, wout, main_in, tail_in, main_out, tail_out, bias, total,
    load_sem, send_sem, recv_sem, cross_send, cross_recv,
):
    segment, lon, lat = (lax.axis_index(axis) for axis in ("segment", "lon", "lat"))
    lons, lats = lax.axis_size("lon"), lax.axis_size("lat")
    levels, width = latents_ref.shape[2:]
    pieces = width // PAIR
    at = lambda a, b: (segment, lax.rem(lon + b + lons, lons), lax.rem(lat + a + lats, lats))
    pick = lambda pair: pair[0] + segment * (pair[1] - pair[0])

    across = (1 - segment, lon, lat)
    partners = [at(a, b) for a in (-1, 0, 1) for b in (-1, 0, 1) if (a, b) != (0, 0)] + [across]
    barrier = pltpu.get_barrier_semaphore()
    for partner in partners:
        pl.semaphore_signal(barrier, inc=1, device_id=partner, device_id_type=pl.DeviceIdType.MESH)

    def load(slot, source_ref, target_ref):
        return pltpu.make_async_copy(source_ref, target_ref, load_sem.at[slot])

    seeds = [load(0, latents_hbm, latents_ref), load(1, mask_hbm, mask_ref), load(2, embed_hbm, embed_ref)]
    shifts, gains = load(3, offsets_hbm, offsets_ref), load(4, gain_hbm, gain_ref)
    weights = [load(5, wqkv_hbm.at[0], wqkv), load(6, wout_hbm.at[0], wout)]

    @pl.when(segment == 0)
    def _():
        for copy in seeds:
            copy.start()

    for copy in (shifts, gains, *weights):
        copy.start()

    on_small = segment == small_step
    edge_lat, edge_lon = lat_signs[small_step][small_step], lon_signs[small_step][small_step]

    def small_exchange(ref, level):
        low, right = at(-edge_lat, 0), at(0, -edge_lon)
        plan = (
            (0, lines.at[level, pl.ds(0, QUAD)], (pl.ds(4 * QUAD, QUAD), pl.ds(0, width)), low),
            (1, lines.at[level, pl.ds(QUAD, QUAD)], (pl.ds(6 * QUAD, QUAD), pl.ds(0, width)), right),
            (3, corners.at[level], (pl.ds(8 * QUAD, QUAD), pl.ds(width, PAIR)), at(-edge_lat, -edge_lon)),
        )
        return [
            pltpu.make_async_remote_copy(
                src_ref=held,
                dst_ref=ref.at[level, *target],
                send_sem=send_sem.at[small_step, level, slot],
                recv_sem=recv_sem.at[small_step, level, slot],
                device_id=device,
                device_id_type=pl.DeviceIdType.MESH,
            )
            for slot, held, target, device in plan
        ]

    def edges(cells, level):
        store_edges(cells, edge_lat, edge_lon, lines, corners, level, pieces)

    @pl.when(on_small)
    def _():
        ref = (entering, leaving)[small_step]
        for level in range(levels):
            for start in (5 * QUAD, 7 * QUAD):
                ref[level, pl.ds(start, QUAD), :] = jnp.zeros((QUAD, width + PAIR), BF16)
            for start in (4 * QUAD, 6 * QUAD):
                ref[level, pl.ds(start, QUAD), pl.ds(width, PAIR)] = jnp.zeros((QUAD, PAIR), BF16)
            ref[level, pl.ds(8 * QUAD, QUAD), pl.ds(0, width)] = jnp.zeros((QUAD, width), BF16)

    def exchange(index, ref, level):
        a, b = pick(lat_signs[index]), pick(lon_signs[index])
        low, right = (1 - a) // 2, (1 - b) // 2
        plan = (
            (2 * QUAD * low, 2 * QUAD, 4 * QUAD, at(-a, 0)),
            (QUAD * right, QUAD, 6 * QUAD, at(0, -b)),
            (2 * QUAD + QUAD * right, QUAD, 7 * QUAD, at(0, -b)),
            (2 * QUAD * low + QUAD * right, QUAD, 8 * QUAD, at(-a, -b)),
        )
        return [
            pltpu.make_async_remote_copy(
                src_ref=ref.at[level, pl.ds(pl.multiple_of(start, QUAD), count)],
                dst_ref=ref.at[level, pl.ds(target, count)],
                send_sem=send_sem.at[index, level, slot],
                recv_sem=recv_sem.at[index, level, slot],
                device_id=device,
                device_id_type=pl.DeviceIdType.MESH,
            )
            for slot, (start, count, target, device) in enumerate(plan)
        ]

    def each_transfer(index, level, act):
        ref = (entering, leaving)[index]

        def whole():
            for copy in exchange(index, ref, level):
                act(copy)

        def edge():
            for copy in small_exchange(ref, level):
                act(copy)

        if index == small_step:
            pl.when(on_small)(edge)
            pl.when(jnp.logical_not(on_small))(whole)
        else:
            whole()

    low_next = (1 - lat_signs[0][1]) // 2

    def crossing(level, part):
        rows = pl.ds(2 * QUAD * (low_next if part == 0 else 1 - low_next), 2 * QUAD)
        return pltpu.make_async_remote_copy(
            src_ref=leaving.at[level, rows],
            dst_ref=entering.at[level, rows],
            send_sem=cross_send.at[level, part],
            recv_sem=cross_recv.at[level, part],
            device_id=across,
            device_id_type=pl.DeviceIdType.MESH,
        )

    def each_level(step):
        def run(level, carry):
            step(level)
            return carry

        lax.fori_loop(0, levels, run, 0)

    @pl.when(segment == 0)
    def _():
        for copy in seeds:
            copy.wait()
        seed(
            entering, latents_ref, mask_ref, embed_ref, pieces,
            edges if small_step == 0 else lambda cells, level: None,
        )

    pl.semaphore_wait(barrier, len(partners))

    def enter(level):
        each_transfer(0, level, lambda copy: copy.start())

    @pl.when(segment == 0)
    def _():
        each_level(enter)

    shifts.wait()
    lat_base = [based(offsets_ref[s, 0], WLAT) for s in (0, 1)]
    lon_base = [based(offsets_ref[s, 1], WLON) for s in (0, 1)]
    first = segment == 0
    lat_own, lon_own = jnp.where(first, lat_base[0], lat_base[1]), jnp.where(first, lon_base[0], lon_base[1])
    lat_in = jnp.where(first, lat_base[0], lat_base[1] - lat_base[0])
    lon_in = jnp.where(first, lon_base[0], lon_base[1] - lon_base[0])
    offset = jnp.where(first, offsets_ref[0, 0], offsets_ref[1, 0])

    row, column = quarter_cell(iota((CELLS, 1), 0))
    choosers(
        row + lat_in, column + lon_in, pick(lat_signs[0]), pick(lon_signs[0]),
        on_small if small_step == 0 else None, pieces, main_in, tail_in,
    )
    line = iota((CELLS * levels, 1), 0)
    row, column = split_by(line, WLON * levels, WLAT)
    column, held_level = split_by(column, levels, WLON)
    for level in range(levels):
        choosers(
            row - lat_own, column - lon_own, pick(lat_signs[1]), pick(lon_signs[1]),
            on_small if small_step == 1 else None, pieces, main_out.at[level], tail_out.at[level], held_level == level,
        )

    def wrapped(shape, axis):
        row, _ = quarter_cell(iota(shape, axis))
        held = lat * WLAT + lat_own + row
        held = jnp.where(held < 0, held + lats * WLAT, held)
        held = jnp.where(held >= lats * WLAT, held - lats * WLAT, held)
        return (held < offset).astype(jnp.int32)

    excluded = jnp.where(wrapped((CELLS, 1), 0) == wrapped((1, CELLS), 1), 0.0, -1e30)
    bias[pl.ds(0, CELLS), :] = excluded
    bias[pl.ds(CELLS, CELLS), :] = excluded
    gains.wait()
    for copy in weights:
        copy.wait()

    @pl.when(segment == 1)
    def _():
        def forward(level):
            copies = exchange(0, entering, level)
            crossing(level, 0).wait_recv()
            for slot in (0, 3, 1 + low_next):
                copies[slot].start()
            crossing(level, 1).wait_recv()
            copies[2 - low_next].start()

        each_level(forward)

    gain = jnp.where(first, gain_ref[0:1, :], gain_ref[1:2, :])

    def work(level):
        each_transfer(0, level, lambda copy: copy.wait_recv())
        x = gathered(entering[level], main_in, tail_in, width, pieces).astype(BF16)
        cells = section(x, bias[...], wqkv, wout, gain)
        store_quarters(cells, leaving, level, width, pieces)

        @pl.when(segment == 0)
        def _():
            for part in (0, 1):
                crossing(level, part).start()

        if small_step == 1:
            pl.when(on_small)(lambda: edges(cells, level))
        each_transfer(1, level, lambda copy: copy.start())

    each_level(work)

    total[...] = jnp.zeros_like(total)

    def finish(level):
        each_transfer(1, level, lambda copy: copy.wait_recv())
        total[...] += gathered(leaving[level], main_out.at[level], tail_out.at[level], width, pieces)

    each_level(finish)
    out_ref[...] = total[...].astype(BF16).reshape(out_ref.shape)

    def settle(level):
        for index in (0, 1):
            each_transfer(index, level, lambda copy: copy.wait_send())

        @pl.when(segment == 0)
        def _():
            for part in (0, 1):
                crossing(level, part).wait_send()

    each_level(settle)


def sections(variant, offsets, latents, land_mask, land_embed, qkv_weight, out_weight, norm_gain):
    _, _, levels, width = latents.shape
    second_known = variant >= 4
    signs = []
    for bit in (2, 1):
        other = -1 if variant & bit else 1
        if second_known:
            entering, leaving = (other, -other), (-other, 1)
        else:
            entering, leaving = (-1, other), (1, -other)
        signs.append((entering, leaving))
    pieces = width // PAIR
    in_vmem = pl.BlockSpec(memory_space=pltpu.VMEM)
    in_hbm = pl.BlockSpec(memory_space=pl.ANY)
    block = (levels, 9 * QUAD, width + PAIR)
    return pl.pallas_call(
        functools.partial(kernel, signs[0], signs[1], int(second_known)),
        out_shape=jax.ShapeDtypeStruct(latents.shape, BF16),
        in_specs=[in_hbm] * 7,
        out_specs=in_vmem,
        scratch_shapes=[
            pltpu.SMEM(offsets.shape, offsets.dtype),
            pltpu.VMEM(latents.shape, latents.dtype),
            pltpu.VMEM(land_mask.shape, land_mask.dtype),
            pltpu.VMEM(land_embed.shape, land_embed.dtype),
            pltpu.VMEM(norm_gain.shape, norm_gain.dtype),
            pltpu.VMEM(block, BF16),
            pltpu.VMEM(block, BF16),
            pltpu.VMEM((levels, 2 * QUAD, width), BF16),
            pltpu.VMEM((levels, QUAD, PAIR), BF16),
            pltpu.VMEM(qkv_weight.shape[1:], BF16),
            pltpu.VMEM(out_weight.shape[1:], BF16),
            pltpu.VMEM((CELLS, 9 * QUAD), BF16),
            pltpu.VMEM((CELLS * pieces, 9 * QUAD), BF16),
            pltpu.VMEM((levels, CELLS * levels, 9 * QUAD), BF16),
            pltpu.VMEM((levels, CELLS * levels * pieces, 9 * QUAD), BF16),
            pltpu.VMEM((2 * CELLS, CELLS), F32),
            pltpu.VMEM((CELLS * levels, width), F32),
            pltpu.SemaphoreType.DMA((7,)),
            pltpu.SemaphoreType.DMA((2, levels, 4)),
            pltpu.SemaphoreType.DMA((2, levels, 4)),
            pltpu.SemaphoreType.DMA((levels, 2)),
            pltpu.SemaphoreType.DMA((levels, 2)),
        ],
        compiler_params=pltpu.CompilerParams(
            collective_id=variant, has_side_effects=True, vmem_limit_bytes=48 * 1024 * 1024
        ),
    )(offsets, latents, land_mask, land_embed, qkv_weight, out_weight, norm_gain)


def body(latents, land_mask, land_embed, qkv_weight, out_weight, norm_gain, offsets):
    assert latents.shape[1:3] == (WLAT, WLON)
    lat_part, lon_part = offsets[:, 0:1], offsets[:, 1:2]
    signs = 2 * (lat_part >= HALF_LAT).astype(jnp.int32) + (lon_part >= HALF_LON).astype(jnp.int32)
    known = (lat_part == WLAT - 1) & (lon_part == WLON - 1)
    term = jnp.where(iota((2, 1), 0) == 0, jnp.where(known, 0, 1 + signs), signs)
    variant = jnp.sum(term)
    ways = [functools.partial(sections, v) for v in range(8)]
    out = lax.switch(
        variant, ways,
        offsets, latents.transpose(1, 2, 0, 3), land_mask, land_embed, qkv_weight, out_weight, norm_gain,
    )
    return out.transpose(2, 0, 1, 3)[None]


def solution(mesh):
    return jax.shard_map(
        body,
        mesh=mesh,
        in_specs=(
            P(None, "lat", "lon", None),
            P("lat", "lon"),
            P(),
            P("segment", None, None),
            P("segment", None, None),
            P(),
            P(),
        ),
        out_specs=P("segment", None, "lat", "lon", None),
        check_vma=False,
    )
```

```python
import functools
import math

import jax
import jax.numpy as jnp
from jax import lax
from jax.experimental import pallas as pl
from jax.experimental.pallas import tpu as pltpu
from jax.sharding import PartitionSpec as P

HEADS = 16
WLAT = 6
WLON = 12
HALF_LAT = WLAT // 2
HALF_LON = WLON // 2
CELLS = WLAT * WLON
QUAD = 16
PAIR = 128
NT = (((1,), (1,)), ((), ()))
F32 = jnp.float32
BF16 = jnp.bfloat16


def dot(a, b):
    return jnp.dot(a, b, preferred_element_type=F32)


def iota(shape, axis):
    return lax.broadcasted_iota(jnp.int32, shape, axis)


def based(offset, window):
    return jnp.where(offset >= window // 2, offset - window, offset)


def split_by(value, size, count):
    high = sum((value >= size * k).astype(jnp.int32) for k in range(1, count))
    return high, value - size * high


def quarter_cell(t):
    late = t >= 4 * QUAD
    quarter = jnp.where(late, (t - 4 * QUAD) >> 1, t >> 4)
    j = jnp.where(late, QUAD + (t & 1), t & (QUAD - 1))
    row, column = split_by(j, HALF_LON, 3)
    return HALF_LAT * (quarter >> 1) + row, HALF_LON * (quarter & 1) + column


def source(row, column, lat_sign, lon_sign, small, beyond):
    row_out = (row < 0) | (row >= WLAT)
    column_out = (column < 0) | (column >= WLON)
    row = jnp.where(row_out, row - WLAT * lat_sign, row)
    column = jnp.where(column_out, column - WLON * lon_sign, column)
    low, near_row = split_by(row, HALF_LAT, 2)
    right, near_column = split_by(column, HALF_LON, 2)
    base = jnp.where(
        row_out,
        jnp.where(column_out, 8 * QUAD, 4 * QUAD + QUAD * right),
        jnp.where(column_out, 6 * QUAD + QUAD * low, 2 * QUAD * low + QUAD * right),
    )
    j = HALF_LON * near_row + near_column
    if small is not None:
        small_base = jnp.where(row_out, jnp.where(column_out, 8 * QUAD, 4 * QUAD), 6 * QUAD)
        small_j = jnp.where(row_out, jnp.where(column_out, QUAD, column), row)
        whole = ~(row_out | column_out) | jnp.logical_not(small)
        base, j = jnp.where(whole, base, small_base), jnp.where(whole, j, small_j)
    lines, line = beyond
    far = QUAD * line + jnp.where(column_out, QUAD * lines, 0) + column
    return base, j, far


def choosers(row, column, signs, small, beyond, wanted, pieces, main_ref, tail_ref, far_ref):
    lines, line, past, live = beyond
    base, j, far = source(row, column, *signs, small, (lines, line))
    near = live & wanted & jnp.logical_not(past)
    held = live & wanted & past & (line >= 0) & (line < lines)
    base = jnp.where(near, base, -5000)
    count = row.shape[0]
    lane = iota((count, 9 * QUAD), 1)
    main_ref[...] = (lane == jnp.where(j < QUAD, base + j, -1000)).astype(F32).astype(BF16)
    tail = jnp.where(j >= QUAD, base + j - QUAD, -1000)
    for piece in range(pieces):
        tail_ref[pl.ds(piece * count, count), :] = (lane == tail + 2 * piece).astype(F32).astype(BF16)
    lane = iota(far_ref.shape, 1)
    far_ref[...] = (lane == jnp.where(held, far, -1000)).astype(F32).astype(BF16)


def gathered(block, far, main_ref, tail_ref, far_ref, width, pieces):
    count = main_ref.shape[0]
    tail = dot(tail_ref[...], block[:, width:])
    tail = jnp.concatenate([tail[p * count : (p + 1) * count] for p in range(pieces)], axis=1)
    return dot(main_ref[...], block[:, :width]) + dot(far_ref[...], far) + tail


def store_quarters(cells, ref, level, width, pieces):
    cells = cells[:CELLS].astype(F32)
    piece = width // pieces
    ref[level, pl.ds(0, 4 * QUAD), pl.ds(0, width)] = cells[: 4 * QUAD].astype(BF16)
    stack = jnp.concatenate([cells[4 * QUAD :, p * piece : (p + 1) * piece] for p in range(pieces)], axis=0)
    to, at = iota((4 * QUAD, 8 * pieces), 0), iota((4 * QUAD, 8 * pieces), 1)
    wanted = 8 * ((to & (QUAD - 1)) >> 1) + 2 * (to >> 4) + (to & 1)
    pick = (at == wanted).astype(F32).astype(BF16)
    ref[level, pl.ds(0, 4 * QUAD), pl.ds(width, piece)] = dot(pick, stack.astype(BF16)).astype(BF16)


def store_edges(cells, lat_sign, lon_sign, line_ref, corner_ref, level, pieces):
    row_at, column_at = (0 if lat_sign > 0 else WLAT - 1), (0 if lon_sign > 0 else WLON - 1)
    to = iota((2 * QUAD, CELLS), 0)
    row, column = quarter_cell(iota((2 * QUAD, CELLS), 1))
    pick = ((row == row_at) & (column == to)) | ((column == column_at) & (row == to - QUAD))
    line_ref[level] = dot(pick.astype(F32).astype(BF16), cells[:CELLS].astype(BF16)).astype(BF16)
    half = HALF_LON * (row_at % HALF_LAT) + column_at % HALF_LON
    quarter = 2 * (row_at // HALF_LAT) + column_at // HALF_LON
    place = QUAD * quarter + half if half < QUAD else 4 * QUAD + 2 * quarter + half - QUAD
    piece = cells.shape[1] // pieces
    line = iota((QUAD, piece), 0)
    corner = jnp.zeros((QUAD, piece), F32)
    for p in range(pieces):
        corner = jnp.where(line == 2 * p, cells[place : place + 1, p * piece : (p + 1) * piece], corner)
    corner_ref[level] = corner.astype(BF16)


def seed(entering, latents_ref, mask_ref, embed_ref, pieces, edges):
    levels, width = latents_ref.shape[2:]
    embed = embed_ref[...].astype(F32).reshape(1, width)
    across = WLON * levels
    spread = iota((across, WLON), 0)
    spread = (spread >= levels * iota((across, WLON), 1)) & (spread < levels * iota((across, WLON), 1) + levels)
    rows = []
    for row in range(WLAT):
        land = jnp.where(spread, mask_ref[row : row + 1, :].astype(F32), 0.0)
        land = jnp.sum(land, axis=1, keepdims=True)
        rows.append(latents_ref[row].astype(F32).reshape(across, width) + land * embed)
    cells = jnp.concatenate(rows, axis=0).astype(BF16)
    row, column = quarter_cell(iota((CELLS, CELLS * levels), 0))
    wanted = levels * (WLON * row + column)
    at = iota((CELLS, CELLS * levels), 1)
    for level in range(levels):
        order = (at == wanted + level).astype(F32).astype(BF16)
        ordered = dot(order, cells)
        store_quarters(ordered, entering, level, width, pieces)
        edges(ordered, level)


def attended(q, k, v, bias, head_size):
    cells = q.shape[0]
    first = iota((cells, PAIR), 1) < head_size
    ones = jnp.ones((cells, PAIR), BF16)
    pairs = [slice(p * PAIR, (p + 1) * PAIR) for p in range(q.shape[1] // PAIR)]
    scores = []
    for pair in pairs:
        zero = jnp.zeros((cells, PAIR), F32)
        both = jnp.concatenate([jnp.where(first, q[:, pair], zero), jnp.where(first, zero, q[:, pair])], axis=0)
        scores.append(lax.dot_general(both.astype(BF16), k[:, pair].astype(BF16), NT, preferred_element_type=F32))
    weights = []
    for score in scores:
        score = score + bias
        weights.append(jnp.exp(score - jnp.max(score, axis=-1, keepdims=True)).astype(BF16))
    sums = [
        dot(weight, jnp.concatenate([v[:, pair].astype(BF16), ones], axis=1))
        for weight, pair in zip(weights, pairs)
    ]
    parts = []
    for both in sums:
        value = jnp.where(first, both[:cells, :PAIR], both[cells:, :PAIR])
        total = jnp.where(first, both[:cells, PAIR:], both[cells:, PAIR:])
        parts.append((value / total).astype(BF16))
    return jnp.concatenate(parts, axis=1)


def section(x, bias, wqkv, wout, gain):
    width = x.shape[1]
    head_size = width // HEADS
    q = dot(x, wqkv[:, :width]) * (1.0 / math.sqrt(head_size))
    k = dot(x, wqkv[:, width : 2 * width])
    v = dot(x, wqkv[:, 2 * width :])
    projected = dot(attended(q, k, v, bias, head_size), wout[...])
    centered = projected - jnp.mean(projected, axis=-1, keepdims=True)
    variance = jnp.mean(centered * centered, axis=-1, keepdims=True)
    branch = centered * lax.rsqrt(variance + 1e-05) * gain
    return x.astype(F32) + branch


def kernel(
    lat_signs, lon_signs, small_step, line_counts,
    offsets_hbm, latents_hbm, mask_hbm, embed_hbm, wqkv_hbm, wout_hbm, gain_hbm, out_ref,
    offsets_ref, latents_ref, mask_ref, embed_ref, gain_ref,
    entering, leaving, far_entering, far_leaving, lines, corners, wqkv, wout,
    main_in, tail_in, far_in, main_out, tail_out, far_out, bias, total,
    load_sem, send_sem, recv_sem, cross_send, cross_recv,
):
    segment, lon, lat = (lax.axis_index(axis) for axis in ("segment", "lon", "lat"))
    lons, lats = lax.axis_size("lon"), lax.axis_size("lat")
    levels, width = latents_ref.shape[2:]
    pieces = width // PAIR
    at = lambda a, b: (segment, lax.rem(lon + b + lons, lons), lax.rem(lat + a + lats, lats))
    pick = lambda pair: pair[0] + segment * (pair[1] - pair[0])

    across = (1 - segment, lon, lat)
    own_signs = tuple(-sign for sign in lat_signs[1])
    edge_of = lambda sign: lats - 1 if sign < 0 else 0
    edges_at = tuple(edge_of(sign) for sign in own_signs)
    on_edge = lat == pick(edges_at)
    on_first_edge = lat == edges_at[0]
    extra = max(line_counts)
    barrier = pltpu.get_barrier_semaphore()

    def greet(partner):
        pl.semaphore_signal(barrier, inc=1, device_id=partner, device_id_type=pl.DeviceIdType.MESH)

    for partner in (at(0, -1), at(0, 1), across):
        greet(partner)
    for a in (-1, 1):
        @pl.when((lat + a >= 0) & (lat + a < lats))
        def _():
            for b in (-1, 0, 1):
                greet(at(a, b))

    greetings = 3 + 3 * ((lat > 0).astype(jnp.int32) + (lat < lats - 1).astype(jnp.int32))

    def load(slot, source_ref, target_ref):
        return pltpu.make_async_copy(source_ref, target_ref, load_sem.at[slot])

    seeds = [load(0, latents_hbm, latents_ref), load(1, mask_hbm, mask_ref), load(2, embed_hbm, embed_ref)]
    shifts, gains = load(3, offsets_hbm, offsets_ref), load(4, gain_hbm, gain_ref)
    weights = [load(5, wqkv_hbm.at[0], wqkv), load(6, wout_hbm.at[0], wout)]

    @pl.when(segment == 0)
    def _():
        for copy in seeds:
            copy.start()

    for copy in (shifts, gains, *weights):
        copy.start()

    on_small = segment == small_step
    edge_lat, edge_lon = lat_signs[small_step][small_step], lon_signs[small_step][small_step]

    def small_exchange(ref, level):
        low, right = at(-edge_lat, 0), at(0, -edge_lon)
        plan = (
            (0, lines.at[level, pl.ds(0, QUAD)], (pl.ds(4 * QUAD, QUAD), pl.ds(0, width)), low),
            (1, lines.at[level, pl.ds(QUAD, QUAD)], (pl.ds(6 * QUAD, QUAD), pl.ds(0, width)), right),
            (3, corners.at[level], (pl.ds(8 * QUAD, QUAD), pl.ds(width, PAIR)), at(-edge_lat, -edge_lon)),
        )
        return [
            pltpu.make_async_remote_copy(
                src_ref=held,
                dst_ref=ref.at[level, *target],
                send_sem=send_sem.at[small_step, level, slot],
                recv_sem=recv_sem.at[small_step, level, slot],
                device_id=device,
                device_id_type=pl.DeviceIdType.MESH,
            )
            for slot, held, target, device in plan
        ]

    def edges(cells, level):
        store_edges(cells, edge_lat, edge_lon, lines, corners, level, pieces)

    @pl.when(on_small)
    def _():
        ref = (entering, leaving)[small_step]
        for level in range(levels):
            for start in (5 * QUAD, 7 * QUAD):
                ref[level, pl.ds(start, QUAD), :] = jnp.zeros((QUAD, width + PAIR), BF16)
            for start in (4 * QUAD, 6 * QUAD):
                ref[level, pl.ds(start, QUAD), pl.ds(width, PAIR)] = jnp.zeros((QUAD, PAIR), BF16)
            ref[level, pl.ds(8 * QUAD, QUAD), pl.ds(0, width)] = jnp.zeros((QUAD, width), BF16)

    for index, ref in enumerate((entering, leaving)):
        behind = lat + pick(lat_signs[index])

        @pl.when((behind < 0) | (behind >= lats))
        def _():
            for level in range(levels):
                for start, count in ((4 * QUAD, 2 * QUAD), (8 * QUAD, QUAD)):
                    ref[level, pl.ds(start, count), :] = jnp.zeros((count, width + PAIR), BF16)

    crossed = QUAD * line_counts[0]
    far_here = (segment == 1) & on_first_edge
    for level in range(levels):
        for start in (0, QUAD * extra):
            @pl.when(jnp.logical_not(far_here))
            def _():
                far_entering[level, pl.ds(start, crossed), :] = jnp.zeros((crossed, width), BF16)

            if crossed < QUAD * extra:
                left = QUAD * extra - crossed
                far_entering[level, pl.ds(start + crossed, left), :] = jnp.zeros((left, width), BF16)

        @pl.when(jnp.logical_not(on_edge))
        def _():
            far_leaving[level, pl.ds(QUAD * extra, QUAD * extra), :] = jnp.zeros((QUAD * extra, width), BF16)

    def far_exchange(index, level):
        ref, count = ((far_entering, crossed), (far_leaving, QUAD * extra))[index]
        return pltpu.make_async_remote_copy(
            src_ref=ref.at[level, pl.ds(0, count)],
            dst_ref=ref.at[level, pl.ds(QUAD * extra, count)],
            send_sem=send_sem.at[index, level, 4],
            recv_sem=recv_sem.at[index, level, 4],
            device_id=at(0, -pick(lon_signs[index])),
            device_id_type=pl.DeviceIdType.MESH,
        )

    def exchange(index, ref, level):
        a, b = pick(lat_signs[index]), pick(lon_signs[index])
        low, right = (1 - a) // 2, (1 - b) // 2
        plan = (
            (2 * QUAD * low, 2 * QUAD, 4 * QUAD, at(-a, 0)),
            (QUAD * right, QUAD, 6 * QUAD, at(0, -b)),
            (2 * QUAD + QUAD * right, QUAD, 7 * QUAD, at(0, -b)),
            (2 * QUAD * low + QUAD * right, QUAD, 8 * QUAD, at(-a, -b)),
        )
        return [
            pltpu.make_async_remote_copy(
                src_ref=ref.at[level, pl.ds(pl.multiple_of(start, QUAD), count)],
                dst_ref=ref.at[level, pl.ds(target, count)],
                send_sem=send_sem.at[index, level, slot],
                recv_sem=recv_sem.at[index, level, slot],
                device_id=device,
                device_id_type=pl.DeviceIdType.MESH,
            )
            for slot, (start, count, target, device) in enumerate(plan)
        ]

    def guarded(copies, other, act, far_slots):
        inside = (other >= 0) & (other < lats)
        for slot, copy in enumerate(copies):
            if slot in far_slots:
                pl.when(inside)(functools.partial(act, copy))
            else:
                act(copy)

    def each_transfer(index, level, act, way):
        ref = (entering, leaving)[index]

        def whole():
            guarded(exchange(index, ref, level), lat + way * pick(lat_signs[index]), act, (0, 3))

        def edge():
            guarded(small_exchange(ref, level), lat + way * edge_lat, act, (0, 2))

        if index == small_step:
            pl.when(on_small)(edge)
            pl.when(jnp.logical_not(on_small))(whole)
        else:
            whole()
        pl.when(far_here if index == 0 else on_edge)(lambda: act(far_exchange(index, level)))

    low_next = (1 - lat_signs[0][1]) // 2

    def crossing(level, part):
        if part == 2:
            rows, held, target = pl.ds(0, crossed), far_leaving, far_entering
        else:
            rows = pl.ds(2 * QUAD * (low_next if part == 0 else 1 - low_next), 2 * QUAD)
            held, target = leaving, entering
        return pltpu.make_async_remote_copy(
            src_ref=held.at[level, rows],
            dst_ref=target.at[level, rows],
            send_sem=cross_send.at[level, part],
            recv_sem=cross_recv.at[level, part],
            device_id=across,
            device_id_type=pl.DeviceIdType.MESH,
        )

    def each_crossing(level, act):
        act(crossing(level, 0))
        pl.when(on_first_edge)(lambda: act(crossing(level, 2)))
        act(crossing(level, 1))

    def each_level(step):
        def run(level, carry):
            step(level)
            return carry

        lax.fori_loop(0, levels, run, 0)

    @pl.when(segment == 0)
    def _():
        for copy in seeds:
            copy.wait()
        seed(
            entering, latents_ref, mask_ref, embed_ref, pieces,
            edges if small_step == 0 else lambda cells, level: None,
        )

    pl.semaphore_wait(barrier, greetings)

    def enter(level):
        each_transfer(0, level, lambda copy: copy.start(), -1)

    @pl.when(segment == 0)
    def _():
        each_level(enter)

    shifts.wait()
    lat_base = [based(offsets_ref[s, 0], WLAT) for s in (0, 1)]
    lon_base = [based(offsets_ref[s, 1], WLON) for s in (0, 1)]
    first = segment == 0
    lat_own, lon_own = jnp.where(first, lat_base[0], lat_base[1]), jnp.where(first, lon_base[0], lon_base[1])
    lat_from, lon_from = jnp.where(first, 0, lat_base[0]), jnp.where(first, 0, lon_base[0])
    own_sign = pick(own_signs)
    count = CELLS + QUAD * extra

    def targets(shape, axis):
        t = iota(shape, axis)
        row, column = quarter_cell(t)
        outside = t >= CELLS
        line, place = (t - CELLS) >> 3 >> 1, (t - CELLS) & (QUAD - 1)
        edge_row = jnp.where(own_sign < 0, WLAT - 1 - line, line)
        row = jnp.where(outside, edge_row, row + lat_own)
        column = jnp.where(outside, place, column) + lon_own
        ground = row + lat * WLAT
        kept = on_edge & (place < WLON) & (line < jnp.abs(lat_own))
        live = (outside & kept) | (jnp.logical_not(outside) & (ground >= 0) & (ground < lats * WLAT))
        group = jnp.where(live, outside.astype(jnp.int32), 2)
        return row, column, live, group

    def past_edge(row, held_sign, held_base):
        line = row + held_base
        line = jnp.where(held_sign < 0, WLAT - 1 - line, line)
        past = ((row < 0) & (lat == 0)) | ((row >= WLAT) & (lat == lats - 1))
        return line, past

    row, column, live, group = targets((count, 1), 0)
    row, column = row - lat_from, column - lon_from
    line, past = past_edge(row, own_signs[0], lat_base[0])
    choosers(
        row, column, (pick(lat_signs[0]), pick(lon_signs[0])), on_small if small_step == 0 else None,
        (extra, line, past, live), live, pieces, main_in, tail_in, far_in,
    )
    _, _, _, group_across = targets((1, count), 1)
    excluded = jnp.where(group == group_across, 0.0, -1e30)
    bias[pl.ds(0, count), :] = excluded
    bias[pl.ds(count, count), :] = excluded

    place = iota((CELLS * levels, 1), 0)
    row, column = split_by(place, WLON * levels, WLAT)
    column, held_level = split_by(column, levels, WLON)
    row, column = row - lat_own, column - lon_own
    line, past = past_edge(row, own_sign, lat_own)
    for level in range(levels):
        wanted = held_level == level
        choosers(
            row, column, (pick(lat_signs[1]), pick(lon_signs[1])), on_small if small_step == 1 else None,
            (extra, line, past, wanted), wanted, pieces,
            main_out.at[level], tail_out.at[level], far_out.at[level],
        )

    gains.wait()
    for copy in weights:
        copy.wait()

    @pl.when(segment == 1)
    def _():
        def forward(level):
            copies = exchange(0, entering, level)
            start = lambda copy: copy.start()
            crossing(level, 0).wait_recv()
            guarded([copies[0], copies[3]], lat - lat_signs[0][1], start, (0, 1))
            copies[1 + low_next].start()

            @pl.when(on_first_edge)
            def _():
                crossing(level, 2).wait_recv()
                far_exchange(0, level).start()

            crossing(level, 1).wait_recv()
            copies[2 - low_next].start()

        each_level(forward)

    gain = jnp.where(first, gain_ref[0:1, :], gain_ref[1:2, :])

    def work(level):
        each_transfer(0, level, lambda copy: copy.wait_recv(), 1)
        x = gathered(entering[level], far_entering[level], main_in, tail_in, far_in, width, pieces).astype(BF16)
        cells = section(x, bias[...], wqkv, wout, gain)
        store_quarters(cells, leaving, level, width, pieces)
        far_leaving[level, pl.ds(0, QUAD * extra), :] = cells[CELLS:].astype(BF16)

        @pl.when(segment == 0)
        def _():
            each_crossing(level, lambda copy: copy.start())

        if small_step == 1:
            pl.when(on_small)(lambda: edges(cells, level))
        each_transfer(1, level, lambda copy: copy.start(), -1)

    each_level(work)

    total[...] = jnp.zeros_like(total)

    def finish(level):
        each_transfer(1, level, lambda copy: copy.wait_recv(), 1)
        total[...] += gathered(
            leaving[level], far_leaving[level],
            main_out.at[level], tail_out.at[level], far_out.at[level], width, pieces,
        )

    each_level(finish)
    out_ref[...] = total[...].astype(BF16).reshape(out_ref.shape)

    def settle(level):
        for index in (0, 1):
            each_transfer(index, level, lambda copy: copy.wait_send(), -1)

        @pl.when(segment == 0)
        def _():
            each_crossing(level, lambda copy: copy.wait_send())

    each_level(settle)


def sections(variant, offsets, latents, land_mask, land_embed, qkv_weight, out_weight, norm_gain):
    _, _, levels, width = latents.shape
    second_known = variant >= 4
    signs = []
    for bit in (2, 1):
        other = -1 if variant & bit else 1
        if second_known:
            entering, leaving = (other, -other), (-other, 1)
        else:
            entering, leaving = (-1, other), (1, -other)
        signs.append((entering, leaving))
    if second_known:
        line_counts = (HALF_LAT if signs[0][0][0] < 0 else HALF_LAT - 1, 1)
    else:
        line_counts = (1, HALF_LAT if signs[0][1][1] > 0 else HALF_LAT - 1)
    extra = max(line_counts)
    count = CELLS + QUAD * extra
    far_block = (levels, 2 * QUAD * extra, width)
    pieces = width // PAIR
    in_vmem = pl.BlockSpec(memory_space=pltpu.VMEM)
    in_hbm = pl.BlockSpec(memory_space=pl.ANY)
    block = (levels, 9 * QUAD, width + PAIR)
    return pl.pallas_call(
        functools.partial(kernel, signs[0], signs[1], int(second_known), line_counts),
        out_shape=jax.ShapeDtypeStruct(latents.shape, BF16),
        in_specs=[in_hbm] * 7,
        out_specs=in_vmem,
        scratch_shapes=[
            pltpu.SMEM(offsets.shape, offsets.dtype),
            pltpu.VMEM(latents.shape, latents.dtype),
            pltpu.VMEM(land_mask.shape, land_mask.dtype),
            pltpu.VMEM(land_embed.shape, land_embed.dtype),
            pltpu.VMEM(norm_gain.shape, norm_gain.dtype),
            pltpu.VMEM(block, BF16),
            pltpu.VMEM(block, BF16),
            pltpu.VMEM(far_block, BF16),
            pltpu.VMEM(far_block, BF16),
            pltpu.VMEM((levels, 2 * QUAD, width), BF16),
            pltpu.VMEM((levels, QUAD, PAIR), BF16),
            pltpu.VMEM(qkv_weight.shape[1:], BF16),
            pltpu.VMEM(out_weight.shape[1:], BF16),
            pltpu.VMEM((count, 9 * QUAD), BF16),
            pltpu.VMEM((count * pieces, 9 * QUAD), BF16),
            pltpu.VMEM((count, 2 * QUAD * extra), BF16),
            pltpu.VMEM((levels, CELLS * levels, 9 * QUAD), BF16),
            pltpu.VMEM((levels, CELLS * levels * pieces, 9 * QUAD), BF16),
            pltpu.VMEM((levels, CELLS * levels, 2 * QUAD * extra), BF16),
            pltpu.VMEM((2 * count, count), F32),
            pltpu.VMEM((CELLS * levels, width), F32),
            pltpu.SemaphoreType.DMA((7,)),
            pltpu.SemaphoreType.DMA((2, levels, 5)),
            pltpu.SemaphoreType.DMA((2, levels, 5)),
            pltpu.SemaphoreType.DMA((levels, 3)),
            pltpu.SemaphoreType.DMA((levels, 3)),
        ],
        compiler_params=pltpu.CompilerParams(
            collective_id=variant, has_side_effects=True, vmem_limit_bytes=48 * 1024 * 1024
        ),
    )(offsets, latents, land_mask, land_embed, qkv_weight, out_weight, norm_gain)


def body(latents, land_mask, land_embed, qkv_weight, out_weight, norm_gain, offsets):
    assert latents.shape[1:3] == (WLAT, WLON)
    lat_part, lon_part = offsets[:, 0:1], offsets[:, 1:2]
    signs = 2 * (lat_part >= HALF_LAT).astype(jnp.int32) + (lon_part >= HALF_LON).astype(jnp.int32)
    known = (lat_part == WLAT - 1) & (lon_part == WLON - 1)
    term = jnp.where(iota((2, 1), 0) == 0, jnp.where(known, 0, 1 + signs), signs)
    variant = jnp.sum(term)
    ways = [functools.partial(sections, v) for v in range(8)]
    out = lax.switch(
        variant, ways,
        offsets, latents.transpose(1, 2, 0, 3), land_mask, land_embed, qkv_weight, out_weight, norm_gain,
    )
    return out.transpose(2, 0, 1, 3)[None]


def solution(mesh):
    return jax.shard_map(
        body,
        mesh=mesh,
        in_specs=(
            P(None, "lat", "lon", None),
            P("lat", "lon"),
            P(),
            P("segment", None, None),
            P("segment", None, None),
            P(),
            P(),
        ),
        out_specs=P("segment", None, "lat", "lon", None),
        check_vma=False,
    )
```

```python
import functools
import math

import jax
import jax.numpy as jnp
from jax import lax
from jax.experimental import pallas as pl
from jax.experimental.pallas import tpu as pltpu
from jax.sharding import PartitionSpec as P

HEADS = 16
WLAT = 6
WLON = 12
HALF_LAT = WLAT // 2
HALF_LON = WLON // 2
CELLS = WLAT * WLON
HELD = 80
QUAD = 16
PAIR = 128
NT = (((1,), (1,)), ((), ()))
F32 = jnp.float32
BF16 = jnp.bfloat16


def dot(a, b):
    return jnp.dot(a, b, preferred_element_type=F32)


def iota(shape, axis):
    return lax.broadcasted_iota(jnp.int32, shape, axis)


def based(offset, window):
    return jnp.where(offset >= window // 2, offset - window, offset)


def split_by(value, size, count):
    high = sum((value >= size * k).astype(jnp.int32) for k in range(1, count))
    return high, value - size * high


def quarter_cell(t):
    late = t >= 4 * QUAD
    quarter = jnp.where(late, (t - 4 * QUAD) >> 1, t >> 4)
    j = jnp.where(late, QUAD + (t & 1), t & (QUAD - 1))
    row, column = split_by(j, HALF_LON, 3)
    return HALF_LAT * (quarter >> 1) + row, HALF_LON * (quarter & 1) + column


def source(row, column, lat_sign, lon_sign, small):
    row_out = (row < 0) | (row >= WLAT)
    column_out = (column < 0) | (column >= WLON)
    row = jnp.where(row_out, row - WLAT * lat_sign, row)
    column = jnp.where(column_out, column - WLON * lon_sign, column)
    low, near_row = split_by(row, HALF_LAT, 2)
    right, near_column = split_by(column, HALF_LON, 2)
    base = jnp.where(
        row_out,
        jnp.where(column_out, 8 * QUAD, 4 * QUAD + QUAD * right),
        jnp.where(column_out, 6 * QUAD + QUAD * low, 2 * QUAD * low + QUAD * right),
    )
    j = HALF_LON * near_row + near_column
    if small is not None:
        small_base = jnp.where(row_out, jnp.where(column_out, 8 * QUAD, 4 * QUAD), 6 * QUAD)
        small_j = jnp.where(row_out, jnp.where(column_out, QUAD, column), row)
        whole = ~(row_out | column_out) | jnp.logical_not(small)
        base, j = jnp.where(whole, base, small_base), jnp.where(whole, j, small_j)
    return base, j, column_out, column


def choosers(row, column, signs, small, beyond, wanted, pieces, main_ref, tail_ref, far_ref):
    base, j, column_out, column = source(row, column, *signs, small)
    near = wanted
    if beyond is not None:
        lines, line, past = beyond
        near = wanted & jnp.logical_not(past)
        held = wanted & past & (line >= 0) & (line < lines)
        far = QUAD * line + jnp.where(column_out, QUAD * lines, 0) + column
        lane = iota(far_ref.shape, 1)
        far_ref[...] = (lane == jnp.where(held, far, -1000)).astype(F32).astype(BF16)
    base = jnp.where(near, base, -5000)
    count = row.shape[0]
    lane = iota((count, 9 * QUAD), 1)
    main_ref[...] = (lane == jnp.where(j < QUAD, base + j, -1000)).astype(F32).astype(BF16)
    tail = jnp.where(j >= QUAD, base + j - QUAD, -1000)

    def fill(piece, carry):
        start = pl.multiple_of(piece * count, QUAD)
        tail_ref[pl.ds(start, count), :] = (lane == tail + 2 * piece).astype(F32).astype(BF16)
        return carry

    lax.fori_loop(0, pieces, fill, 0)


def gathered(block, far, main_ref, tail_ref, far_ref, width, pieces):
    count = main_ref.shape[0]
    tail = dot(tail_ref[...], block[:, width:])
    tail = jnp.concatenate([tail[p * count : (p + 1) * count] for p in range(pieces)], axis=1)
    tail = dot(main_ref[...], block[:, :width]) + tail
    return tail if far is None else tail + dot(far_ref[...], far)


def store_quarters(cells, ref, level, width, pieces):
    cells = cells[:CELLS].astype(F32)
    piece = width // pieces
    ref[level, pl.ds(0, 4 * QUAD), pl.ds(0, width)] = cells[: 4 * QUAD].astype(BF16)
    stack = jnp.concatenate([cells[4 * QUAD :, p * piece : (p + 1) * piece] for p in range(pieces)], axis=0)
    to, at = iota((4 * QUAD, 8 * pieces), 0), iota((4 * QUAD, 8 * pieces), 1)
    wanted = 8 * ((to & (QUAD - 1)) >> 1) + 2 * (to >> 4) + (to & 1)
    pick = (at == wanted).astype(F32).astype(BF16)
    ref[level, pl.ds(0, 4 * QUAD), pl.ds(width, piece)] = dot(pick, stack.astype(BF16)).astype(BF16)


def store_edges(cells, lat_sign, lon_sign, line_ref, corner_ref, level, pieces):
    row_at, column_at = (0 if lat_sign > 0 else WLAT - 1), (0 if lon_sign > 0 else WLON - 1)
    to = iota((2 * QUAD, CELLS), 0)
    row, column = quarter_cell(iota((2 * QUAD, CELLS), 1))
    pick = ((row == row_at) & (column == to)) | ((column == column_at) & (row == to - QUAD))
    line_ref[level] = dot(pick.astype(F32).astype(BF16), cells[:CELLS].astype(BF16)).astype(BF16)
    half = HALF_LON * (row_at % HALF_LAT) + column_at % HALF_LON
    quarter = 2 * (row_at // HALF_LAT) + column_at // HALF_LON
    place = QUAD * quarter + half if half < QUAD else 4 * QUAD + 2 * quarter + half - QUAD
    piece = cells.shape[1] // pieces
    line = iota((QUAD, piece), 0)
    corner = jnp.zeros((QUAD, piece), F32)
    for p in range(pieces):
        corner = jnp.where(line == 2 * p, cells[place : place + 1, p * piece : (p + 1) * piece], corner)
    corner_ref[level] = corner.astype(BF16)


def seed(entering, latents_ref, mask_ref, embed_ref, pieces, edges):
    levels, width = latents_ref.shape[2:]
    embed = embed_ref[...].astype(F32).reshape(1, width)
    across = WLON * levels
    spread = iota((across, WLON), 0)
    spread = (spread >= levels * iota((across, WLON), 1)) & (spread < levels * iota((across, WLON), 1) + levels)
    rows = []
    for row in range(WLAT):
        land = jnp.where(spread, mask_ref[row : row + 1, :].astype(F32), 0.0)
        land = jnp.sum(land, axis=1, keepdims=True)
        rows.append(latents_ref[row].astype(F32).reshape(across, width) + land * embed)
    cells = jnp.concatenate(rows, axis=0).astype(BF16)
    row, column = quarter_cell(iota((CELLS, CELLS * levels), 0))
    wanted = levels * (WLON * row + column)
    at = iota((CELLS, CELLS * levels), 1)
    for level in range(levels):
        order = (at == wanted + level).astype(F32).astype(BF16)
        ordered = dot(order, cells)
        store_quarters(ordered, entering, level, width, pieces)
        edges(ordered, level)


def attended(q, k, v, bias, head_size):
    cells = q.shape[0]
    first = iota((cells, PAIR), 1) < head_size
    ones = jnp.ones((cells, PAIR), BF16)
    pairs = [slice(p * PAIR, (p + 1) * PAIR) for p in range(q.shape[1] // PAIR)]
    scores = []
    for pair in pairs:
        zero = jnp.zeros((cells, PAIR), F32)
        both = jnp.concatenate([jnp.where(first, q[:, pair], zero), jnp.where(first, zero, q[:, pair])], axis=0)
        scores.append(lax.dot_general(both.astype(BF16), k[:, pair].astype(BF16), NT, preferred_element_type=F32))
    weights = []
    for score in scores:
        score = score + bias
        weights.append(jnp.exp(score - jnp.max(score, axis=-1, keepdims=True)).astype(BF16))
    sums = [
        dot(weight, jnp.concatenate([v[:, pair].astype(BF16), ones], axis=1))
        for weight, pair in zip(weights, pairs)
    ]
    parts = []
    for both in sums:
        value = jnp.where(first, both[:cells, :PAIR], both[cells:, :PAIR])
        total = jnp.where(first, both[:cells, PAIR:], both[cells:, PAIR:])
        parts.append((value / total).astype(BF16))
    return jnp.concatenate(parts, axis=1)


def section(x, bias, wqkv, wout, gain):
    width = x.shape[1]
    head_size = width // HEADS
    q = dot(x, wqkv[:, :width]) * (1.0 / math.sqrt(head_size))
    k = dot(x, wqkv[:, width : 2 * width])
    v = dot(x, wqkv[:, 2 * width :])
    projected = dot(attended(q, k, v, bias, head_size), wout[...])
    centered = projected - jnp.mean(projected, axis=-1, keepdims=True)
    variance = jnp.mean(centered * centered, axis=-1, keepdims=True)
    branch = centered * lax.rsqrt(variance + 1e-05) * gain
    return x.astype(F32) + branch


def kernel(
    lat_signs, lon_signs, small_step, line_counts,
    offsets_hbm, latents_hbm, mask_hbm, embed_hbm, wqkv_hbm, wout_hbm, gain_hbm, out_ref,
    offsets_ref, latents_ref, mask_ref, embed_ref, gain_ref,
    entering, leaving, far_entering, far_leaving, lines, corners, wqkv, wout,
    main_in, tail_in, far_in, main_out, tail_out, far_out, bias, total,
    load_sem, send_sem, recv_sem, cross_send, cross_recv,
):
    segment, lon, lat = (lax.axis_index(axis) for axis in ("segment", "lon", "lat"))
    lons, lats = lax.axis_size("lon"), lax.axis_size("lat")
    levels, width = latents_ref.shape[2:]
    pieces = width // PAIR
    at = lambda a, b: (segment, lax.rem(lon + b + lons, lons), lax.rem(lat + a + lats, lats))
    pick = lambda pair: pair[0] + segment * (pair[1] - pair[0])

    across = (1 - segment, lon, lat)
    own_signs = tuple(-sign for sign in lat_signs[1])
    edge_of = lambda sign: lats - 1 if sign < 0 else 0
    edges_at = tuple(edge_of(sign) for sign in own_signs)
    on_edge = lat == pick(edges_at)
    on_first_edge = lat == edges_at[0]
    extra = max(line_counts)
    barrier = pltpu.get_barrier_semaphore()

    def greet(partner):
        pl.semaphore_signal(barrier, inc=1, device_id=partner, device_id_type=pl.DeviceIdType.MESH)

    for partner in (at(0, -1), at(0, 1), across):
        greet(partner)
    for a in (-1, 1):
        def greet_row():
            for b in (-1, 0, 1):
                greet(at(a, b))

        if extra:
            pl.when((lat + a >= 0) & (lat + a < lats))(greet_row)
        else:
            greet_row()

    greetings = 9
    if extra:
        greetings = 3 + 3 * ((lat > 0).astype(jnp.int32) + (lat < lats - 1).astype(jnp.int32))

    def load(slot, source_ref, target_ref):
        return pltpu.make_async_copy(source_ref, target_ref, load_sem.at[slot])

    seeds = [load(0, latents_hbm, latents_ref), load(1, mask_hbm, mask_ref), load(2, embed_hbm, embed_ref)]
    shifts, gains = load(3, offsets_hbm, offsets_ref), load(4, gain_hbm, gain_ref)
    weights = [load(5, wqkv_hbm.at[0], wqkv), load(6, wout_hbm.at[0], wout)]

    @pl.when(segment == 0)
    def _():
        for copy in seeds:
            copy.start()

    for copy in (shifts, gains, *weights):
        copy.start()

    on_small = segment == small_step
    edge_lat, edge_lon = lat_signs[small_step][small_step], lon_signs[small_step][small_step]

    def small_exchange(ref, level):
        low, right = at(-edge_lat, 0), at(0, -edge_lon)
        plan = (
            (0, lines.at[level, pl.ds(0, QUAD)], (pl.ds(4 * QUAD, QUAD), pl.ds(0, width)), low),
            (1, lines.at[level, pl.ds(QUAD, QUAD)], (pl.ds(6 * QUAD, QUAD), pl.ds(0, width)), right),
            (3, corners.at[level], (pl.ds(8 * QUAD, QUAD), pl.ds(width, PAIR)), at(-edge_lat, -edge_lon)),
        )
        return [
            pltpu.make_async_remote_copy(
                src_ref=held,
                dst_ref=ref.at[level, *target],
                send_sem=send_sem.at[small_step, level, slot],
                recv_sem=recv_sem.at[small_step, level, slot],
                device_id=device,
                device_id_type=pl.DeviceIdType.MESH,
            )
            for slot, held, target, device in plan
        ]

    def edges(cells, level):
        store_edges(cells, edge_lat, edge_lon, lines, corners, level, pieces)

    @pl.when(on_small)
    def _():
        ref = (entering, leaving)[small_step]
        for level in range(levels):
            for start in (5 * QUAD, 7 * QUAD):
                ref[level, pl.ds(start, QUAD), :] = jnp.zeros((QUAD, width + PAIR), BF16)
            for start in (4 * QUAD, 6 * QUAD):
                ref[level, pl.ds(start, QUAD), pl.ds(width, PAIR)] = jnp.zeros((QUAD, PAIR), BF16)
            ref[level, pl.ds(8 * QUAD, QUAD), pl.ds(0, width)] = jnp.zeros((QUAD, width), BF16)

    crossed = QUAD * line_counts[0]
    far_here = (segment == 1) & on_first_edge

    def clear(level):
        for index, ref in enumerate((entering, leaving)):
            behind = lat + pick(lat_signs[index])

            @pl.when((behind < 0) | (behind >= lats))
            def _():
                for start, count in ((4 * QUAD, 2 * QUAD), (8 * QUAD, QUAD)):
                    ref[level, pl.ds(start, count), :] = jnp.zeros((count, width + PAIR), BF16)

        for start in (0, QUAD * extra):
            @pl.when(jnp.logical_not(far_here))
            def _():
                far_entering[level, pl.ds(start, crossed), :] = jnp.zeros((crossed, width), BF16)

            if crossed < QUAD * extra:
                left = QUAD * extra - crossed
                far_entering[level, pl.ds(start + crossed, left), :] = jnp.zeros((left, width), BF16)

        @pl.when(jnp.logical_not(on_edge))
        def _():
            far_leaving[level, pl.ds(QUAD * extra, QUAD * extra), :] = jnp.zeros((QUAD * extra, width), BF16)

    def far_exchange(index, level):
        ref, count = ((far_entering, crossed), (far_leaving, QUAD * extra))[index]
        return pltpu.make_async_remote_copy(
            src_ref=ref.at[level, pl.ds(0, count)],
            dst_ref=ref.at[level, pl.ds(QUAD * extra, count)],
            send_sem=send_sem.at[index, level, 4],
            recv_sem=recv_sem.at[index, level, 4],
            device_id=at(0, -pick(lon_signs[index])),
            device_id_type=pl.DeviceIdType.MESH,
        )

    def exchange(index, ref, level):
        a, b = pick(lat_signs[index]), pick(lon_signs[index])
        low, right = (1 - a) // 2, (1 - b) // 2
        plan = (
            (2 * QUAD * low, 2 * QUAD, 4 * QUAD, at(-a, 0)),
            (QUAD * right, QUAD, 6 * QUAD, at(0, -b)),
            (2 * QUAD + QUAD * right, QUAD, 7 * QUAD, at(0, -b)),
            (2 * QUAD * low + QUAD * right, QUAD, 8 * QUAD, at(-a, -b)),
        )
        return [
            pltpu.make_async_remote_copy(
                src_ref=ref.at[level, pl.ds(pl.multiple_of(start, QUAD), count)],
                dst_ref=ref.at[level, pl.ds(target, count)],
                send_sem=send_sem.at[index, level, slot],
                recv_sem=recv_sem.at[index, level, slot],
                device_id=device,
                device_id_type=pl.DeviceIdType.MESH,
            )
            for slot, (start, count, target, device) in enumerate(plan)
        ]

    def guarded(copies, other, act, far_slots):
        inside = (other >= 0) & (other < lats)
        for slot, copy in enumerate(copies):
            if extra and slot in far_slots:
                pl.when(inside)(functools.partial(act, copy))
            else:
                act(copy)

    def each_transfer(index, level, act, way):
        ref = (entering, leaving)[index]

        def whole():
            guarded(exchange(index, ref, level), lat + way * pick(lat_signs[index]), act, (0, 3))

        def edge():
            guarded(small_exchange(ref, level), lat + way * edge_lat, act, (0, 2))

        if index == small_step:
            pl.when(on_small)(edge)
            pl.when(jnp.logical_not(on_small))(whole)
        else:
            whole()
        if extra:
            pl.when(far_here if index == 0 else on_edge)(lambda: act(far_exchange(index, level)))

    low_next = (1 - lat_signs[0][1]) // 2

    def crossing(level, part):
        if part == 2:
            rows, held, target = pl.ds(0, crossed), far_leaving, far_entering
        else:
            rows = pl.ds(2 * QUAD * (low_next if part == 0 else 1 - low_next), 2 * QUAD)
            held, target = leaving, entering
        return pltpu.make_async_remote_copy(
            src_ref=held.at[level, rows],
            dst_ref=target.at[level, rows],
            send_sem=cross_send.at[level, part],
            recv_sem=cross_recv.at[level, part],
            device_id=across,
            device_id_type=pl.DeviceIdType.MESH,
        )

    def each_crossing(level, act):
        act(crossing(level, 0))
        if extra:
            pl.when(on_first_edge)(lambda: act(crossing(level, 2)))
        act(crossing(level, 1))

    def each_level(step):
        def run(level, carry):
            step(level)
            return carry

        lax.fori_loop(0, levels, run, 0)

    if extra:
        each_level(clear)

    @pl.when(segment == 0)
    def _():
        for copy in seeds:
            copy.wait()
        seed(
            entering, latents_ref, mask_ref, embed_ref, pieces,
            edges if small_step == 0 else lambda cells, level: None,
        )

    pl.semaphore_wait(barrier, greetings)

    def enter(level):
        each_transfer(0, level, lambda copy: copy.start(), -1)

    @pl.when(segment == 0)
    def _():
        each_level(enter)

    shifts.wait()
    lat_base = [based(offsets_ref[s, 0], WLAT) for s in (0, 1)]
    lon_base = [based(offsets_ref[s, 1], WLON) for s in (0, 1)]
    first = segment == 0
    lat_own, lon_own = jnp.where(first, lat_base[0], lat_base[1]), jnp.where(first, lon_base[0], lon_base[1])
    lat_from, lon_from = jnp.where(first, 0, lat_base[0]), jnp.where(first, 0, lon_base[0])
    own_sign = pick(own_signs)
    offset = jnp.where(first, offsets_ref[0, 0], offsets_ref[1, 0])
    count = HELD + QUAD * extra

    def targets(shape, axis):
        t = iota(shape, axis)
        row, column = quarter_cell(t)
        ground = row + lat_own + lat * WLAT
        if not extra:
            ground = jnp.where(ground < 0, ground + lats * WLAT, ground)
            ground = jnp.where(ground >= lats * WLAT, ground - lats * WLAT, ground)
            live = t < CELLS
            group = jnp.where(live, (ground < offset).astype(jnp.int32), 2)
            return row + lat_own, column + lon_own, live, group
        outside = t >= HELD
        line, place = (t - HELD) >> 4, (t - HELD) & (QUAD - 1)
        edge_row = jnp.where(own_sign < 0, WLAT - 1 - line, line)
        row = jnp.where(outside, edge_row, row + lat_own)
        column = jnp.where(outside, place, column) + lon_own
        kept = on_edge & (place < WLON) & (line < jnp.abs(lat_own))
        live = (outside & kept) | ((t < CELLS) & (ground >= 0) & (ground < lats * WLAT))
        group = jnp.where(live, outside.astype(jnp.int32), 2)
        return row, column, live, group

    def beyond(row, held_sign, held_base):
        if not extra:
            return None
        line = row + held_base
        line = jnp.where(held_sign < 0, WLAT - 1 - line, line)
        past = ((row < 0) & (lat == 0)) | ((row >= WLAT) & (lat == lats - 1))
        return extra, line, past

    row, column, live, group = targets((count, 1), 0)
    row, column = row - lat_from, column - lon_from
    choosers(
        row, column, (pick(lat_signs[0]), pick(lon_signs[0])), on_small if small_step == 0 else None,
        beyond(row, own_signs[0], lat_base[0]), live, pieces, main_in, tail_in, far_in,
    )
    _, _, _, group_across = targets((1, count), 1)
    excluded = jnp.where(group == group_across, 0.0, -1e30)
    bias[pl.ds(0, count), :] = excluded
    bias[pl.ds(count, count), :] = excluded

    place = iota((CELLS * levels, 1), 0)
    row, column = split_by(place, WLON * levels, WLAT)
    column, held_level = split_by(column, levels, WLON)
    row, column = row - lat_own, column - lon_own

    def choose_leaving(level):
        choosers(
            row, column, (pick(lat_signs[1]), pick(lon_signs[1])), on_small if small_step == 1 else None,
            beyond(row, own_sign, lat_own), held_level == level, pieces,
            main_out.at[level], tail_out.at[level], far_out.at[level],
        )

    each_level(choose_leaving)
    gains.wait()
    for copy in weights:
        copy.wait()

    @pl.when(segment == 1)
    def _():
        def forward(level):
            copies = exchange(0, entering, level)
            start = lambda copy: copy.start()
            crossing(level, 0).wait_recv()
            guarded([copies[0], copies[3]], lat - lat_signs[0][1], start, (0, 1))
            copies[1 + low_next].start()

            if extra:
                @pl.when(on_first_edge)
                def _():
                    crossing(level, 2).wait_recv()
                    far_exchange(0, level).start()

            crossing(level, 1).wait_recv()
            copies[2 - low_next].start()

        each_level(forward)

    gain = jnp.where(first, gain_ref[0:1, :], gain_ref[1:2, :])

    def work(level):
        each_transfer(0, level, lambda copy: copy.wait_recv(), 1)
        x = gathered(entering[level], far_entering[level] if extra else None, main_in, tail_in, far_in, width, pieces).astype(BF16)
        cells = section(x, bias[...], wqkv, wout, gain)
        store_quarters(cells, leaving, level, width, pieces)
        if extra:
            far_leaving[level, pl.ds(0, QUAD * extra), :] = cells[HELD:].astype(BF16)

        @pl.when(segment == 0)
        def _():
            each_crossing(level, lambda copy: copy.start())

        if small_step == 1:
            pl.when(on_small)(lambda: edges(cells, level))
        each_transfer(1, level, lambda copy: copy.start(), -1)

    each_level(work)

    total[...] = jnp.zeros_like(total)

    def finish(level):
        each_transfer(1, level, lambda copy: copy.wait_recv(), 1)
        total[...] += gathered(
            leaving[level], far_leaving[level] if extra else None,
            main_out.at[level], tail_out.at[level], far_out.at[level], width, pieces,
        )

    each_level(finish)
    out_ref[...] = total[...].astype(BF16).reshape(out_ref.shape)

    def settle(level):
        for index in (0, 1):
            each_transfer(index, level, lambda copy: copy.wait_send(), -1)

        @pl.when(segment == 0)
        def _():
            each_crossing(level, lambda copy: copy.wait_send())

    each_level(settle)


def sections(variant, offsets, latents, land_mask, land_embed, qkv_weight, out_weight, norm_gain):
    _, _, levels, width = latents.shape
    second_known = variant >= 4
    signs = []
    for bit in (2, 1):
        other = -1 if variant & bit else 1
        if second_known:
            entering, leaving = (other, -other), (-other, 1)
        else:
            entering, leaving = (-1, other), (1, -other)
        signs.append((entering, leaving))
    if not second_known:
        line_counts = (1, HALF_LAT if signs[0][1][1] > 0 else HALF_LAT - 1)
    elif signs[0][0][0] > 0:
        line_counts = (HALF_LAT - 1, 1)
    else:
        line_counts = (0, 0)
    extra = max(line_counts)
    count = HELD + QUAD * extra
    far_rows = 2 * QUAD * max(extra, 1)
    far_block = (levels, far_rows, width)
    pieces = width // PAIR
    in_vmem = pl.BlockSpec(memory_space=pltpu.VMEM)
    in_hbm = pl.BlockSpec(memory_space=pl.ANY)
    block = (levels, 9 * QUAD, width + PAIR)
    return pl.pallas_call(
        functools.partial(kernel, signs[0], signs[1], int(second_known), line_counts),
        out_shape=jax.ShapeDtypeStruct(latents.shape, BF16),
        in_specs=[in_hbm] * 7,
        out_specs=in_vmem,
        scratch_shapes=[
            pltpu.SMEM(offsets.shape, offsets.dtype),
            pltpu.VMEM(latents.shape, latents.dtype),
            pltpu.VMEM(land_mask.shape, land_mask.dtype),
            pltpu.VMEM(land_embed.shape, land_embed.dtype),
            pltpu.VMEM(norm_gain.shape, norm_gain.dtype),
            pltpu.VMEM(block, BF16),
            pltpu.VMEM(block, BF16),
            pltpu.VMEM(far_block, BF16),
            pltpu.VMEM(far_block, BF16),
            pltpu.VMEM((levels, 2 * QUAD, width), BF16),
            pltpu.VMEM((levels, QUAD, PAIR), BF16),
            pltpu.VMEM(qkv_weight.shape[1:], BF16),
            pltpu.VMEM(out_weight.shape[1:], BF16),
            pltpu.VMEM((count, 9 * QUAD), BF16),
            pltpu.VMEM((count * pieces, 9 * QUAD), BF16),
            pltpu.VMEM((count, far_rows), BF16),
            pltpu.VMEM((levels, CELLS * levels, 9 * QUAD), BF16),
            pltpu.VMEM((levels, CELLS * levels * pieces, 9 * QUAD), BF16),
            pltpu.VMEM((levels, CELLS * levels, far_rows), BF16),
            pltpu.VMEM((2 * count, count), F32),
            pltpu.VMEM((CELLS * levels, width), F32),
            pltpu.SemaphoreType.DMA((7,)),
            pltpu.SemaphoreType.DMA((2, levels, 5)),
            pltpu.SemaphoreType.DMA((2, levels, 5)),
            pltpu.SemaphoreType.DMA((levels, 3)),
            pltpu.SemaphoreType.DMA((levels, 3)),
        ],
        compiler_params=pltpu.CompilerParams(
            collective_id=variant, has_side_effects=True, vmem_limit_bytes=48 * 1024 * 1024
        ),
    )(offsets, latents, land_mask, land_embed, qkv_weight, out_weight, norm_gain)


def body(latents, land_mask, land_embed, qkv_weight, out_weight, norm_gain, offsets):
    assert latents.shape[1:3] == (WLAT, WLON)
    lat_part, lon_part = offsets[:, 0:1], offsets[:, 1:2]
    signs = 2 * (lat_part >= HALF_LAT).astype(jnp.int32) + (lon_part >= HALF_LON).astype(jnp.int32)
    known = (lat_part == WLAT - 1) & (lon_part == WLON - 1)
    term = jnp.where(iota((2, 1), 0) == 0, jnp.where(known, 0, 1 + signs), signs)
    variant = jnp.sum(term)
    ways = [functools.partial(sections, v) for v in range(8)]
    out = lax.switch(
        variant, ways,
        offsets, latents.transpose(1, 2, 0, 3), land_mask, land_embed, qkv_weight, out_weight, norm_gain,
    )
    return out.transpose(2, 0, 1, 3)[None]


def solution(mesh):
    return jax.shard_map(
        body,
        mesh=mesh,
        in_specs=(
            P(None, "lat", "lon", None),
            P("lat", "lon"),
            P(),
            P("segment", None, None),
            P("segment", None, None),
            P(),
            P(),
        ),
        out_specs=P("segment", None, "lat", "lon", None),
        check_vma=False,
    )
```

```python
import functools
import math

import jax
import jax.numpy as jnp
from jax import lax
from jax.experimental import pallas as pl
from jax.experimental.pallas import tpu as pltpu
from jax.sharding import PartitionSpec as P

HEADS = 16
WLAT = 6
WLON = 12
HALF_LAT = WLAT // 2
HALF_LON = WLON // 2
CELLS = WLAT * WLON
HELD = 80
QUAD = 16
PAIR = 128
NT = (((1,), (1,)), ((), ()))
F32 = jnp.float32
BF16 = jnp.bfloat16


def dot(a, b):
    return jnp.dot(a, b, preferred_element_type=F32)


def iota(shape, axis):
    return lax.broadcasted_iota(jnp.int32, shape, axis)


def based(offset, window):
    return jnp.where(offset >= window // 2, offset - window, offset)


def split_by(value, size, count):
    high = sum((value >= size * k).astype(jnp.int32) for k in range(1, count))
    return high, value - size * high


def quarter_cell(t):
    late = t >= 4 * QUAD
    quarter = jnp.where(late, (t - 4 * QUAD) >> 1, t >> 4)
    j = jnp.where(late, QUAD + (t & 1), t & (QUAD - 1))
    row, column = split_by(j, HALF_LON, 3)
    return HALF_LAT * (quarter >> 1) + row, HALF_LON * (quarter & 1) + column


def source(row, column, lat_sign, lon_sign, small):
    row_out = (row < 0) | (row >= WLAT)
    column_out = (column < 0) | (column >= WLON)
    row = jnp.where(row_out, row - WLAT * lat_sign, row)
    column = jnp.where(column_out, column - WLON * lon_sign, column)
    low, near_row = split_by(row, HALF_LAT, 2)
    right, near_column = split_by(column, HALF_LON, 2)
    base = jnp.where(
        row_out,
        jnp.where(column_out, 8 * QUAD, 4 * QUAD + QUAD * right),
        jnp.where(column_out, 6 * QUAD + QUAD * low, 2 * QUAD * low + QUAD * right),
    )
    j = HALF_LON * near_row + near_column
    if small is not None:
        small_base = jnp.where(row_out, jnp.where(column_out, 8 * QUAD, 4 * QUAD), 6 * QUAD)
        small_j = jnp.where(row_out, jnp.where(column_out, QUAD, column), row)
        whole = ~(row_out | column_out) | jnp.logical_not(small)
        base, j = jnp.where(whole, base, small_base), jnp.where(whole, j, small_j)
    return base, j, column_out, column


def choosers(row, column, signs, small, beyond, wanted, pieces, main_ref, tail_ref, far_ref):
    base, j, column_out, column = source(row, column, *signs, small)
    near = wanted
    if beyond is not None:
        lines, line, past = beyond
        near = wanted & jnp.logical_not(past)
        held = wanted & past & (line >= 0) & (line < lines)
        far = QUAD * line + jnp.where(column_out, QUAD * lines, 0) + column
        lane = iota(far_ref.shape, 1)
        far_ref[...] = (lane == jnp.where(held, far, -1000)).astype(F32).astype(BF16)
    base = jnp.where(near, base, -5000)
    count = row.shape[0]
    lane = iota((count, 9 * QUAD), 1)
    main_ref[...] = (lane == jnp.where(j < QUAD, base + j, -1000)).astype(F32).astype(BF16)
    tail = jnp.where(j >= QUAD, base + j - QUAD, -1000)

    def fill(piece, carry):
        start = pl.multiple_of(piece * count, QUAD)
        tail_ref[pl.ds(start, count), :] = (lane == tail + 2 * piece).astype(F32).astype(BF16)
        return carry

    lax.fori_loop(0, pieces, fill, 0)


def gathered(block, far, main_ref, tail_ref, far_ref, width, pieces):
    count = main_ref.shape[0]
    tail = dot(tail_ref[...], block[:, width:])
    tail = jnp.concatenate([tail[p * count : (p + 1) * count] for p in range(pieces)], axis=1)
    tail = dot(main_ref[...], block[:, :width]) + tail
    return tail if far is None else tail + dot(far_ref[...], far)


def store_quarters(cells, ref, level, width, pieces):
    cells = cells[:CELLS].astype(F32)
    piece = width // pieces
    ref[level, pl.ds(0, 4 * QUAD), pl.ds(0, width)] = cells[: 4 * QUAD].astype(BF16)
    stack = jnp.concatenate([cells[4 * QUAD :, p * piece : (p + 1) * piece] for p in range(pieces)], axis=0)
    to, at = iota((4 * QUAD, 8 * pieces), 0), iota((4 * QUAD, 8 * pieces), 1)
    wanted = 8 * ((to & (QUAD - 1)) >> 1) + 2 * (to >> 4) + (to & 1)
    pick = (at == wanted).astype(F32).astype(BF16)
    ref[level, pl.ds(0, 4 * QUAD), pl.ds(width, piece)] = dot(pick, stack.astype(BF16)).astype(BF16)


def store_edges(cells, lat_sign, lon_sign, line_ref, corner_ref, level, pieces):
    row_at, column_at = (0 if lat_sign > 0 else WLAT - 1), (0 if lon_sign > 0 else WLON - 1)
    to = iota((2 * QUAD, CELLS), 0)
    row, column = quarter_cell(iota((2 * QUAD, CELLS), 1))
    pick = ((row == row_at) & (column == to)) | ((column == column_at) & (row == to - QUAD))
    line_ref[level] = dot(pick.astype(F32).astype(BF16), cells[:CELLS].astype(BF16)).astype(BF16)
    half = HALF_LON * (row_at % HALF_LAT) + column_at % HALF_LON
    quarter = 2 * (row_at // HALF_LAT) + column_at // HALF_LON
    place = QUAD * quarter + half if half < QUAD else 4 * QUAD + 2 * quarter + half - QUAD
    piece = cells.shape[1] // pieces
    line = iota((QUAD, piece), 0)
    corner = jnp.zeros((QUAD, piece), F32)
    for p in range(pieces):
        corner = jnp.where(line == 2 * p, cells[place : place + 1, p * piece : (p + 1) * piece], corner)
    corner_ref[level] = corner.astype(BF16)


def seed(entering, latents_ref, mask_ref, embed_ref, pieces, edges, ready):
    levels, width = latents_ref.shape[2:]
    embed = embed_ref[...].astype(F32).reshape(1, width)
    across = WLON * levels
    spread = iota((across, WLON), 0)
    spread = (spread >= levels * iota((across, WLON), 1)) & (spread < levels * iota((across, WLON), 1) + levels)
    rows = []
    for row in range(WLAT):
        land = jnp.where(spread, mask_ref[row : row + 1, :].astype(F32), 0.0)
        land = jnp.sum(land, axis=1, keepdims=True)
        rows.append(latents_ref[row].astype(F32).reshape(across, width) + land * embed)
    cells = jnp.concatenate(rows, axis=0).astype(BF16)
    row, column = quarter_cell(iota((CELLS, CELLS * levels), 0))
    wanted = levels * (WLON * row + column)
    at = iota((CELLS, CELLS * levels), 1)
    for level in range(levels):
        order = (at == wanted + level).astype(F32).astype(BF16)
        ordered = dot(order, cells)
        store_quarters(ordered, entering, level, width, pieces)
        edges(ordered, level)
        ready(level)


def attended(q, k, v, bias, head_size):
    cells = q.shape[0]
    first = iota((cells, PAIR), 1) < head_size
    ones = jnp.ones((cells, PAIR), BF16)
    pairs = [slice(p * PAIR, (p + 1) * PAIR) for p in range(q.shape[1] // PAIR)]
    scores = []
    for pair in pairs:
        zero = jnp.zeros((cells, PAIR), F32)
        both = jnp.concatenate([jnp.where(first, q[:, pair], zero), jnp.where(first, zero, q[:, pair])], axis=0)
        scores.append(lax.dot_general(both.astype(BF16), k[:, pair].astype(BF16), NT, preferred_element_type=F32))
    weights = []
    for score in scores:
        score = score + bias
        weights.append(jnp.exp(score - jnp.max(score, axis=-1, keepdims=True)).astype(BF16))
    sums = [
        dot(weight, jnp.concatenate([v[:, pair].astype(BF16), ones], axis=1))
        for weight, pair in zip(weights, pairs)
    ]
    parts = []
    for both in sums:
        value = jnp.where(first, both[:cells, :PAIR], both[cells:, :PAIR])
        total = jnp.where(first, both[:cells, PAIR:], both[cells:, PAIR:])
        parts.append((value / total).astype(BF16))
    return jnp.concatenate(parts, axis=1)


def section(x, bias, wqkv, wout, gain):
    width = x.shape[1]
    head_size = width // HEADS
    q = dot(x, wqkv[:, :width]) * (1.0 / math.sqrt(head_size))
    k = dot(x, wqkv[:, width : 2 * width])
    v = dot(x, wqkv[:, 2 * width :])
    projected = dot(attended(q, k, v, bias, head_size), wout[...])
    centered = projected - jnp.mean(projected, axis=-1, keepdims=True)
    variance = jnp.mean(centered * centered, axis=-1, keepdims=True)
    branch = centered * lax.rsqrt(variance + 1e-05) * gain
    return x.astype(F32) + branch


def kernel(
    lat_signs, lon_signs, small_step, line_counts,
    offsets_hbm, latents_hbm, mask_hbm, embed_hbm, wqkv_hbm, wout_hbm, gain_hbm, out_ref,
    offsets_ref, latents_ref, mask_ref, embed_ref, gain_ref,
    entering, leaving, far_entering, far_leaving, lines, corners, wqkv, wout,
    main_in, tail_in, far_in, main_out, tail_out, far_out, bias, total,
    load_sem, send_sem, recv_sem, cross_send, cross_recv,
):
    segment, lon, lat = (lax.axis_index(axis) for axis in ("segment", "lon", "lat"))
    lons, lats = lax.axis_size("lon"), lax.axis_size("lat")
    levels, width = latents_ref.shape[2:]
    pieces = width // PAIR
    at = lambda a, b: (segment, lax.rem(lon + b + lons, lons), lax.rem(lat + a + lats, lats))
    pick = lambda pair: pair[0] + segment * (pair[1] - pair[0])

    across = (1 - segment, lon, lat)
    own_signs = tuple(-sign for sign in lat_signs[1])
    edge_of = lambda sign: lats - 1 if sign < 0 else 0
    edges_at = tuple(edge_of(sign) for sign in own_signs)
    on_edge = lat == pick(edges_at)
    on_first_edge = lat == edges_at[0]
    extra = max(line_counts)
    barrier = pltpu.get_barrier_semaphore()

    def greet(partner):
        pl.semaphore_signal(barrier, inc=1, device_id=partner, device_id_type=pl.DeviceIdType.MESH)

    for partner in (at(0, -1), at(0, 1), across):
        greet(partner)
    for a in (-1, 1):
        def greet_row():
            for b in (-1, 0, 1):
                greet(at(a, b))

        if extra:
            pl.when((lat + a >= 0) & (lat + a < lats))(greet_row)
        else:
            greet_row()

    greetings = 9
    if extra:
        greetings = 3 + 3 * ((lat > 0).astype(jnp.int32) + (lat < lats - 1).astype(jnp.int32))

    def load(slot, source_ref, target_ref):
        return pltpu.make_async_copy(source_ref, target_ref, load_sem.at[slot])

    seeds = [load(0, latents_hbm, latents_ref), load(1, mask_hbm, mask_ref), load(2, embed_hbm, embed_ref)]
    shifts, gains = load(3, offsets_hbm, offsets_ref), load(4, gain_hbm, gain_ref)
    weights = [load(5, wqkv_hbm.at[0], wqkv), load(6, wout_hbm.at[0], wout)]

    @pl.when(segment == 0)
    def _():
        for copy in seeds:
            copy.start()

    for copy in (shifts, gains, *weights):
        copy.start()

    on_small = segment == small_step
    edge_lat, edge_lon = lat_signs[small_step][small_step], lon_signs[small_step][small_step]

    def small_exchange(ref, level):
        low, right = at(-edge_lat, 0), at(0, -edge_lon)
        plan = (
            (0, lines.at[level, pl.ds(0, QUAD)], (pl.ds(4 * QUAD, QUAD), pl.ds(0, width)), low),
            (1, lines.at[level, pl.ds(QUAD, QUAD)], (pl.ds(6 * QUAD, QUAD), pl.ds(0, width)), right),
            (3, corners.at[level], (pl.ds(8 * QUAD, QUAD), pl.ds(width, PAIR)), at(-edge_lat, -edge_lon)),
        )
        return [
            pltpu.make_async_remote_copy(
                src_ref=held,
                dst_ref=ref.at[level, *target],
                send_sem=send_sem.at[small_step, level, slot],
                recv_sem=recv_sem.at[small_step, level, slot],
                device_id=device,
                device_id_type=pl.DeviceIdType.MESH,
            )
            for slot, held, target, device in plan
        ]

    def edges(cells, level):
        store_edges(cells, edge_lat, edge_lon, lines, corners, level, pieces)

    @pl.when(on_small)
    def _():
        ref = (entering, leaving)[small_step]
        for level in range(levels):
            for start in (5 * QUAD, 7 * QUAD):
                ref[level, pl.ds(start, QUAD), :] = jnp.zeros((QUAD, width + PAIR), BF16)
            for start in (4 * QUAD, 6 * QUAD):
                ref[level, pl.ds(start, QUAD), pl.ds(width, PAIR)] = jnp.zeros((QUAD, PAIR), BF16)
            ref[level, pl.ds(8 * QUAD, QUAD), pl.ds(0, width)] = jnp.zeros((QUAD, width), BF16)

    crossed = QUAD * line_counts[0]
    far_here = (segment == 1) & on_first_edge

    def clear(level):
        for index, ref in enumerate((entering, leaving)):
            behind = lat + pick(lat_signs[index])

            @pl.when((behind < 0) | (behind >= lats))
            def _():
                for start, count in ((4 * QUAD, 2 * QUAD), (8 * QUAD, QUAD)):
                    ref[level, pl.ds(start, count), :] = jnp.zeros((count, width + PAIR), BF16)

        for start in (0, QUAD * extra):
            @pl.when(jnp.logical_not(far_here))
            def _():
                far_entering[level, pl.ds(start, crossed), :] = jnp.zeros((crossed, width), BF16)

            if crossed < QUAD * extra:
                left = QUAD * extra - crossed
                far_entering[level, pl.ds(start + crossed, left), :] = jnp.zeros((left, width), BF16)

        @pl.when(jnp.logical_not(on_edge))
        def _():
            far_leaving[level, pl.ds(QUAD * extra, QUAD * extra), :] = jnp.zeros((QUAD * extra, width), BF16)

    def far_exchange(index, level):
        ref, count = ((far_entering, crossed), (far_leaving, QUAD * extra))[index]
        return pltpu.make_async_remote_copy(
            src_ref=ref.at[level, pl.ds(0, count)],
            dst_ref=ref.at[level, pl.ds(QUAD * extra, count)],
            send_sem=send_sem.at[index, level, 4],
            recv_sem=recv_sem.at[index, level, 4],
            device_id=at(0, -pick(lon_signs[index])),
            device_id_type=pl.DeviceIdType.MESH,
        )

    def exchange(index, ref, level):
        a, b = pick(lat_signs[index]), pick(lon_signs[index])
        low, right = (1 - a) // 2, (1 - b) // 2
        plan = (
            (2 * QUAD * low, 2 * QUAD, 4 * QUAD, at(-a, 0)),
            (QUAD * right, QUAD, 6 * QUAD, at(0, -b)),
            (2 * QUAD + QUAD * right, QUAD, 7 * QUAD, at(0, -b)),
            (2 * QUAD * low + QUAD * right, QUAD, 8 * QUAD, at(-a, -b)),
        )
        return [
            pltpu.make_async_remote_copy(
                src_ref=ref.at[level, pl.ds(pl.multiple_of(start, QUAD), count)],
                dst_ref=ref.at[level, pl.ds(target, count)],
                send_sem=send_sem.at[index, level, slot],
                recv_sem=recv_sem.at[index, level, slot],
                device_id=device,
                device_id_type=pl.DeviceIdType.MESH,
            )
            for slot, (start, count, target, device) in enumerate(plan)
        ]

    def guarded(copies, other, act, far_slots):
        inside = (other >= 0) & (other < lats)
        for slot, copy in enumerate(copies):
            if extra and slot in far_slots:
                pl.when(inside)(functools.partial(act, copy))
            else:
                act(copy)

    def each_transfer(index, level, act, way):
        ref = (entering, leaving)[index]

        def whole():
            guarded(exchange(index, ref, level), lat + way * pick(lat_signs[index]), act, (0, 3))

        def edge():
            guarded(small_exchange(ref, level), lat + way * edge_lat, act, (0, 2))

        if index == small_step:
            pl.when(on_small)(edge)
            pl.when(jnp.logical_not(on_small))(whole)
        else:
            whole()
        if extra:
            pl.when(far_here if index == 0 else on_edge)(lambda: act(far_exchange(index, level)))

    low_next = (1 - lat_signs[0][1]) // 2

    def crossing(level, part):
        if part == 2:
            rows, held, target = pl.ds(0, crossed), far_leaving, far_entering
        else:
            rows = pl.ds(2 * QUAD * (low_next if part == 0 else 1 - low_next), 2 * QUAD)
            held, target = leaving, entering
        return pltpu.make_async_remote_copy(
            src_ref=held.at[level, rows],
            dst_ref=target.at[level, rows],
            send_sem=cross_send.at[level, part],
            recv_sem=cross_recv.at[level, part],
            device_id=across,
            device_id_type=pl.DeviceIdType.MESH,
        )

    def each_crossing(level, act):
        act(crossing(level, 0))
        if extra:
            pl.when(on_first_edge)(lambda: act(crossing(level, 2)))
        act(crossing(level, 1))

    def each_level(step):
        def run(level, carry):
            step(level)
            return carry

        lax.fori_loop(0, levels, run, 0)

    def enter(level):
        each_transfer(0, level, lambda copy: copy.start(), -1)

    def ready(level):
        if level == 0:
            pl.semaphore_wait(barrier, greetings)
        enter(level)

    @pl.when(segment == 1)
    def _():
        pl.semaphore_wait(barrier, greetings)

    @pl.when(segment == 0)
    def _():
        for copy in seeds:
            copy.wait()
        seed(
            entering, latents_ref, mask_ref, embed_ref, pieces,
            edges if small_step == 0 else lambda cells, level: None, ready,
        )

    if extra:
        each_level(clear)
    shifts.wait()
    lat_base = [based(offsets_ref[s, 0], WLAT) for s in (0, 1)]
    lon_base = [based(offsets_ref[s, 1], WLON) for s in (0, 1)]
    first = segment == 0
    lat_own, lon_own = jnp.where(first, lat_base[0], lat_base[1]), jnp.where(first, lon_base[0], lon_base[1])
    lat_from, lon_from = jnp.where(first, 0, lat_base[0]), jnp.where(first, 0, lon_base[0])
    own_sign = pick(own_signs)
    offset = jnp.where(first, offsets_ref[0, 0], offsets_ref[1, 0])
    count = HELD + QUAD * extra

    def targets(shape, axis):
        t = iota(shape, axis)
        row, column = quarter_cell(t)
        ground = row + lat_own + lat * WLAT
        if not extra:
            ground = jnp.where(ground < 0, ground + lats * WLAT, ground)
            ground = jnp.where(ground >= lats * WLAT, ground - lats * WLAT, ground)
            live = t < CELLS
            group = jnp.where(live, (ground < offset).astype(jnp.int32), 2)
            return row + lat_own, column + lon_own, live, group
        outside = t >= HELD
        line, place = (t - HELD) >> 4, (t - HELD) & (QUAD - 1)
        edge_row = jnp.where(own_sign < 0, WLAT - 1 - line, line)
        row = jnp.where(outside, edge_row, row + lat_own)
        column = jnp.where(outside, place, column) + lon_own
        kept = on_edge & (place < WLON) & (line < jnp.abs(lat_own))
        live = (outside & kept) | ((t < CELLS) & (ground >= 0) & (ground < lats * WLAT))
        group = jnp.where(live, outside.astype(jnp.int32), 2)
        return row, column, live, group

    def beyond(row, held_sign, held_base):
        if not extra:
            return None
        line = row + held_base
        line = jnp.where(held_sign < 0, WLAT - 1 - line, line)
        past = ((row < 0) & (lat == 0)) | ((row >= WLAT) & (lat == lats - 1))
        return extra, line, past

    row, column, live, group = targets((count, 1), 0)
    row, column = row - lat_from, column - lon_from
    choosers(
        row, column, (pick(lat_signs[0]), pick(lon_signs[0])), on_small if small_step == 0 else None,
        beyond(row, own_signs[0], lat_base[0]), live, pieces, main_in, tail_in, far_in,
    )
    _, _, _, group_across = targets((1, count), 1)
    excluded = jnp.where(group == group_across, 0.0, -1e30)
    bias[pl.ds(0, count), :] = excluded
    bias[pl.ds(count, count), :] = excluded

    place = iota((CELLS * levels, 1), 0)
    row, column = split_by(place, WLON * levels, WLAT)
    column, held_level = split_by(column, levels, WLON)
    row, column = row - lat_own, column - lon_own

    def choose_leaving(level):
        choosers(
            row, column, (pick(lat_signs[1]), pick(lon_signs[1])), on_small if small_step == 1 else None,
            beyond(row, own_sign, lat_own), held_level == level, pieces,
            main_out.at[level], tail_out.at[level], far_out.at[level],
        )

    each_level(choose_leaving)
    gains.wait()
    for copy in weights:
        copy.wait()

    @pl.when(segment == 1)
    def _():
        def forward(level):
            copies = exchange(0, entering, level)
            start = lambda copy: copy.start()
            crossing(level, 0).wait_recv()
            guarded([copies[0], copies[3]], lat - lat_signs[0][1], start, (0, 1))
            copies[1 + low_next].start()

            if extra:
                @pl.when(on_first_edge)
                def _():
                    crossing(level, 2).wait_recv()
                    far_exchange(0, level).start()

            crossing(level, 1).wait_recv()
            copies[2 - low_next].start()

        each_level(forward)

    gain = jnp.where(first, gain_ref[0:1, :], gain_ref[1:2, :])

    def work(level):
        each_transfer(0, level, lambda copy: copy.wait_recv(), 1)
        x = gathered(entering[level], far_entering[level] if extra else None, main_in, tail_in, far_in, width, pieces).astype(BF16)
        cells = section(x, bias[...], wqkv, wout, gain)
        store_quarters(cells, leaving, level, width, pieces)
        if extra:
            far_leaving[level, pl.ds(0, QUAD * extra), :] = cells[HELD:].astype(BF16)

        @pl.when(segment == 0)
        def _():
            each_crossing(level, lambda copy: copy.start())

        if small_step == 1:
            pl.when(on_small)(lambda: edges(cells, level))
        each_transfer(1, level, lambda copy: copy.start(), -1)

    each_level(work)

    total[...] = jnp.zeros_like(total)

    def finish(level):
        each_transfer(1, level, lambda copy: copy.wait_recv(), 1)
        total[...] += gathered(
            leaving[level], far_leaving[level] if extra else None,
            main_out.at[level], tail_out.at[level], far_out.at[level], width, pieces,
        )

    each_level(finish)
    out_ref[...] = total[...].astype(BF16).reshape(out_ref.shape)

    def settle(level):
        for index in (0, 1):
            each_transfer(index, level, lambda copy: copy.wait_send(), -1)

        @pl.when(segment == 0)
        def _():
            each_crossing(level, lambda copy: copy.wait_send())

    each_level(settle)


def sections(variant, offsets, latents, land_mask, land_embed, qkv_weight, out_weight, norm_gain):
    _, _, levels, width = latents.shape
    second_known = variant >= 4
    signs = []
    for bit in (2, 1):
        other = -1 if variant & bit else 1
        if second_known:
            entering, leaving = (other, -other), (-other, 1)
        else:
            entering, leaving = (-1, other), (1, -other)
        signs.append((entering, leaving))
    if not second_known:
        line_counts = (1, HALF_LAT if signs[0][1][1] > 0 else HALF_LAT - 1)
    elif signs[0][0][0] > 0:
        line_counts = (HALF_LAT - 1, 1)
    else:
        line_counts = (0, 0)
    extra = max(line_counts)
    count = HELD + QUAD * extra
    far_rows = 2 * QUAD * max(extra, 1)
    far_block = (levels, far_rows, width)
    pieces = width // PAIR
    in_vmem = pl.BlockSpec(memory_space=pltpu.VMEM)
    in_hbm = pl.BlockSpec(memory_space=pl.ANY)
    block = (levels, 9 * QUAD, width + PAIR)
    return pl.pallas_call(
        functools.partial(kernel, signs[0], signs[1], int(second_known), line_counts),
        out_shape=jax.ShapeDtypeStruct(latents.shape, BF16),
        in_specs=[in_hbm] * 7,
        out_specs=in_vmem,
        scratch_shapes=[
            pltpu.SMEM(offsets.shape, offsets.dtype),
            pltpu.VMEM(latents.shape, latents.dtype),
            pltpu.VMEM(land_mask.shape, land_mask.dtype),
            pltpu.VMEM(land_embed.shape, land_embed.dtype),
            pltpu.VMEM(norm_gain.shape, norm_gain.dtype),
            pltpu.VMEM(block, BF16),
            pltpu.VMEM(block, BF16),
            pltpu.VMEM(far_block, BF16),
            pltpu.VMEM(far_block, BF16),
            pltpu.VMEM((levels, 2 * QUAD, width), BF16),
            pltpu.VMEM((levels, QUAD, PAIR), BF16),
            pltpu.VMEM(qkv_weight.shape[1:], BF16),
            pltpu.VMEM(out_weight.shape[1:], BF16),
            pltpu.VMEM((count, 9 * QUAD), BF16),
            pltpu.VMEM((count * pieces, 9 * QUAD), BF16),
            pltpu.VMEM((count, far_rows), BF16),
            pltpu.VMEM((levels, CELLS * levels, 9 * QUAD), BF16),
            pltpu.VMEM((levels, CELLS * levels * pieces, 9 * QUAD), BF16),
            pltpu.VMEM((levels, CELLS * levels, far_rows), BF16),
            pltpu.VMEM((2 * count, count), F32),
            pltpu.VMEM((CELLS * levels, width), F32),
            pltpu.SemaphoreType.DMA((7,)),
            pltpu.SemaphoreType.DMA((2, levels, 5)),
            pltpu.SemaphoreType.DMA((2, levels, 5)),
            pltpu.SemaphoreType.DMA((levels, 3)),
            pltpu.SemaphoreType.DMA((levels, 3)),
        ],
        compiler_params=pltpu.CompilerParams(
            collective_id=variant, has_side_effects=True, vmem_limit_bytes=48 * 1024 * 1024
        ),
    )(offsets, latents, land_mask, land_embed, qkv_weight, out_weight, norm_gain)


def variant_kernel(offsets_ref, variant_ref):
    shifts = [(offsets_ref[s, 0], offsets_ref[s, 1]) for s in (0, 1)]
    signs = [
        2 * (a >= HALF_LAT).astype(jnp.int32) + (b >= HALF_LON).astype(jnp.int32) for a, b in shifts
    ]
    known = (shifts[0][0] == WLAT - 1) & (shifts[0][1] == WLON - 1)
    variant_ref[0] = jnp.where(known, signs[1], 4 + signs[0])


def body(latents, land_mask, land_embed, qkv_weight, out_weight, norm_gain, offsets):
    assert latents.shape[1:3] == (WLAT, WLON)
    variant = pl.pallas_call(
        variant_kernel,
        out_shape=jax.ShapeDtypeStruct((1,), jnp.int32),
        in_specs=[pl.BlockSpec(memory_space=pltpu.SMEM)],
        out_specs=pl.BlockSpec(memory_space=pltpu.SMEM),
    )(offsets).reshape(())
    ways = [functools.partial(sections, v) for v in range(8)]
    out = lax.switch(
        variant, ways,
        offsets, latents.transpose(1, 2, 0, 3), land_mask, land_embed, qkv_weight, out_weight, norm_gain,
    )
    return out.transpose(2, 0, 1, 3)[None]


def solution(mesh):
    return jax.shard_map(
        body,
        mesh=mesh,
        in_specs=(
            P(None, "lat", "lon", None),
            P("lat", "lon"),
            P(),
            P("segment", None, None),
            P("segment", None, None),
            P(),
            P(),
        ),
        out_specs=P("segment", None, "lat", "lon", None),
        check_vma=False,
    )
```

```python
import functools
import math

import jax
import jax.numpy as jnp
from jax import lax
from jax.experimental import pallas as pl
from jax.experimental.pallas import tpu as pltpu
from jax.sharding import PartitionSpec as P

HEADS = 16
WLAT = 6
WLON = 12
HALF_LAT = WLAT // 2
HALF_LON = WLON // 2
CELLS = WLAT * WLON
HELD = 80
QUAD = 16
PAIR = 128
NT = (((1,), (1,)), ((), ()))
F32 = jnp.float32
BF16 = jnp.bfloat16


def dot(a, b):
    return jnp.dot(a, b, preferred_element_type=F32)


def iota(shape, axis):
    return lax.broadcasted_iota(jnp.int32, shape, axis)


def based(offset, window):
    return jnp.where(offset >= window // 2, offset - window, offset)


def split_by(value, size, count):
    high = sum((value >= size * k).astype(jnp.int32) for k in range(1, count))
    return high, value - size * high


def quarter_cell(t):
    late = t >= 4 * QUAD
    quarter = jnp.where(late, (t - 4 * QUAD) >> 1, t >> 4)
    j = jnp.where(late, QUAD + (t & 1), t & (QUAD - 1))
    row, column = split_by(j, HALF_LON, 3)
    return HALF_LAT * (quarter >> 1) + row, HALF_LON * (quarter & 1) + column


def source(row, column, lat_sign, lon_sign, small):
    row_out = (row < 0) | (row >= WLAT)
    column_out = (column < 0) | (column >= WLON)
    row = jnp.where(row_out, row - WLAT * lat_sign, row)
    column = jnp.where(column_out, column - WLON * lon_sign, column)
    low, near_row = split_by(row, HALF_LAT, 2)
    right, near_column = split_by(column, HALF_LON, 2)
    base = jnp.where(
        row_out,
        jnp.where(column_out, 8 * QUAD, 4 * QUAD + QUAD * right),
        jnp.where(column_out, 6 * QUAD + QUAD * low, 2 * QUAD * low + QUAD * right),
    )
    j = HALF_LON * near_row + near_column
    if small is not None:
        small_base = jnp.where(row_out, jnp.where(column_out, 8 * QUAD, 4 * QUAD), 6 * QUAD)
        small_j = jnp.where(row_out, jnp.where(column_out, QUAD, column), row)
        whole = ~(row_out | column_out) | jnp.logical_not(small)
        base, j = jnp.where(whole, base, small_base), jnp.where(whole, j, small_j)
    return base, j, column_out, column


def choosers(row, column, signs, small, beyond, wanted, pieces, main_ref, tail_ref, far_ref):
    base, j, column_out, column = source(row, column, *signs, small)
    near = wanted
    if beyond is not None:
        lines, line, past = beyond
        near = wanted & jnp.logical_not(past)
        held = wanted & past & (line >= 0) & (line < lines)
        far = QUAD * line + jnp.where(column_out, QUAD * lines, 0) + column
        lane = iota(far_ref.shape, 1)
        far_ref[...] = (lane == jnp.where(held, far, -1000)).astype(F32).astype(BF16)
    base = jnp.where(near, base, -5000)
    count = row.shape[0]
    lane = iota((count, 9 * QUAD), 1)
    main_ref[...] = (lane == jnp.where(j < QUAD, base + j, -1000)).astype(F32).astype(BF16)
    tail = jnp.where(j >= QUAD, base + j - QUAD, -1000)

    def fill(piece, carry):
        start = pl.multiple_of(piece * count, QUAD)
        tail_ref[pl.ds(start, count), :] = (lane == tail + 2 * piece).astype(F32).astype(BF16)
        return carry

    lax.fori_loop(0, pieces, fill, 0)


def gathered(block, far, main_ref, tail_ref, far_ref, width, pieces):
    count = main_ref.shape[0]
    tail = dot(tail_ref[...], block[:, width:])
    tail = jnp.concatenate([tail[p * count : (p + 1) * count] for p in range(pieces)], axis=1)
    tail = dot(main_ref[...], block[:, :width]) + tail
    return tail if far is None else tail + dot(far_ref[...], far)


def store_quarters(cells, ref, level, width, pieces):
    cells = cells[:CELLS].astype(F32)
    piece = width // pieces
    ref[level, pl.ds(0, 4 * QUAD), pl.ds(0, width)] = cells[: 4 * QUAD].astype(BF16)
    stack = jnp.concatenate([cells[4 * QUAD :, p * piece : (p + 1) * piece] for p in range(pieces)], axis=0)
    to, at = iota((4 * QUAD, 8 * pieces), 0), iota((4 * QUAD, 8 * pieces), 1)
    wanted = 8 * ((to & (QUAD - 1)) >> 1) + 2 * (to >> 4) + (to & 1)
    pick = (at == wanted).astype(F32).astype(BF16)
    ref[level, pl.ds(0, 4 * QUAD), pl.ds(width, piece)] = dot(pick, stack.astype(BF16)).astype(BF16)


def store_edges(cells, lat_sign, lon_sign, line_ref, corner_ref, level, pieces):
    row_at, column_at = (0 if lat_sign > 0 else WLAT - 1), (0 if lon_sign > 0 else WLON - 1)
    to = iota((2 * QUAD, CELLS), 0)
    row, column = quarter_cell(iota((2 * QUAD, CELLS), 1))
    pick = ((row == row_at) & (column == to)) | ((column == column_at) & (row == to - QUAD))
    line_ref[level] = dot(pick.astype(F32).astype(BF16), cells[:CELLS].astype(BF16)).astype(BF16)
    half = HALF_LON * (row_at % HALF_LAT) + column_at % HALF_LON
    quarter = 2 * (row_at // HALF_LAT) + column_at // HALF_LON
    place = QUAD * quarter + half if half < QUAD else 4 * QUAD + 2 * quarter + half - QUAD
    piece = cells.shape[1] // pieces
    line = iota((QUAD, piece), 0)
    corner = jnp.zeros((QUAD, piece), F32)
    for p in range(pieces):
        corner = jnp.where(line == 2 * p, cells[place : place + 1, p * piece : (p + 1) * piece], corner)
    corner_ref[level] = corner.astype(BF16)


def seed(entering, latents_ref, mask_ref, embed_ref, pieces, edges, ready):
    levels, width = latents_ref.shape[2:]
    embed = embed_ref[...].astype(F32).reshape(1, width)
    across = WLON * levels
    spread = iota((across, WLON), 0)
    spread = (spread >= levels * iota((across, WLON), 1)) & (spread < levels * iota((across, WLON), 1) + levels)
    rows = []
    for row in range(WLAT):
        land = jnp.where(spread, mask_ref[row : row + 1, :].astype(F32), 0.0)
        land = jnp.sum(land, axis=1, keepdims=True)
        rows.append(latents_ref[row].astype(F32).reshape(across, width) + land * embed)
    cells = jnp.concatenate(rows, axis=0).astype(BF16)
    row, column = quarter_cell(iota((CELLS, CELLS * levels), 0))
    wanted = levels * (WLON * row + column)
    at = iota((CELLS, CELLS * levels), 1)
    for level in range(levels):
        order = (at == wanted + level).astype(F32).astype(BF16)
        ordered = dot(order, cells)
        store_quarters(ordered, entering, level, width, pieces)
        edges(ordered, level)
        ready(level)


def attended(q, k, v, bias, head_size):
    cells = q.shape[0]
    first = iota((cells, PAIR), 1) < head_size
    ones = jnp.ones((cells, PAIR), BF16)
    pairs = [slice(p * PAIR, (p + 1) * PAIR) for p in range(q.shape[1] // PAIR)]
    scores = []
    for pair in pairs:
        zero = jnp.zeros((cells, PAIR), F32)
        both = jnp.concatenate([jnp.where(first, q[:, pair], zero), jnp.where(first, zero, q[:, pair])], axis=0)
        scores.append(lax.dot_general(both.astype(BF16), k[:, pair].astype(BF16), NT, preferred_element_type=F32))
    weights = []
    for score in scores:
        score = score + bias
        weights.append(jnp.exp(score - jnp.max(score, axis=-1, keepdims=True)).astype(BF16))
    sums = [
        dot(weight, jnp.concatenate([v[:, pair].astype(BF16), ones], axis=1))
        for weight, pair in zip(weights, pairs)
    ]
    parts = []
    for both in sums:
        value = jnp.where(first, both[:cells, :PAIR], both[cells:, :PAIR])
        total = jnp.where(first, both[:cells, PAIR:], both[cells:, PAIR:])
        parts.append((value / total).astype(BF16))
    return jnp.concatenate(parts, axis=1)


def section(x, bias, wqkv, wout, gain):
    width = x.shape[1]
    head_size = width // HEADS
    q = dot(x, wqkv[:, :width]) * (1.0 / math.sqrt(head_size))
    k = dot(x, wqkv[:, width : 2 * width])
    v = dot(x, wqkv[:, 2 * width :])
    projected = dot(attended(q, k, v, bias, head_size), wout[...])
    centered = projected - jnp.mean(projected, axis=-1, keepdims=True)
    variance = jnp.mean(centered * centered, axis=-1, keepdims=True)
    branch = centered * lax.rsqrt(variance + 1e-05) * gain
    return x.astype(F32) + branch


def kernel(
    lat_signs, lon_signs, small_step, line_counts,
    offsets_hbm, latents_hbm, mask_hbm, embed_hbm, wqkv_hbm, wout_hbm, gain_hbm, out_ref,
    offsets_ref, latents_ref, mask_ref, embed_ref, gain_ref,
    entering, leaving, far_entering, far_leaving, lines, corners, wqkv, wout,
    main_in, tail_in, far_in, main_out, tail_out, far_out, bias, total,
    load_sem, send_sem, recv_sem, cross_send, cross_recv,
):
    segment, lon, lat = (lax.axis_index(axis) for axis in ("segment", "lon", "lat"))
    lons, lats = lax.axis_size("lon"), lax.axis_size("lat")
    levels, width = latents_ref.shape[2:]
    pieces = width // PAIR
    at = lambda a, b: (segment, lax.rem(lon + b + lons, lons), lax.rem(lat + a + lats, lats))
    pick = lambda pair: pair[0] + segment * (pair[1] - pair[0])

    across = (1 - segment, lon, lat)
    own_signs = tuple(-sign for sign in lat_signs[1])
    edge_of = lambda sign: lats - 1 if sign < 0 else 0
    edges_at = tuple(edge_of(sign) for sign in own_signs)
    on_edge = lat == pick(edges_at)
    on_first_edge = lat == edges_at[0]
    extra = max(line_counts)
    barrier = pltpu.get_barrier_semaphore()

    def greet(partner):
        pl.semaphore_signal(barrier, inc=1, device_id=partner, device_id_type=pl.DeviceIdType.MESH)

    for partner in (at(0, -1), at(0, 1), across):
        greet(partner)
    for a in (-1, 1):
        def greet_row():
            for b in (-1, 0, 1):
                greet(at(a, b))

        if extra:
            pl.when((lat + a >= 0) & (lat + a < lats))(greet_row)
        else:
            greet_row()

    greetings = 9
    if extra:
        greetings = 3 + 3 * ((lat > 0).astype(jnp.int32) + (lat < lats - 1).astype(jnp.int32))

    def load(slot, source_ref, target_ref):
        return pltpu.make_async_copy(source_ref, target_ref, load_sem.at[slot])

    seeds = [load(0, latents_hbm, latents_ref), load(1, mask_hbm, mask_ref), load(2, embed_hbm, embed_ref)]
    shifts, gains = load(3, offsets_hbm, offsets_ref), load(4, gain_hbm, gain_ref)
    weights = [load(5, wqkv_hbm.at[0], wqkv), load(6, wout_hbm.at[0], wout)]

    @pl.when(segment == 0)
    def _():
        for copy in seeds:
            copy.start()

    for copy in (shifts, gains, *weights):
        copy.start()

    on_small = segment == small_step
    edge_lat, edge_lon = lat_signs[small_step][small_step], lon_signs[small_step][small_step]

    def small_exchange(ref, level):
        low, right = at(-edge_lat, 0), at(0, -edge_lon)
        plan = (
            (0, lines.at[level, pl.ds(0, QUAD)], (pl.ds(4 * QUAD, QUAD), pl.ds(0, width)), low),
            (1, lines.at[level, pl.ds(QUAD, QUAD)], (pl.ds(6 * QUAD, QUAD), pl.ds(0, width)), right),
            (3, corners.at[level], (pl.ds(8 * QUAD, QUAD), pl.ds(width, PAIR)), at(-edge_lat, -edge_lon)),
        )
        return [
            pltpu.make_async_remote_copy(
                src_ref=held,
                dst_ref=ref.at[level, *target],
                send_sem=send_sem.at[small_step, level, slot],
                recv_sem=recv_sem.at[small_step, level, slot],
                device_id=device,
                device_id_type=pl.DeviceIdType.MESH,
            )
            for slot, held, target, device in plan
        ]

    def edges(cells, level):
        store_edges(cells, edge_lat, edge_lon, lines, corners, level, pieces)

    @pl.when(on_small)
    def _():
        ref = (entering, leaving)[small_step]
        for level in range(levels):
            for start in (5 * QUAD, 7 * QUAD):
                ref[level, pl.ds(start, QUAD), :] = jnp.zeros((QUAD, width + PAIR), BF16)
            for start in (4 * QUAD, 6 * QUAD):
                ref[level, pl.ds(start, QUAD), pl.ds(width, PAIR)] = jnp.zeros((QUAD, PAIR), BF16)
            ref[level, pl.ds(8 * QUAD, QUAD), pl.ds(0, width)] = jnp.zeros((QUAD, width), BF16)

    crossed = QUAD * line_counts[0]
    far_here = (segment == 1) & on_first_edge

    def clear(level):
        for index, ref in enumerate((entering, leaving)):
            behind = lat + pick(lat_signs[index])

            @pl.when((behind < 0) | (behind >= lats))
            def _():
                for start, count in ((4 * QUAD, 2 * QUAD), (8 * QUAD, QUAD)):
                    ref[level, pl.ds(start, count), :] = jnp.zeros((count, width + PAIR), BF16)

        for start in (0, QUAD * extra):
            @pl.when(jnp.logical_not(far_here))
            def _():
                far_entering[level, pl.ds(start, crossed), :] = jnp.zeros((crossed, width), BF16)

            if crossed < QUAD * extra:
                left = QUAD * extra - crossed
                far_entering[level, pl.ds(start + crossed, left), :] = jnp.zeros((left, width), BF16)

        @pl.when(jnp.logical_not(on_edge))
        def _():
            far_leaving[level, pl.ds(QUAD * extra, QUAD * extra), :] = jnp.zeros((QUAD * extra, width), BF16)

    def far_exchange(index, level):
        ref, count = ((far_entering, crossed), (far_leaving, QUAD * extra))[index]
        return pltpu.make_async_remote_copy(
            src_ref=ref.at[level, pl.ds(0, count)],
            dst_ref=ref.at[level, pl.ds(QUAD * extra, count)],
            send_sem=send_sem.at[index, level, 4],
            recv_sem=recv_sem.at[index, level, 4],
            device_id=at(0, -pick(lon_signs[index])),
            device_id_type=pl.DeviceIdType.MESH,
        )

    def exchange(index, ref, level):
        a, b = pick(lat_signs[index]), pick(lon_signs[index])
        low, right = (1 - a) // 2, (1 - b) // 2
        piece = QUAD * right
        plan = (
            (0, 2 * QUAD * low + piece, 4 * QUAD + piece, at(-a, 0)),
            (1, piece, 6 * QUAD, at(0, -b)),
            (2, 2 * QUAD + piece, 7 * QUAD, at(0, -b)),
            (3, 2 * QUAD * low + piece, 8 * QUAD, at(-a, -b)),
            (5, 2 * QUAD * low + QUAD - piece, 5 * QUAD - piece, at(-a, 0)),
        )
        return [
            pltpu.make_async_remote_copy(
                src_ref=ref.at[level, pl.ds(pl.multiple_of(start, QUAD), QUAD)],
                dst_ref=ref.at[level, pl.ds(pl.multiple_of(target, QUAD), QUAD)],
                send_sem=send_sem.at[index, level, slot],
                recv_sem=recv_sem.at[index, level, slot],
                device_id=device,
                device_id_type=pl.DeviceIdType.MESH,
            )
            for slot, start, target, device in plan
        ]

    def guarded(copies, other, act, far_slots):
        inside = (other >= 0) & (other < lats)
        for slot, copy in enumerate(copies):
            if extra and slot in far_slots:
                pl.when(inside)(functools.partial(act, copy))
            else:
                act(copy)

    def each_transfer(index, level, act, way):
        ref = (entering, leaving)[index]

        def whole():
            guarded(exchange(index, ref, level), lat + way * pick(lat_signs[index]), act, (0, 3, 4))

        def edge():
            guarded(small_exchange(ref, level), lat + way * edge_lat, act, (0, 2))

        if index == small_step:
            pl.when(on_small)(edge)
            pl.when(jnp.logical_not(on_small))(whole)
        else:
            whole()
        if extra:
            pl.when(far_here if index == 0 else on_edge)(lambda: act(far_exchange(index, level)))

    low_next, right_next = (1 - lat_signs[0][1]) // 2, (1 - lon_signs[0][1]) // 2

    def crossing(level, part):
        if part == 2:
            rows, held, target = pl.ds(0, crossed), far_leaving, far_entering
        else:
            start, many = (
                (2 * QUAD * low_next + QUAD * right_next, QUAD),
                (2 * QUAD * low_next + QUAD * (1 - right_next), QUAD),
                None,
                (2 * QUAD * (1 - low_next), 2 * QUAD),
            )[part]
            rows = pl.ds(start, many)
            held, target = leaving, entering
        return pltpu.make_async_remote_copy(
            src_ref=held.at[level, rows],
            dst_ref=target.at[level, rows],
            send_sem=cross_send.at[level, part],
            recv_sem=cross_recv.at[level, part],
            device_id=across,
            device_id_type=pl.DeviceIdType.MESH,
        )

    def each_crossing(level, act):
        act(crossing(level, 0))
        act(crossing(level, 1))
        if extra:
            pl.when(on_first_edge)(lambda: act(crossing(level, 2)))
        act(crossing(level, 3))

    def each_level(step):
        def run(level, carry):
            step(level)
            return carry

        lax.fori_loop(0, levels, run, 0)

    def enter(level):
        each_transfer(0, level, lambda copy: copy.start(), -1)

    def ready(level):
        if level == 0:
            pl.semaphore_wait(barrier, greetings)
        enter(level)

    @pl.when(segment == 1)
    def _():
        pl.semaphore_wait(barrier, greetings)

    @pl.when(segment == 0)
    def _():
        for copy in seeds:
            copy.wait()
        seed(
            entering, latents_ref, mask_ref, embed_ref, pieces,
            edges if small_step == 0 else lambda cells, level: None, ready,
        )

    if extra:
        each_level(clear)
    shifts.wait()
    lat_base = [based(offsets_ref[s, 0], WLAT) for s in (0, 1)]
    lon_base = [based(offsets_ref[s, 1], WLON) for s in (0, 1)]
    first = segment == 0
    lat_own, lon_own = jnp.where(first, lat_base[0], lat_base[1]), jnp.where(first, lon_base[0], lon_base[1])
    lat_from, lon_from = jnp.where(first, 0, lat_base[0]), jnp.where(first, 0, lon_base[0])
    own_sign = pick(own_signs)
    offset = jnp.where(first, offsets_ref[0, 0], offsets_ref[1, 0])
    count = HELD + QUAD * extra

    def targets(shape, axis):
        t = iota(shape, axis)
        row, column = quarter_cell(t)
        ground = row + lat_own + lat * WLAT
        if not extra:
            ground = jnp.where(ground < 0, ground + lats * WLAT, ground)
            ground = jnp.where(ground >= lats * WLAT, ground - lats * WLAT, ground)
            live = t < CELLS
            group = jnp.where(live, (ground < offset).astype(jnp.int32), 2)
            return row + lat_own, column + lon_own, live, group
        outside = t >= HELD
        line, place = (t - HELD) >> 4, (t - HELD) & (QUAD - 1)
        edge_row = jnp.where(own_sign < 0, WLAT - 1 - line, line)
        row = jnp.where(outside, edge_row, row + lat_own)
        column = jnp.where(outside, place, column) + lon_own
        kept = on_edge & (place < WLON) & (line < jnp.abs(lat_own))
        live = (outside & kept) | ((t < CELLS) & (ground >= 0) & (ground < lats * WLAT))
        group = jnp.where(live, outside.astype(jnp.int32), 2)
        return row, column, live, group

    def beyond(row, held_sign, held_base):
        if not extra:
            return None
        line = row + held_base
        line = jnp.where(held_sign < 0, WLAT - 1 - line, line)
        past = ((row < 0) & (lat == 0)) | ((row >= WLAT) & (lat == lats - 1))
        return extra, line, past

    row, column, live, group = targets((count, 1), 0)
    row, column = row - lat_from, column - lon_from
    choosers(
        row, column, (pick(lat_signs[0]), pick(lon_signs[0])), on_small if small_step == 0 else None,
        beyond(row, own_signs[0], lat_base[0]), live, pieces, main_in, tail_in, far_in,
    )
    _, _, _, group_across = targets((1, count), 1)
    excluded = jnp.where(group == group_across, 0.0, -1e30)
    bias[pl.ds(0, count), :] = excluded
    bias[pl.ds(count, count), :] = excluded

    place = iota((CELLS * levels, 1), 0)
    row, column = split_by(place, WLON * levels, WLAT)
    column, held_level = split_by(column, levels, WLON)
    row, column = row - lat_own, column - lon_own

    def choose_leaving(level):
        choosers(
            row, column, (pick(lat_signs[1]), pick(lon_signs[1])), on_small if small_step == 1 else None,
            beyond(row, own_sign, lat_own), held_level == level, pieces,
            main_out.at[level], tail_out.at[level], far_out.at[level],
        )

    each_level(choose_leaving)
    gains.wait()
    for copy in weights:
        copy.wait()

    @pl.when(segment == 1)
    def _():
        def forward(level):
            copies = exchange(0, entering, level)
            start = lambda copy: copy.start()
            crossing(level, 0).wait_recv()
            guarded([copies[0], copies[3]], lat - lat_signs[0][1], start, (0, 1))
            copies[1 + low_next].start()
            crossing(level, 1).wait_recv()
            guarded([copies[4]], lat - lat_signs[0][1], start, (0,))

            if extra:
                @pl.when(on_first_edge)
                def _():
                    crossing(level, 2).wait_recv()
                    far_exchange(0, level).start()

            crossing(level, 3).wait_recv()
            copies[2 - low_next].start()

        each_level(forward)

    gain = jnp.where(first, gain_ref[0:1, :], gain_ref[1:2, :])

    def work(level):
        each_transfer(0, level, lambda copy: copy.wait_recv(), 1)
        x = gathered(entering[level], far_entering[level] if extra else None, main_in, tail_in, far_in, width, pieces).astype(BF16)
        cells = section(x, bias[...], wqkv, wout, gain)
        store_quarters(cells, leaving, level, width, pieces)
        if extra:
            far_leaving[level, pl.ds(0, QUAD * extra), :] = cells[HELD:].astype(BF16)

        @pl.when(segment == 0)
        def _():
            each_crossing(level, lambda copy: copy.start())

        if small_step == 1:
            pl.when(on_small)(lambda: edges(cells, level))
        each_transfer(1, level, lambda copy: copy.start(), -1)

    each_level(work)

    total[...] = jnp.zeros_like(total)

    def finish(level):
        each_transfer(1, level, lambda copy: copy.wait_recv(), 1)
        total[...] += gathered(
            leaving[level], far_leaving[level] if extra else None,
            main_out.at[level], tail_out.at[level], far_out.at[level], width, pieces,
        )

    each_level(finish)
    out_ref[...] = total[...].astype(BF16).reshape(out_ref.shape)

    def settle(level):
        for index in (0, 1):
            each_transfer(index, level, lambda copy: copy.wait_send(), -1)

        @pl.when(segment == 0)
        def _():
            each_crossing(level, lambda copy: copy.wait_send())

    each_level(settle)


def sections(variant, offsets, latents, land_mask, land_embed, qkv_weight, out_weight, norm_gain):
    _, _, levels, width = latents.shape
    second_known = variant >= 4
    signs = []
    for bit in (2, 1):
        other = -1 if variant & bit else 1
        if second_known:
            entering, leaving = (other, -other), (-other, 1)
        else:
            entering, leaving = (-1, other), (1, -other)
        signs.append((entering, leaving))
    if not second_known:
        line_counts = (1, HALF_LAT if signs[0][1][1] > 0 else HALF_LAT - 1)
    elif signs[0][0][0] > 0:
        line_counts = (HALF_LAT - 1, 1)
    else:
        line_counts = (0, 0)
    extra = max(line_counts)
    count = HELD + QUAD * extra
    far_rows = 2 * QUAD * max(extra, 1)
    far_block = (levels, far_rows, width)
    pieces = width // PAIR
    in_vmem = pl.BlockSpec(memory_space=pltpu.VMEM)
    in_hbm = pl.BlockSpec(memory_space=pl.ANY)
    block = (levels, 9 * QUAD, width + PAIR)
    return pl.pallas_call(
        functools.partial(kernel, signs[0], signs[1], int(second_known), line_counts),
        out_shape=jax.ShapeDtypeStruct(latents.shape, BF16),
        in_specs=[in_hbm] * 7,
        out_specs=in_vmem,
        scratch_shapes=[
            pltpu.SMEM(offsets.shape, offsets.dtype),
            pltpu.VMEM(latents.shape, latents.dtype),
            pltpu.VMEM(land_mask.shape, land_mask.dtype),
            pltpu.VMEM(land_embed.shape, land_embed.dtype),
            pltpu.VMEM(norm_gain.shape, norm_gain.dtype),
            pltpu.VMEM(block, BF16),
            pltpu.VMEM(block, BF16),
            pltpu.VMEM(far_block, BF16),
            pltpu.VMEM(far_block, BF16),
            pltpu.VMEM((levels, 2 * QUAD, width), BF16),
            pltpu.VMEM((levels, QUAD, PAIR), BF16),
            pltpu.VMEM(qkv_weight.shape[1:], BF16),
            pltpu.VMEM(out_weight.shape[1:], BF16),
            pltpu.VMEM((count, 9 * QUAD), BF16),
            pltpu.VMEM((count * pieces, 9 * QUAD), BF16),
            pltpu.VMEM((count, far_rows), BF16),
            pltpu.VMEM((levels, CELLS * levels, 9 * QUAD), BF16),
            pltpu.VMEM((levels, CELLS * levels * pieces, 9 * QUAD), BF16),
            pltpu.VMEM((levels, CELLS * levels, far_rows), BF16),
            pltpu.VMEM((2 * count, count), F32),
            pltpu.VMEM((CELLS * levels, width), F32),
            pltpu.SemaphoreType.DMA((7,)),
            pltpu.SemaphoreType.DMA((2, levels, 6)),
            pltpu.SemaphoreType.DMA((2, levels, 6)),
            pltpu.SemaphoreType.DMA((levels, 4)),
            pltpu.SemaphoreType.DMA((levels, 4)),
        ],
        compiler_params=pltpu.CompilerParams(
            collective_id=variant, has_side_effects=True, vmem_limit_bytes=48 * 1024 * 1024
        ),
    )(offsets, latents, land_mask, land_embed, qkv_weight, out_weight, norm_gain)


def variant_kernel(offsets_ref, variant_ref):
    shifts = [(offsets_ref[s, 0], offsets_ref[s, 1]) for s in (0, 1)]
    signs = [
        2 * (a >= HALF_LAT).astype(jnp.int32) + (b >= HALF_LON).astype(jnp.int32) for a, b in shifts
    ]
    known = (shifts[0][0] == WLAT - 1) & (shifts[0][1] == WLON - 1)
    variant_ref[0] = jnp.where(known, signs[1], 4 + signs[0])


def body(latents, land_mask, land_embed, qkv_weight, out_weight, norm_gain, offsets):
    assert latents.shape[1:3] == (WLAT, WLON)
    variant = pl.pallas_call(
        variant_kernel,
        out_shape=jax.ShapeDtypeStruct((1,), jnp.int32),
        in_specs=[pl.BlockSpec(memory_space=pltpu.SMEM)],
        out_specs=pl.BlockSpec(memory_space=pltpu.SMEM),
    )(offsets).reshape(())
    ways = [functools.partial(sections, v) for v in range(8)]
    out = lax.switch(
        variant, ways,
        offsets, latents.transpose(1, 2, 0, 3), land_mask, land_embed, qkv_weight, out_weight, norm_gain,
    )
    return out.transpose(2, 0, 1, 3)[None]


def solution(mesh):
    return jax.shard_map(
        body,
        mesh=mesh,
        in_specs=(
            P(None, "lat", "lon", None),
            P("lat", "lon"),
            P(),
            P("segment", None, None),
            P("segment", None, None),
            P(),
            P(),
        ),
        out_specs=P("segment", None, "lat", "lon", None),
        check_vma=False,
    )
```

```python
import functools
import math

import jax
import jax.numpy as jnp
from jax import lax
from jax.experimental import pallas as pl
from jax.experimental.pallas import tpu as pltpu
from jax.sharding import PartitionSpec as P

HEADS = 16
WLAT = 6
WLON = 12
HALF_LAT = WLAT // 2
HALF_LON = WLON // 2
CELLS = WLAT * WLON
HELD = 80
QUAD = 16
PAIR = 128
NT = (((1,), (1,)), ((), ()))
F32 = jnp.float32
BF16 = jnp.bfloat16


def dot(a, b):
    return jnp.dot(a, b, preferred_element_type=F32)


def iota(shape, axis):
    return lax.broadcasted_iota(jnp.int32, shape, axis)


def based(offset, window):
    return jnp.where(offset >= window // 2, offset - window, offset)


def split_by(value, size, count):
    high = sum((value >= size * k).astype(jnp.int32) for k in range(1, count))
    return high, value - size * high


def quarter_cell(t):
    late = t >= 4 * QUAD
    quarter = jnp.where(late, (t - 4 * QUAD) >> 1, t >> 4)
    j = jnp.where(late, QUAD + (t & 1), t & (QUAD - 1))
    row, column = split_by(j, HALF_LON, 3)
    return HALF_LAT * (quarter >> 1) + row, HALF_LON * (quarter & 1) + column


def source(row, column, lat_sign, lon_sign, small):
    row_out = (row < 0) | (row >= WLAT)
    column_out = (column < 0) | (column >= WLON)
    row = jnp.where(row_out, row - WLAT * lat_sign, row)
    column = jnp.where(column_out, column - WLON * lon_sign, column)
    low, near_row = split_by(row, HALF_LAT, 2)
    right, near_column = split_by(column, HALF_LON, 2)
    base = jnp.where(
        row_out,
        jnp.where(column_out, 8 * QUAD, 4 * QUAD + QUAD * right),
        jnp.where(column_out, 6 * QUAD + QUAD * low, 2 * QUAD * low + QUAD * right),
    )
    j = HALF_LON * near_row + near_column
    if small is not None:
        small_base = jnp.where(row_out, jnp.where(column_out, 8 * QUAD, 4 * QUAD), 6 * QUAD)
        small_j = jnp.where(row_out, jnp.where(column_out, QUAD, column), row)
        whole = ~(row_out | column_out) | jnp.logical_not(small)
        base, j = jnp.where(whole, base, small_base), jnp.where(whole, j, small_j)
    return base, j, column_out, column


def choosers(row, column, signs, small, beyond, wanted, pieces, main_ref, tail_ref, far_ref):
    base, j, column_out, column = source(row, column, *signs, small)
    near = wanted
    if beyond is not None:
        lines, line, past = beyond
        near = wanted & jnp.logical_not(past)
        held = wanted & past & (line >= 0) & (line < lines)
        far = QUAD * line + jnp.where(column_out, QUAD * lines, 0) + column
        lane = iota(far_ref.shape, 1)
        far_ref[...] = (lane == jnp.where(held, far, -1000)).astype(F32).astype(BF16)
    base = jnp.where(near, base, -5000)
    count = row.shape[0]
    lane = iota((count, 9 * QUAD), 1)
    main_ref[...] = (lane == jnp.where(j < QUAD, base + j, -1000)).astype(F32).astype(BF16)
    tail = jnp.where(j >= QUAD, base + j - QUAD, -1000)

    def fill(piece, carry):
        start = pl.multiple_of(piece * count, QUAD)
        tail_ref[pl.ds(start, count), :] = (lane == tail + 2 * piece).astype(F32).astype(BF16)
        return carry

    lax.fori_loop(0, pieces, fill, 0)


def gathered(block, far, main_ref, tail_ref, far_ref, width, pieces):
    count = main_ref.shape[0]
    tail = dot(tail_ref[...], block[:, width:])
    tail = jnp.concatenate([tail[p * count : (p + 1) * count] for p in range(pieces)], axis=1)
    tail = dot(main_ref[...], block[:, :width]) + tail
    return tail if far is None else tail + dot(far_ref[...], far)


def store_quarters(cells, ref, level, width, pieces):
    cells = cells[:CELLS].astype(F32)
    piece = width // pieces
    ref[level, pl.ds(0, 4 * QUAD), pl.ds(0, width)] = cells[: 4 * QUAD].astype(BF16)
    stack = jnp.concatenate([cells[4 * QUAD :, p * piece : (p + 1) * piece] for p in range(pieces)], axis=0)
    to, at = iota((4 * QUAD, 8 * pieces), 0), iota((4 * QUAD, 8 * pieces), 1)
    wanted = 8 * ((to & (QUAD - 1)) >> 1) + 2 * (to >> 4) + (to & 1)
    pick = (at == wanted).astype(F32).astype(BF16)
    ref[level, pl.ds(0, 4 * QUAD), pl.ds(width, piece)] = dot(pick, stack.astype(BF16)).astype(BF16)


def store_edges(cells, lat_sign, lon_sign, line_ref, corner_ref, level, pieces):
    row_at, column_at = (0 if lat_sign > 0 else WLAT - 1), (0 if lon_sign > 0 else WLON - 1)
    to = iota((2 * QUAD, CELLS), 0)
    row, column = quarter_cell(iota((2 * QUAD, CELLS), 1))
    pick = ((row == row_at) & (column == to)) | ((column == column_at) & (row == to - QUAD))
    line_ref[level] = dot(pick.astype(F32).astype(BF16), cells[:CELLS].astype(BF16)).astype(BF16)
    half = HALF_LON * (row_at % HALF_LAT) + column_at % HALF_LON
    quarter = 2 * (row_at // HALF_LAT) + column_at // HALF_LON
    place = QUAD * quarter + half if half < QUAD else 4 * QUAD + 2 * quarter + half - QUAD
    piece = cells.shape[1] // pieces
    line = iota((QUAD, piece), 0)
    corner = jnp.zeros((QUAD, piece), F32)
    for p in range(pieces):
        corner = jnp.where(line == 2 * p, cells[place : place + 1, p * piece : (p + 1) * piece], corner)
    corner_ref[level] = corner.astype(BF16)


def seed(entering, latents_ref, mask_ref, embed_ref, pieces, edges, ready):
    levels, width = latents_ref.shape[2:]
    embed = embed_ref[...].astype(F32).reshape(1, width)
    across = WLON * levels
    spread = iota((across, WLON), 0)
    spread = (spread >= levels * iota((across, WLON), 1)) & (spread < levels * iota((across, WLON), 1) + levels)
    rows = []
    for row in range(WLAT):
        land = jnp.where(spread, mask_ref[row : row + 1, :].astype(F32), 0.0)
        land = jnp.sum(land, axis=1, keepdims=True)
        rows.append(latents_ref[row].astype(F32).reshape(across, width) + land * embed)
    cells = jnp.concatenate(rows, axis=0).astype(BF16)
    row, column = quarter_cell(iota((CELLS, CELLS * levels), 0))
    wanted = levels * (WLON * row + column)
    at = iota((CELLS, CELLS * levels), 1)
    for level in range(levels):
        order = (at == wanted + level).astype(F32).astype(BF16)
        ordered = dot(order, cells)
        store_quarters(ordered, entering, level, width, pieces)
        edges(ordered, level)
        ready(level)


def attended(q, k, v, bias, head_size):
    cells = q.shape[0]
    first = iota((cells, PAIR), 1) < head_size
    ones = jnp.ones((cells, PAIR), BF16)
    pairs = [slice(p * PAIR, (p + 1) * PAIR) for p in range(q.shape[1] // PAIR)]
    scores = []
    for pair in pairs:
        zero = jnp.zeros((cells, PAIR), F32)
        both = jnp.concatenate([jnp.where(first, q[:, pair], zero), jnp.where(first, zero, q[:, pair])], axis=0)
        scores.append(lax.dot_general(both.astype(BF16), k[:, pair].astype(BF16), NT, preferred_element_type=F32))
    weights = []
    for score in scores:
        score = score + bias
        weights.append(jnp.exp(score - jnp.max(score, axis=-1, keepdims=True)).astype(BF16))
    sums = [
        dot(weight, jnp.concatenate([v[:, pair].astype(BF16), ones], axis=1))
        for weight, pair in zip(weights, pairs)
    ]
    parts = []
    for both in sums:
        value = jnp.where(first, both[:cells, :PAIR], both[cells:, :PAIR])
        total = jnp.where(first, both[:cells, PAIR:], both[cells:, PAIR:])
        parts.append((value / total).astype(BF16))
    return jnp.concatenate(parts, axis=1)


def section(x, bias, wqkv, wout, gain):
    width = x.shape[1]
    head_size = width // HEADS
    q = dot(x, wqkv[:, :width]) * (1.0 / math.sqrt(head_size))
    k = dot(x, wqkv[:, width : 2 * width])
    v = dot(x, wqkv[:, 2 * width :])
    projected = dot(attended(q, k, v, bias, head_size), wout[...])
    centered = projected - jnp.mean(projected, axis=-1, keepdims=True)
    variance = jnp.mean(centered * centered, axis=-1, keepdims=True)
    branch = centered * lax.rsqrt(variance + 1e-05) * gain
    return x.astype(F32) + branch


def kernel(
    lat_signs, lon_signs, small_step, line_counts,
    offsets_hbm, latents_hbm, mask_hbm, embed_hbm, wqkv_hbm, wout_hbm, gain_hbm, out_ref,
    offsets_ref, latents_ref, mask_ref, embed_ref, gain_ref,
    entering, leaving, far_entering, far_leaving, lines, corners, wqkv, wout,
    main_in, tail_in, far_in, main_out, tail_out, far_out, bias, total,
    load_sem, send_sem, recv_sem, cross_send, cross_recv,
):
    segment, lon, lat = (lax.axis_index(axis) for axis in ("segment", "lon", "lat"))
    lons, lats = lax.axis_size("lon"), lax.axis_size("lat")
    levels, width = latents_ref.shape[2:]
    pieces = width // PAIR
    at = lambda a, b: (segment, lax.rem(lon + b + lons, lons), lax.rem(lat + a + lats, lats))
    pick = lambda pair: pair[0] + segment * (pair[1] - pair[0])

    across = (1 - segment, lon, lat)
    own_signs = tuple(-sign for sign in lat_signs[1])
    edge_of = lambda sign: lats - 1 if sign < 0 else 0
    edges_at = tuple(edge_of(sign) for sign in own_signs)
    on_edge = lat == pick(edges_at)
    on_first_edge = lat == edges_at[0]
    extra = max(line_counts)
    barrier = pltpu.get_barrier_semaphore()

    def greet(partner):
        pl.semaphore_signal(barrier, inc=1, device_id=partner, device_id_type=pl.DeviceIdType.MESH)

    for partner in (at(0, -1), at(0, 1), across):
        greet(partner)
    for a in (-1, 1):
        def greet_row():
            for b in (-1, 0, 1):
                greet(at(a, b))

        if extra:
            pl.when((lat + a >= 0) & (lat + a < lats))(greet_row)
        else:
            greet_row()

    greetings = 9
    if extra:
        greetings = 3 + 3 * ((lat > 0).astype(jnp.int32) + (lat < lats - 1).astype(jnp.int32))

    def load(slot, source_ref, target_ref):
        return pltpu.make_async_copy(source_ref, target_ref, load_sem.at[slot])

    seeds = [load(0, latents_hbm, latents_ref), load(1, mask_hbm, mask_ref), load(2, embed_hbm, embed_ref)]
    shifts, gains = load(3, offsets_hbm, offsets_ref), load(4, gain_hbm, gain_ref)
    weights = [load(5, wqkv_hbm.at[0], wqkv), load(6, wout_hbm.at[0], wout)]

    @pl.when(segment == 0)
    def _():
        for copy in seeds:
            copy.start()

    for copy in (shifts, gains, *weights):
        copy.start()

    on_small = segment == small_step
    edge_lat, edge_lon = lat_signs[small_step][small_step], lon_signs[small_step][small_step]

    def small_exchange(ref, level):
        low, right = at(-edge_lat, 0), at(0, -edge_lon)
        plan = (
            (0, lines.at[level, pl.ds(0, QUAD)], (pl.ds(4 * QUAD, QUAD), pl.ds(0, width)), low),
            (1, lines.at[level, pl.ds(QUAD, QUAD)], (pl.ds(6 * QUAD, QUAD), pl.ds(0, width)), right),
            (3, corners.at[level], (pl.ds(8 * QUAD, QUAD), pl.ds(width, PAIR)), at(-edge_lat, -edge_lon)),
        )
        return [
            pltpu.make_async_remote_copy(
                src_ref=held,
                dst_ref=ref.at[level, *target],
                send_sem=send_sem.at[small_step, level, slot],
                recv_sem=recv_sem.at[small_step, level, slot],
                device_id=device,
                device_id_type=pl.DeviceIdType.MESH,
            )
            for slot, held, target, device in plan
        ]

    def edges(cells, level):
        store_edges(cells, edge_lat, edge_lon, lines, corners, level, pieces)

    @pl.when(on_small)
    def _():
        ref = (entering, leaving)[small_step]
        for level in range(levels):
            for start in (5 * QUAD, 7 * QUAD):
                ref[level, pl.ds(start, QUAD), :] = jnp.zeros((QUAD, width + PAIR), BF16)
            for start in (4 * QUAD, 6 * QUAD):
                ref[level, pl.ds(start, QUAD), pl.ds(width, PAIR)] = jnp.zeros((QUAD, PAIR), BF16)
            ref[level, pl.ds(8 * QUAD, QUAD), pl.ds(0, width)] = jnp.zeros((QUAD, width), BF16)

    crossed = QUAD * line_counts[0]
    far_here = (segment == 1) & on_first_edge

    def clear(level):
        for index, ref in enumerate((entering, leaving)):
            behind = lat + pick(lat_signs[index])

            @pl.when((behind < 0) | (behind >= lats))
            def _():
                for start, count in ((4 * QUAD, 2 * QUAD), (8 * QUAD, QUAD)):
                    ref[level, pl.ds(start, count), :] = jnp.zeros((count, width + PAIR), BF16)

        for start in (0, QUAD * extra):
            @pl.when(jnp.logical_not(far_here))
            def _():
                far_entering[level, pl.ds(start, crossed), :] = jnp.zeros((crossed, width), BF16)

            if crossed < QUAD * extra:
                left = QUAD * extra - crossed
                far_entering[level, pl.ds(start + crossed, left), :] = jnp.zeros((left, width), BF16)

        @pl.when(jnp.logical_not(on_edge))
        def _():
            far_leaving[level, pl.ds(QUAD * extra, QUAD * extra), :] = jnp.zeros((QUAD * extra, width), BF16)

    def far_exchange(index, level):
        ref, count = ((far_entering, crossed), (far_leaving, QUAD * extra))[index]
        return pltpu.make_async_remote_copy(
            src_ref=ref.at[level, pl.ds(0, count)],
            dst_ref=ref.at[level, pl.ds(QUAD * extra, count)],
            send_sem=send_sem.at[index, level, 4],
            recv_sem=recv_sem.at[index, level, 4],
            device_id=at(0, -pick(lon_signs[index])),
            device_id_type=pl.DeviceIdType.MESH,
        )

    def exchange(index, ref, level):
        a, b = pick(lat_signs[index]), pick(lon_signs[index])
        low, right = (1 - a) // 2, (1 - b) // 2
        piece = QUAD * right
        plan = (
            (0, 2 * QUAD * low + piece, 4 * QUAD + piece, at(-a, 0)),
            (1, piece, 6 * QUAD, at(0, -b)),
            (2, 2 * QUAD + piece, 7 * QUAD, at(0, -b)),
            (3, 2 * QUAD * low + piece, 8 * QUAD, at(-a, -b)),
            (5, 2 * QUAD * low + QUAD - piece, 5 * QUAD - piece, at(-a, 0)),
        )
        return [
            pltpu.make_async_remote_copy(
                src_ref=ref.at[level, pl.ds(pl.multiple_of(start, QUAD), QUAD)],
                dst_ref=ref.at[level, pl.ds(pl.multiple_of(target, QUAD), QUAD)],
                send_sem=send_sem.at[index, level, slot],
                recv_sem=recv_sem.at[index, level, slot],
                device_id=device,
                device_id_type=pl.DeviceIdType.MESH,
            )
            for slot, start, target, device in plan
        ]

    def guarded(copies, other, act, far_slots):
        inside = (other >= 0) & (other < lats)
        for slot, copy in enumerate(copies):
            if extra and slot in far_slots:
                pl.when(inside)(functools.partial(act, copy))
            else:
                act(copy)

    def each_transfer(index, level, act, way):
        ref = (entering, leaving)[index]

        def whole():
            guarded(exchange(index, ref, level), lat + way * pick(lat_signs[index]), act, (0, 3, 4))

        def edge():
            guarded(small_exchange(ref, level), lat + way * edge_lat, act, (0, 2))

        if index == small_step:
            pl.when(on_small)(edge)
            pl.when(jnp.logical_not(on_small))(whole)
        else:
            whole()
        if extra:
            pl.when(far_here if index == 0 else on_edge)(lambda: act(far_exchange(index, level)))

    low_next, right_next = (1 - lat_signs[0][1]) // 2, (1 - lon_signs[0][1]) // 2

    def crossing(level, part):
        if part == 2:
            rows, held, target = pl.ds(0, crossed), far_leaving, far_entering
        else:
            start, many = (
                (2 * QUAD * low_next + QUAD * right_next, QUAD),
                (2 * QUAD * low_next + QUAD * (1 - right_next), QUAD),
                None,
                (2 * QUAD * (1 - low_next), 2 * QUAD),
            )[part]
            rows = pl.ds(start, many)
            held, target = leaving, entering
        return pltpu.make_async_remote_copy(
            src_ref=held.at[level, rows],
            dst_ref=target.at[level, rows],
            send_sem=cross_send.at[level, part],
            recv_sem=cross_recv.at[level, part],
            device_id=across,
            device_id_type=pl.DeviceIdType.MESH,
        )

    def each_crossing(level, act):
        act(crossing(level, 0))
        act(crossing(level, 1))
        if extra:
            pl.when(on_first_edge)(lambda: act(crossing(level, 2)))
        act(crossing(level, 3))

    def each_level(step):
        def run(level, carry):
            step(level)
            return carry

        lax.fori_loop(0, levels, run, 0)

    def enter(level):
        each_transfer(0, level, lambda copy: copy.start(), -1)

    def ready(level):
        if level == 0:
            pl.semaphore_wait(barrier, greetings)
        enter(level)

    @pl.when(segment == 1)
    def _():
        pl.semaphore_wait(barrier, greetings)

    @pl.when(segment == 0)
    def _():
        for copy in seeds:
            copy.wait()
        seed(
            entering, latents_ref, mask_ref, embed_ref, pieces,
            edges if small_step == 0 else lambda cells, level: None, ready,
        )

    if extra:
        each_level(clear)
    shifts.wait()
    lat_base = [based(offsets_ref[s, 0], WLAT) for s in (0, 1)]
    lon_base = [based(offsets_ref[s, 1], WLON) for s in (0, 1)]
    first = segment == 0
    lat_own, lon_own = jnp.where(first, lat_base[0], lat_base[1]), jnp.where(first, lon_base[0], lon_base[1])
    lat_from, lon_from = jnp.where(first, 0, lat_base[0]), jnp.where(first, 0, lon_base[0])
    own_sign = pick(own_signs)
    offset = jnp.where(first, offsets_ref[0, 0], offsets_ref[1, 0])
    count = HELD + QUAD * extra

    def targets(shape, axis):
        t = iota(shape, axis)
        row, column = quarter_cell(t)
        ground = row + lat_own + lat * WLAT
        if not extra:
            ground = jnp.where(ground < 0, ground + lats * WLAT, ground)
            ground = jnp.where(ground >= lats * WLAT, ground - lats * WLAT, ground)
            live = t < CELLS
            group = jnp.where(live, (ground < offset).astype(jnp.int32), 2)
            return row + lat_own, column + lon_own, live, group
        outside = t >= HELD
        line, place = (t - HELD) >> 4, (t - HELD) & (QUAD - 1)
        edge_row = jnp.where(own_sign < 0, WLAT - 1 - line, line)
        row = jnp.where(outside, edge_row, row + lat_own)
        column = jnp.where(outside, place, column) + lon_own
        kept = on_edge & (place < WLON) & (line < jnp.abs(lat_own))
        live = (outside & kept) | ((t < CELLS) & (ground >= 0) & (ground < lats * WLAT))
        group = jnp.where(live, outside.astype(jnp.int32), 2)
        return row, column, live, group

    def beyond(row, held_sign, held_base):
        if not extra:
            return None
        line = row + held_base
        line = jnp.where(held_sign < 0, WLAT - 1 - line, line)
        past = ((row < 0) & (lat == 0)) | ((row >= WLAT) & (lat == lats - 1))
        return extra, line, past

    row, column, live, group = targets((count, 1), 0)
    row, column = row - lat_from, column - lon_from
    choosers(
        row, column, (pick(lat_signs[0]), pick(lon_signs[0])), on_small if small_step == 0 else None,
        beyond(row, own_signs[0], lat_base[0]), live, pieces, main_in, tail_in, far_in,
    )
    _, _, _, group_across = targets((1, count), 1)
    excluded = jnp.where(group == group_across, 0.0, -1e30)
    bias[pl.ds(0, count), :] = excluded
    bias[pl.ds(count, count), :] = excluded

    place = iota((CELLS * levels, 1), 0)
    row, column = split_by(place, WLON * levels, WLAT)
    column, held_level = split_by(column, levels, WLON)
    row, column = row - lat_own, column - lon_own

    def choose_leaving(level):
        choosers(
            row, column, (pick(lat_signs[1]), pick(lon_signs[1])), on_small if small_step == 1 else None,
            beyond(row, own_sign, lat_own), held_level == level, pieces,
            main_out.at[level], tail_out.at[level], far_out.at[level],
        )

    pl.when(segment == 1)(lambda: each_level(choose_leaving))
    gains.wait()
    for copy in weights:
        copy.wait()

    @pl.when(segment == 1)
    def _():
        def forward(level):
            copies = exchange(0, entering, level)
            start = lambda copy: copy.start()
            crossing(level, 0).wait_recv()
            guarded([copies[0], copies[3]], lat - lat_signs[0][1], start, (0, 1))
            copies[1 + low_next].start()
            crossing(level, 1).wait_recv()
            guarded([copies[4]], lat - lat_signs[0][1], start, (0,))

            if extra:
                @pl.when(on_first_edge)
                def _():
                    crossing(level, 2).wait_recv()
                    far_exchange(0, level).start()

            crossing(level, 3).wait_recv()
            copies[2 - low_next].start()

        each_level(forward)

    gain = jnp.where(first, gain_ref[0:1, :], gain_ref[1:2, :])

    def work(level):
        each_transfer(0, level, lambda copy: copy.wait_recv(), 1)
        x = gathered(entering[level], far_entering[level] if extra else None, main_in, tail_in, far_in, width, pieces).astype(BF16)
        cells = section(x, bias[...], wqkv, wout, gain)
        store_quarters(cells, leaving, level, width, pieces)
        if extra:
            far_leaving[level, pl.ds(0, QUAD * extra), :] = cells[HELD:].astype(BF16)

        @pl.when(segment == 0)
        def _():
            each_crossing(level, lambda copy: copy.start())

        if small_step == 1:
            pl.when(on_small)(lambda: edges(cells, level))
        each_transfer(1, level, lambda copy: copy.start(), -1)

    each_level(work)
    pl.when(segment == 0)(lambda: each_level(choose_leaving))

    def arrived(level):
        each_transfer(1, level, lambda copy: copy.wait_recv(), 1)
        return gathered(
            leaving[level], far_leaving[level] if extra else None,
            main_out.at[level], tail_out.at[level], far_out.at[level], width, pieces,
        )

    def early(level, carry):
        total[...] = arrived(level) + (0.0 if levels == 2 else jnp.where(level == 0, 0.0, total[...]))
        return carry

    lax.fori_loop(0, levels - 1, early, 0)
    out_ref[...] = (total[...] + arrived(levels - 1)).astype(BF16).reshape(out_ref.shape)

    def settle(level):
        for index in (0, 1):
            each_transfer(index, level, lambda copy: copy.wait_send(), -1)

        @pl.when(segment == 0)
        def _():
            each_crossing(level, lambda copy: copy.wait_send())

    each_level(settle)


def sections(variant, offsets, latents, land_mask, land_embed, qkv_weight, out_weight, norm_gain):
    _, _, levels, width = latents.shape
    second_known = variant >= 4
    signs = []
    for bit in (2, 1):
        other = -1 if variant & bit else 1
        if second_known:
            entering, leaving = (other, -other), (-other, 1)
        else:
            entering, leaving = (-1, other), (1, -other)
        signs.append((entering, leaving))
    if not second_known:
        line_counts = (1, HALF_LAT if signs[0][1][1] > 0 else HALF_LAT - 1)
    elif signs[0][0][0] > 0:
        line_counts = (HALF_LAT - 1, 1)
    else:
        line_counts = (0, 0)
    extra = max(line_counts)
    count = HELD + QUAD * extra
    far_rows = 2 * QUAD * max(extra, 1)
    far_block = (levels, far_rows, width)
    pieces = width // PAIR
    in_vmem = pl.BlockSpec(memory_space=pltpu.VMEM)
    in_hbm = pl.BlockSpec(memory_space=pl.ANY)
    block = (levels, 9 * QUAD, width + PAIR)
    return pl.pallas_call(
        functools.partial(kernel, signs[0], signs[1], int(second_known), line_counts),
        out_shape=jax.ShapeDtypeStruct(latents.shape, BF16),
        in_specs=[in_hbm] * 7,
        out_specs=in_vmem,
        scratch_shapes=[
            pltpu.SMEM(offsets.shape, offsets.dtype),
            pltpu.VMEM(latents.shape, latents.dtype),
            pltpu.VMEM(land_mask.shape, land_mask.dtype),
            pltpu.VMEM(land_embed.shape, land_embed.dtype),
            pltpu.VMEM(norm_gain.shape, norm_gain.dtype),
            pltpu.VMEM(block, BF16),
            pltpu.VMEM(block, BF16),
            pltpu.VMEM(far_block, BF16),
            pltpu.VMEM(far_block, BF16),
            pltpu.VMEM((levels, 2 * QUAD, width), BF16),
            pltpu.VMEM((levels, QUAD, PAIR), BF16),
            pltpu.VMEM(qkv_weight.shape[1:], BF16),
            pltpu.VMEM(out_weight.shape[1:], BF16),
            pltpu.VMEM((count, 9 * QUAD), BF16),
            pltpu.VMEM((count * pieces, 9 * QUAD), BF16),
            pltpu.VMEM((count, far_rows), BF16),
            pltpu.VMEM((levels, CELLS * levels, 9 * QUAD), BF16),
            pltpu.VMEM((levels, CELLS * levels * pieces, 9 * QUAD), BF16),
            pltpu.VMEM((levels, CELLS * levels, far_rows), BF16),
            pltpu.VMEM((2 * count, count), F32),
            pltpu.VMEM((CELLS * levels, width), F32),
            pltpu.SemaphoreType.DMA((7,)),
            pltpu.SemaphoreType.DMA((2, levels, 6)),
            pltpu.SemaphoreType.DMA((2, levels, 6)),
            pltpu.SemaphoreType.DMA((levels, 4)),
            pltpu.SemaphoreType.DMA((levels, 4)),
        ],
        compiler_params=pltpu.CompilerParams(
            collective_id=variant, has_side_effects=True, vmem_limit_bytes=48 * 1024 * 1024
        ),
    )(offsets, latents, land_mask, land_embed, qkv_weight, out_weight, norm_gain)


def variant_kernel(offsets_ref, variant_ref):
    shifts = [(offsets_ref[s, 0], offsets_ref[s, 1]) for s in (0, 1)]
    signs = [
        2 * (a >= HALF_LAT).astype(jnp.int32) + (b >= HALF_LON).astype(jnp.int32) for a, b in shifts
    ]
    known = (shifts[0][0] == WLAT - 1) & (shifts[0][1] == WLON - 1)
    variant_ref[0] = jnp.where(known, signs[1], 4 + signs[0])


def body(latents, land_mask, land_embed, qkv_weight, out_weight, norm_gain, offsets):
    assert latents.shape[1:3] == (WLAT, WLON)
    variant = pl.pallas_call(
        variant_kernel,
        out_shape=jax.ShapeDtypeStruct((1,), jnp.int32),
        in_specs=[pl.BlockSpec(memory_space=pltpu.SMEM)],
        out_specs=pl.BlockSpec(memory_space=pltpu.SMEM),
    )(offsets).reshape(())
    ways = [functools.partial(sections, v) for v in range(8)]
    out = lax.switch(
        variant, ways,
        offsets, latents.transpose(1, 2, 0, 3), land_mask, land_embed, qkv_weight, out_weight, norm_gain,
    )
    return out.transpose(2, 0, 1, 3)[None]


def solution(mesh):
    return jax.shard_map(
        body,
        mesh=mesh,
        in_specs=(
            P(None, "lat", "lon", None),
            P("lat", "lon"),
            P(),
            P("segment", None, None),
            P("segment", None, None),
            P(),
            P(),
        ),
        out_specs=P("segment", None, "lat", "lon", None),
        check_vma=False,
    )
```
